256 devices in a mesh: rows: 16 (over y, z_hi, core), bricks: 16 (over x, z_lo).
Axes of the slice: x: 4, y: 4, z: 8 (z_hi: 2, z_lo: 4; z = z_hi * 4 + z_lo), core: 2. Of those that a mesh axis runs over, the one named last changes fastest.
Arguments:
- load: float32 [16, 16, 576], P('rows', 'bricks'), may hold values from -12 to 12
- stiffness: float32 [16, 16, 576, 576], P('rows', 'bricks'), may hold values from -1 to 10, as said below
- local_inverse: float32 [16, 16, 576, 576], P('rows', 'bricks'), may hold values from -1 to 4, as said below
- intact: int32 [16, 16, 96, 96], P('rows', 'bricks'), may hold values from 0 to 1, as said below
- face_lists: int32 [16, 16, 4, 24], P('rows', 'bricks'), may hold values from 0 to 95, as said below
- coarse_basis: float32 [16, 16, 64, 576], P('rows', 'bricks'), may hold values from -0.25 to 0.25
- coarse_matrix: float32 [16, 16, 16, 64, 64], P('rows', 'bricks'), may hold values from -1 to 10, as said below
- coarse_pattern: int32 [16, 16, 16], P('rows', 'bricks'), may hold values from 0 to 1, as said below
Outputs:
- solution: float32 [16, 16, 576], P('rows', 'bricks')
- residual: float32 [16, 16, 576], P('rows', 'bricks')
The draws below stay inside these ranges and needn't reach their ends.
Inputs may be any that keep to these rules, and one draw needn't show every extreme that they name: stiffness[r, b] is symmetric positive definite, and stays so with any symmetric set of its off-diagonal node blocks zeroed. local_inverse[r, b] is symmetric positive definite. intact[r, b] is symmetric in its two node indices, with ones on the diagonal. `face_lists`: each list of 24 node numbers holds distinct numbers. `coarse_matrix`: for each r, block (i, j) of the coarse operator is exactly the transpose of block (j, i); the whole is positive definite, and stays so with any symmetric set of off-diagonal blocks dropped. coarse_pattern[r] is symmetric in its two brick indices, with ones on the diagonal.
All inputs are finite; a program needn't handle non-finite values.
Results may differ from the reference program's by a relative error of at most 0.0003.
Values sent between devices are 32-bit elements; how exact they have to be, the bound alone decides.
A program may use at most 128 MiB of HBM per device.

```python
import jax
import jax.numpy as jnp
from jax import lax

NODES = 96
NDOF = 576
COARSE = 64
FACE = 24
ITERS = 3
BROWS = 16
NBR = 16


def symmetric_blocks(random_key, count, spread, lowest, highest, reach):
    first_key, second_key, third_key = jax.random.split(random_key, 3)
    shape_lead = (BROWS, NBR)
    random_part = jax.random.uniform(first_key, shape_lead + (count, count), jnp.float32, -1.0, 1.0) * (spread / count)
    upper = jnp.arange(count)[:, None] < jnp.arange(count)[None, :]
    symmetric = jnp.where(upper, random_part, jnp.swapaxes(random_part, -1, -2))
    diagonal = jax.random.uniform(second_key, shape_lead + (count,), jnp.float32, lowest, highest)
    identity = jnp.eye(count, dtype=bool)
    matrix = jnp.where(identity, diagonal[..., None], symmetric)
    scales = jnp.exp(jax.random.uniform(third_key, shape_lead + (count,), jnp.float32, -reach, reach))
    return matrix * (scales[..., :, None] * scales[..., None, :])


def draw_stiffness(key, part):
    key = jax.random.fold_in(key, 11)
    return symmetric_blocks(key, NDOF, 1.0, 1.1, 2.4, 0.0)


def draw_local_inverse(key, part):
    key = jax.random.fold_in(key, 12)
    return symmetric_blocks(key, NDOF, 0.3, 0.35, 0.9, 0.0)


def coarse_blocks(random_key, reach):
    keys_all = jax.random.split(random_key, 8)
    index = jnp.arange(COARSE, dtype=jnp.float32)
    cosine = jnp.cos(jnp.pi * (2.0 * index[None, :] + 1.0) * index[:, None] / (2.0 * COARSE)) * jnp.sqrt(2.0 / COARSE)
    cosine = jnp.where(index[:, None] == 0.0, cosine * jnp.sqrt(0.5), cosine)
    orders = jax.vmap(lambda single: jax.random.permutation(single, COARSE))(jax.random.split(keys_all[0], BROWS))
    row_signs = (2 * jax.random.randint(keys_all[1], (BROWS, COARSE), 0, 2) - 1).astype(jnp.float32)
    basis = jnp.take(cosine, orders, axis=0) * row_signs[:, :, None]
    modes = jax.random.uniform(keys_all[2], (BROWS, COARSE), jnp.float32, 0.0, 1.0)
    brick_index = jnp.arange(NBR)
    upper_flag = brick_index[:, None] < brick_index[None, :]
    pair_raw = jax.random.uniform(keys_all[3], (BROWS, NBR, NBR, COARSE), jnp.float32, 0.8, 1.0)
    pair_weights = jnp.where(upper_flag[None, :, :, None], pair_raw, jnp.swapaxes(pair_raw, 1, 2))
    strength = 0.95 / (NBR // 2)
    weights = strength * modes[:, None, None, :] * pair_weights
    coupling = jnp.einsum('raq,rijq,rbq->rijab', basis, weights, basis, precision=lax.Precision.HIGHEST)
    upper_pair = upper_flag[None, :, :, None, None]
    mirrored = jnp.transpose(coupling, (0, 2, 1, 4, 3))
    off_blocks = jnp.where(upper_pair, coupling, mirrored)
    own_random = jax.random.uniform(keys_all[5], (BROWS, NBR, COARSE, COARSE), jnp.float32, -1.0, 1.0) * (0.1 / COARSE)
    inner_upper = index[:, None] < index[None, :]
    own_symmetric = jnp.where(inner_upper, own_random, jnp.swapaxes(own_random, -1, -2))
    diagonal = jax.random.uniform(keys_all[6], (BROWS, NBR, COARSE), jnp.float32, 1.1, 1.4)
    own_blocks = jnp.where(jnp.eye(COARSE, dtype=bool), diagonal[..., :, None], own_symmetric)
    same_brick = jnp.eye(NBR, dtype=bool)[None, :, :, None, None]
    matrix = jnp.where(same_brick, own_blocks[:, :, None], off_blocks)
    scales = jnp.exp(jax.random.uniform(keys_all[7], (BROWS, NBR, COARSE), jnp.float32, -reach, reach))
    outer = scales[:, :, None, :, None] * scales[:, None, :, None, :]
    return matrix * outer


def draw_coarse_matrix(key, part):
    key = jax.random.fold_in(key, 13)
    return coarse_blocks(key, 0.0)


def draw_coarse_pattern(key, part):
    key = jax.random.fold_in(key, 14)
    side_key, pick_key = jax.random.split(key)
    orders = jax.vmap(lambda single: jax.random.permutation(single, NBR))(jax.random.split(side_key, BROWS))
    side = (orders < NBR // 2).astype(jnp.int32)
    cross = (side[:, :, None] != side[:, None, :]).astype(jnp.int32)
    picked = (jax.random.randint(pick_key, (BROWS, NBR, NBR), 0, 4) == 0).astype(jnp.int32)
    symmetric = jnp.maximum(picked, jnp.swapaxes(picked, -1, -2))
    return jnp.maximum(jnp.maximum(cross, symmetric), jnp.eye(NBR, dtype=jnp.int32))


def draw_intact(key, part):
    key = jax.random.fold_in(key, 15)
    picked = (jax.random.randint(key, (BROWS, NBR, NODES, NODES), 0, 8) == 0).astype(jnp.int32)
    broken = jnp.maximum(picked, jnp.swapaxes(picked, -1, -2))
    return jnp.maximum(1 - broken, jnp.eye(NODES, dtype=jnp.int32))


def draw_face_lists(key, part):
    key = jax.random.fold_in(key, 16)
    keys_all = jax.random.split(key, BROWS * NBR * 4)
    chosen = jax.vmap(lambda single: jax.random.permutation(single, NODES)[:FACE])(keys_all)
    return chosen.reshape(BROWS, NBR, 4, FACE).astype(jnp.int32)


def draw_load(key, part):
    key = jax.random.fold_in(key, 17)
    values = jax.random.truncated_normal(key, -4.0, 4.0, (BROWS, NBR, NDOF), jnp.float32)
    position = jnp.arange(BROWS, dtype=jnp.float32)[:, None] * NBR + jnp.arange(NBR, dtype=jnp.float32)[None, :]
    fraction = position / (BROWS * NBR - 1)
    return values * (0.6 + 1.2 * fraction)[..., None]


def levels(own_key, shape, cuts, low, top_value):
    gain = 1.0
    for dim, parts in cuts:
        heights = jax.random.uniform(jax.random.fold_in(jax.random.fold_in(own_key, 6), dim), (parts,), jnp.float32, low / len(cuts), top_value / len(cuts))
        gain = gain * jnp.repeat(jnp.exp(heights), shape[dim] // parts).reshape((-1,) + (1,) * (len(shape) - 1 - dim))
    return gain


def scatter_about(own_key, extent, scale, bound, shards=(), kind=jnp.bfloat16):
    values = scale * jax.random.normal(own_key, extent, jnp.float32)
    if shards:
        values = values * levels(own_key, extent, shards, -0.22, 0.18)
    return jnp.clip(values, -bound, bound).astype(kind)


def setup_inputs(seed: int = 0) -> dict:
    seeds = jax.random.split(jax.random.key(seed), 9)
    return {
        "load": draw_load(jax.random.fold_in(seeds[8], 71), 0),
        "stiffness": draw_stiffness(jax.random.fold_in(seeds[8], 71), 0),
        "local_inverse": draw_local_inverse(jax.random.fold_in(seeds[8], 71), 0),
        "intact": draw_intact(jax.random.fold_in(seeds[8], 71), 0),
        "face_lists": draw_face_lists(jax.random.fold_in(seeds[8], 71), 0),
        "coarse_basis": scatter_about(seeds[5], (BROWS, NBR, COARSE, NDOF), NDOF ** -0.5, 0.25, ((0, 16), (1, 16)), jnp.float32),
        "coarse_matrix": draw_coarse_matrix(jax.random.fold_in(seeds[8], 71), 0),
        "coarse_pattern": draw_coarse_pattern(jax.random.fold_in(seeds[8], 71), 0),
    }


precise = lax.Precision.HIGHEST
kappa_face = 1.0

def operate(vector, damaged, selector):
    own_term = jnp.einsum('rbij,rbj->rbi', damaged, vector, precision=precise)
    components = vector.reshape(BROWS, NBR, 6, NODES)
    face_values = jnp.einsum('rbcn,rbdkn->rbdck', components, selector, precision=precise)
    padded = jnp.pad(face_values, ((1, 1), (1, 1), (0, 0), (0, 0), (0, 0)))
    neighbours = jnp.stack([padded[:-2, 1:-1, 1], padded[2:, 1:-1, 0], padded[1:-1, :-2, 3], padded[1:-1, 2:, 2]], axis=2)
    stretch = face_values - neighbours
    forces = jnp.einsum('rbdck,rbdkn->rbcn', stretch, selector, precision=precise)
    return own_term + kappa_face * forces.reshape(BROWS, NBR, NDOF)

def precondition(vector, local_inverse, coarse_basis, factors):
    own_term = jnp.einsum('rbij,rbj->rbi', local_inverse, vector, precision=precise)
    reduced = jnp.einsum('rbqj,rbj->rbq', coarse_basis, vector, precision=precise)
    solved = jax.vmap(lambda factor, target: jax.scipy.linalg.cho_solve((factor, True), target))(factors, reduced.reshape(BROWS, NBR * COARSE))
    solved = solved.reshape(BROWS, NBR, COARSE)
    return own_term + jnp.einsum('rbqj,rbq->rbj', coarse_basis, solved, precision=precise)

def reference(load, stiffness, local_inverse, intact, face_lists, coarse_basis, coarse_matrix, coarse_pattern):
    damaged = stiffness * jnp.tile(intact.astype(jnp.float32), (1, 1, 6, 6))
    selector = (face_lists[..., None] == jnp.arange(NODES, dtype=jnp.int32)).astype(jnp.float32)
    masked = coarse_matrix * coarse_pattern[..., None, None].astype(jnp.float32)
    order = NBR * COARSE
    factors = jnp.linalg.cholesky(jnp.transpose(masked, (0, 1, 3, 2, 4)).reshape(BROWS, order, order))
    solution = jnp.zeros_like(load)
    residual = load
    preconditioned = precondition(residual, local_inverse, coarse_basis, factors)
    direction = preconditioned
    residual_dot = jnp.sum(residual * preconditioned)
    for iteration in range(ITERS):
        mapped = operate(direction, damaged, selector)
        step_size = residual_dot / jnp.sum(direction * mapped)
        solution = solution + step_size * direction
        residual = residual - step_size * mapped
        if iteration + 1 < ITERS:
            preconditioned = precondition(residual, local_inverse, coarse_basis, factors)
            new_dot = jnp.sum(residual * preconditioned)
            direction = preconditioned + new_dot / residual_dot * direction
            residual_dot = new_dot
    return (solution, residual)
```

```python
import functools

import jax
import jax.numpy as jnp
from jax import lax
from jax.experimental import pallas as pl
from jax.experimental.pallas import tpu as pltpu
from jax.sharding import PartitionSpec as P

MESH = pl.DeviceIdType.MESH
HI = lax.Precision.HIGHEST
F32 = jnp.float32
NODES, NDOF, COARSE, FACE, W = 96, 576, 64, 24, 128
LANES = 128


def dot(a, b, dims=((1,), (0,))):
    return lax.dot_general(a, b, (dims, ((), ())), precision=HI, preferred_element_type=F32)


def small_product(a, b):
    out = []
    for row in a:
        line = []
        for j in range(len(b[0])):
            acc = row[0] * b[0][j]
            for k in range(1, len(b)):
                acc = acc + row[k] * b[k][j]
            line.append(acc)
        out.append(line)
    return out


def small_inverse(m):
    n = len(m)
    if n == 2:
        a, b, d = m[0][0], m[0][1], m[1][1]
        r = 1.0 / (a * d - b * b)
        off = -(b * r)
        return [[d * r, off], [off, a * r]]
    h = n // 2
    b = [row[h:] for row in m[:h]]
    e = small_inverse([row[:h] for row in m[:h]])
    w = small_product(e, b)
    s = [[None] * h for _ in range(h)]
    for i in range(h):
        for j in range(i, h):
            acc = b[0][i] * w[0][j]
            for k in range(1, h):
                acc = acc + b[k][i] * w[k][j]
            s[i][j] = s[j][i] = m[h + i][h + j] - acc
    t = small_inverse(s)
    x = small_product(w, t)
    top = [[None] * h for _ in range(h)]
    for i in range(h):
        for j in range(i, h):
            acc = x[i][0] * w[j][0]
            for k in range(1, h):
                acc = acc + x[i][k] * w[j][k]
            top[i][j] = top[j][i] = e[i][j] + acc
    neg = [[-v for v in row] for row in x]
    out = [top[i] + neg[i] for i in range(h)]
    out += [[neg[k][i] for k in range(h)] + t[i] for i in range(h)]
    return out


def block_inverse(v):
    shape = (8, LANES)
    sub = lax.broadcasted_iota(jnp.int32, shape, 0)
    lane = lax.broadcasted_iota(jnp.int32, shape, 1)
    for g in range(len(v)):
        p = 8 * g
        x = v[g]
        rows = [jnp.broadcast_to(x[i : i + 1, :], shape) for i in range(8)]
        cols = [jnp.broadcast_to(x[:, p + t : p + t + 1], shape) for t in range(8)]
        m = [[None] * 8 for _ in range(8)]
        for i in range(8):
            for j in range(i, 8):
                m[i][j] = m[j][i] = jnp.broadcast_to(cols[j][i : i + 1, :], shape)
        e = small_inverse(m)
        pivots = (lane >= p) & (lane < p + 8)
        r = [jnp.where(pivots, (lane == p + i).astype(F32), rows[i]) for i in range(8)]
        q = []
        for i in range(8):
            acc = e[i][0] * r[0]
            for j in range(1, 8):
                acc = acc + e[i][j] * r[j]
            q.append(acc)
        new = []
        for k in range(len(v)):
            if k == g:
                y = q[0]
                for t in range(1, 8):
                    y = jnp.where(sub == t, q[t], y)
                new.append(y)
                continue
            y = v[k]
            acc = jnp.broadcast_to(y[:, p : p + 1], shape) * q[0]
            for t in range(1, 8):
                acc = acc + jnp.broadcast_to(y[:, p + t : p + t + 1], shape) * q[t]
            new.append(jnp.where(pivots, 0.0, y) - acc)
        v = new
    return v


def row_barrier(nb, r, b):
    barrier = pltpu.get_barrier_semaphore()
    for t in range(1, nb):
        pl.semaphore_signal(
            barrier, inc=1, device_id=(r, lax.rem(b + t, nb)), device_id_type=MESH
        )
    return barrier


def spread_kernel(nb, pattern_ref, matrix_ref, all_ref, send_sem, recv_sem):
    r, b = lax.axis_index("rows"), lax.axis_index("bricks")
    tiles = nb // 2
    barrier = row_barrier(nb, r, b)
    mine = pl.ds(pl.multiple_of(b * COARSE, COARSE), COARSE)
    for j in range(tiles):
        left = matrix_ref[2 * j] * pattern_ref[0, 2 * j].astype(F32)
        right = matrix_ref[2 * j + 1] * pattern_ref[0, 2 * j + 1].astype(F32)
        all_ref[j, mine, :] = jnp.concatenate([left, right], axis=1)
    pl.semaphore_wait(barrier, nb - 1)
    half = lax.div(b, 2)
    for k in range(tiles):

        def part(rows):
            return all_ref.at[pl.ds(k, tiles - k), rows, :]

        @pl.when(half == k)
        def _():
            def start(t, carry):
                pltpu.make_async_remote_copy(
                    src_ref=part(mine),
                    dst_ref=part(mine),
                    send_sem=send_sem.at[t],
                    recv_sem=recv_sem.at[b],
                    device_id=(r, lax.rem(b + t, nb)),
                    device_id_type=MESH,
                ).start()
                return carry

            lax.fori_loop(1, nb, start, 0)

            def done(t, carry):
                pltpu.make_async_copy(part(mine), part(mine), send_sem.at[t]).wait()
                return carry

            lax.fori_loop(1, nb, done, 0)

    for s in range(nb):
        part = all_ref.at[pl.ds(s // 2, tiles - s // 2), pl.ds(s * COARSE, COARSE), :]

        @pl.when(b != s)
        def _():
            pltpu.make_async_copy(part, part, recv_sem.at[s]).wait()


def factor_kernel(nb, all_ref, inverse_ref, u_ref, r_ref, l_ref, y_ref, z_ref):
    b = lax.axis_index("bricks")
    tiles = nb // 2
    sub = lax.broadcasted_iota(jnp.int32, (COARSE, W), 0)
    lane = lax.broadcasted_iota(jnp.int32, (COARSE, W), 1)
    for j in range(tiles):
        y_ref[j] = (lane + j * W == sub + b * COARSE).astype(F32)

    def step(k, carry):
        rows = pl.ds(pl.multiple_of(k * W, W), W)

        for j in range(tiles):
            u_ref[j, rows, :] = all_ref[j, rows, :]

        def update(i, inner):
            before = pl.ds(pl.multiple_of(i * W, W), W)
            factor = l_ref[k, i]
            for j in range(tiles):
                u_ref[j, rows, :] -= dot(factor, u_ref[j, before, :])
            return inner

        lax.fori_loop(0, k, update, 0)
        block = [u_ref[k, pl.ds(pl.multiple_of(k * W + 8 * i, 8), 8), :] for i in range(W // 8)]
        inverse = jnp.concatenate(block_inverse(block), axis=0)
        own = y_ref[k]
        z_ref[k] = dot(own, inverse)
        for j in range(tiles):
            scaled = jnp.where(j > k, dot(inverse, u_ref[j, rows, :]), 0.0)
            r_ref[j, rows, :] = scaled
            l_ref[j, k] = scaled.T
            y_ref[j] -= dot(own, scaled)
        return carry

    lax.fori_loop(0, tiles, step, 0)
    solved = [None] * tiles
    for k in reversed(range(tiles)):
        acc = z_ref[k]
        for j in range(k + 1, tiles):
            acc = acc - dot(solved[j], r_ref[j, k * W : k * W + W, :], ((1,), (1,)))
        solved[k] = acc
        low = lax.broadcasted_iota(jnp.int32, (COARSE, W), 1) < COARSE
        inverse_ref[2 * k] = jnp.where(low, acc, 0.0)
        inverse_ref[2 * k + 1] = jnp.where(low, pltpu.roll(acc, COARSE, 1), 0.0)


def gradient_kernel(
    nr, nb, load_ref, stiffness_ref, local_ref, intact_ref, list_row_ref, list_col_ref,
    basis_ref, inverse_ref, out_ref, k_ref, m_ref, c_ref, ct_ref, sel_ref, selt_ref, col_ref, z_ref, w_ref, acc_ref,
    msg_ref, gather_ref, tot_ref, total_ref, face_ref, near_ref,
    gather_send, gather_recv, total_send, total_recv, face_send, face_recv,
):
    r, b = lax.axis_index("rows"), lax.axis_index("bricks")
    barrier = row_barrier(nb, r, b)
    for t in range(1, nr):
        pl.semaphore_signal(
            barrier, inc=1, device_id=(lax.rem(r + t, nr), b), device_id_type=MESH
        )
    lane8 = lax.broadcasted_iota(jnp.int32, (8, LANES), 1)
    lane1 = lax.broadcasted_iota(jnp.int32, (1, LANES), 1)
    gap = jnp.zeros((NDOF, LANES - NODES), F32)
    intact = intact_ref[...].astype(F32)
    for e in range(6):
        span = slice(e * NODES, e * NODES + NODES)
        part = jnp.concatenate([stiffness_ref[:, span], gap], axis=1)
        mask = jnp.concatenate([intact, gap[:NODES]], axis=1)
        for c in range(6):
            rows = slice(c * NODES, c * NODES + NODES)
            k_ref[e, rows, :] = part[rows] * mask
        m_ref[e] = jnp.concatenate([local_ref[:, span], gap], axis=1)
        piece = jnp.concatenate([basis_ref[:, span], gap[:COARSE]], axis=1)
        c_ref[e] = piece
        turned = jnp.concatenate([piece, jnp.zeros((LANES - COARSE, LANES), F32)], axis=0).T
        ct_ref[span, :] = turned[:NODES]
    node_col = lax.broadcasted_iota(jnp.int32, (LANES, LANES), 0)
    node_row = lax.broadcasted_iota(jnp.int32, (LANES, LANES), 1)
    slots = jnp.broadcast_to(list_row_ref[0:1, :], (LANES, LANES))
    swapped = jnp.broadcast_to(list_row_ref[1:2, :], (LANES, LANES))
    sel_ref[:, :LANES] = (node_col == slots).astype(F32)
    sel_ref[:, LANES:] = (node_col == swapped).astype(F32)
    selt_ref[...] = sel_ref[:NODES, :LANES]
    eye = (node_col == node_row)[:NODES]

    def row_to_col(row, ref):
        for c in range(6):
            spread = jnp.where(eye, jnp.broadcast_to(row[c : c + 1, :], (NODES, LANES)), 0.0)
            ref[c * NODES : c * NODES + NODES, :] = jnp.broadcast_to(
                jnp.sum(spread, axis=1, keepdims=True), (NODES, LANES)
            )

    def stack(rows):
        return jnp.concatenate(rows + [jnp.zeros((8 - len(rows), LANES), F32)], axis=0)

    def col_to_row(ref):
        return stack(
            [
                jnp.sum(jnp.where(eye, ref[c * NODES : c * NODES + NODES, :], 0.0), axis=0, keepdims=True)
                for c in range(6)
            ]
        )

    def row_partners(t):
        return (r, lax.rem(b + t, nb))

    def col_partners(t):
        return (lax.rem(r + t, nr), b)

    def exchange(count, partners, msg, land, send_sem, recv_sem):
        for t in range(1, count):
            pltpu.make_async_remote_copy(
                src_ref=msg, dst_ref=land, send_sem=send_sem, recv_sem=recv_sem,
                device_id=partners(t), device_id_type=MESH,
            ).start()

    def wait_bytes(ref, sem):
        pltpu.make_async_copy(ref, ref, sem).wait()

    def gather_start(n, message):
        msg_ref[n] = message
        gather_ref[n, b] = message
        exchange(
            nb, row_partners, msg_ref.at[n], gather_ref.at[n, b], gather_send.at[n], gather_recv.at[n]
        )

    def gather_wait(n):
        wait_bytes(gather_ref.at[n, pl.ds(0, nb - 1)], gather_recv.at[n])

    def total_start(n):
        acc = gather_ref[n, 0]
        for j in range(1, nb):
            acc = acc + gather_ref[n, j]
        tot_ref[n] = acc
        total_ref[n, r] = acc
        exchange(
            nr, col_partners, tot_ref.at[n], total_ref.at[n, r], total_send.at[n], total_recv.at[n]
        )

    def total_wait(n):
        wait_bytes(total_ref.at[n, pl.ds(0, nr - 1)], total_recv.at[n])
        acc = total_ref[n, 0]
        for j in range(1, nr):
            acc = acc + total_ref[n, j]
        first = jnp.sum(jnp.where(lane1 == COARSE, acc, 0.0), axis=1, keepdims=True)
        second = jnp.sum(jnp.where(lane1 == COARSE + 1, acc, 0.0), axis=1, keepdims=True)
        return first, second

    def reduced(ref):
        return jnp.sum(ref[...] * ct_ref[...], axis=0, keepdims=True)

    def with_dots(message, first, second):
        one = jnp.sum(jnp.sum(first, axis=0, keepdims=True), axis=1, keepdims=True)
        two = jnp.sum(jnp.sum(second, axis=0, keepdims=True), axis=1, keepdims=True)
        message = jnp.where(lane1 == COARSE, one, message)
        return jnp.where(lane1 == COARSE + 1, two, message)

    def local_part(ref):
        return [jnp.sum(ref[...] * m_ref[e], axis=0, keepdims=True) for e in range(6)]

    def coarse_part(n):
        acc = inverse_ref[0] * gather_ref[n, 0]
        for j in range(1, nb):
            acc = acc + inverse_ref[j] * gather_ref[n, j]
        solved = jnp.sum(acc, axis=1, keepdims=True)
        return [jnp.sum(solved * c_ref[e], axis=0, keepdims=True) for e in range(6)]

    neighbours = [
        (lax.rem(r + nr - 1, nr), b, r > 0),
        (lax.rem(r + 1, nr), b, r < nr - 1),
        (r, lax.rem(b + nb - 1, nb), b > 0),
        (r, lax.rem(b + 1, nb), b < nb - 1),
    ]

    def face_start(n, row):
        both = dot(row, sel_ref[...])
        face_ref[n] = both[:, LANES:]
        for d in range(4):
            pltpu.make_async_remote_copy(
                src_ref=face_ref.at[n], dst_ref=near_ref.at[n, d ^ 1],
                send_sem=face_send.at[n, d], recv_sem=face_recv.at[n, d ^ 1],
                device_id=neighbours[d][:2], device_id_type=MESH,
            ).start()
        return both[:, :LANES]

    def operate(n, row, face, target):
        for c in range(6):
            rows = slice(c * NODES, c * NODES + NODES)
            acc = k_ref[0, rows, :] * row[0:1, :]
            for e in range(1, 6):
                acc = acc + k_ref[e, rows, :] * row[e : e + 1, :]
            acc_ref[rows, :] = acc
        stretch = face
        for d in range(4):
            wait_bytes(near_ref.at[n, d], face_recv.at[n, d])
            here = (lane8 >= 32 * d) & (lane8 < 32 * d + 32) & neighbours[d][2]
            stretch = stretch - jnp.where(here, near_ref[n, d], 0.0)
        for c in range(6):
            rows = slice(c * NODES, c * NODES + NODES)
            acc = acc_ref[rows, :] + selt_ref[...] * stretch[c : c + 1, :]
            target[rows, :] = jnp.broadcast_to(
                jnp.sum(acc, axis=1, keepdims=True), (NODES, LANES)
            )

    load = stack([jnp.concatenate([load_ref[:, c * NODES : c * NODES + NODES], gap[:1]], axis=1) for c in range(6)])
    row_to_col(load, col_ref)
    pl.semaphore_wait(barrier, nb + nr - 2)

    res = load
    gather_start(0, reduced(col_ref))
    part = local_part(col_ref)
    gather_wait(0)
    u = stack([x + y for x, y in zip(part, coarse_part(0))])
    face = face_start(0, u)
    operate(0, u, face, w_ref)
    w = col_to_row(w_ref)
    p = s = q = sol = None
    dot_old = step_old = None
    for i in range(2):
        gather_start(i + 1, with_dots(reduced(w_ref), res * u, w * u))
        part = local_part(w_ref)
        gather_wait(i + 1)
        total_start(i + 1)
        m = stack([x + y for x, y in zip(part, coarse_part(i + 1))])
        face = face_start(i + 1, m)
        operate(i + 1, m, face, col_ref)
        v = col_to_row(col_ref)
        gamma, delta = total_wait(i + 1)
        if i == 0:
            step_size = gamma / delta
            p, s, q, zr = u, w, m, v
            z_ref[...] = col_ref[...]
            sol = step_size * p
        else:
            ratio = gamma / dot_old
            step_size = gamma / (delta - ratio * gamma / step_old)
            p, s, q, zr = u + ratio * p, w + ratio * s, m + ratio * q, v + ratio * zr
            sol = sol + step_size * p
        res = res - step_size * s
        u = u - step_size * q
        w = w - step_size * zr
        if i == 0:
            w_ref[...] = w_ref[...] - step_size * z_ref[...]
        dot_old, step_old = gamma, step_size
    gather_start(3, with_dots(jnp.zeros((1, LANES), F32), res * u, w * u))
    gather_wait(3)
    total_start(3)
    gamma, delta = total_wait(3)
    ratio = gamma / dot_old
    step_size = gamma / (delta - ratio * gamma / step_old)
    out_ref[0] = sol + step_size * (u + ratio * p)
    out_ref[1] = res - step_size * (w + ratio * s)

    for n in range(4):
        wait_bytes(gather_ref.at[n, pl.ds(0, nb - 1)], gather_send.at[n])
    for n in range(1, 4):
        wait_bytes(total_ref.at[n, pl.ds(0, nr - 1)], total_send.at[n])
    for n in range(3):
        for d in range(4):
            wait_bytes(face_ref.at[n], face_send.at[n, d])


VMEM = pl.BlockSpec(memory_space=pltpu.VMEM)
SMEM = pl.BlockSpec(memory_space=pltpu.SMEM)


def body(nr, nb, load, stiffness, local_inverse, intact, face_lists, coarse_basis, matrix, pattern):
    tiles = nb // 2
    order = nb * COARSE
    limit = 48 * 1024 * 1024
    whole = pl.pallas_call(
        functools.partial(spread_kernel, nb),
        out_shape=jax.ShapeDtypeStruct((tiles, order, LANES), F32),
        in_specs=[SMEM, VMEM],
        out_specs=VMEM,
        scratch_shapes=[pltpu.SemaphoreType.DMA((nb,)), pltpu.SemaphoreType.DMA((nb,))],
        compiler_params=pltpu.CompilerParams(
            collective_id=0, has_side_effects=True, vmem_limit_bytes=limit
        ),
        name="spread",
    )(pattern.reshape(1, nb), matrix.reshape(nb, COARSE, COARSE))
    inverse = pl.pallas_call(
        functools.partial(factor_kernel, nb),
        out_shape=jax.ShapeDtypeStruct((nb, COARSE, LANES), F32),
        in_specs=[VMEM],
        out_specs=VMEM,
        scratch_shapes=[
            pltpu.VMEM((tiles, order, LANES), F32),
            pltpu.VMEM((tiles, order, LANES), F32),
            pltpu.VMEM((tiles, tiles, W, W), F32),
            pltpu.VMEM((tiles, COARSE, W), F32),
            pltpu.VMEM((tiles, COARSE, W), F32),
        ],
        compiler_params=pltpu.CompilerParams(vmem_limit_bytes=limit),
        name="factor",
    )(whole)
    padded = jnp.pad(face_lists.reshape(4, FACE), ((0, 0), (0, 32 - FACE)), constant_values=-1)
    swapped = jnp.stack([padded[1], padded[0], padded[3], padded[2]])
    lists = jnp.stack([padded.reshape(LANES), swapped.reshape(LANES)])
    out = pl.pallas_call(
        functools.partial(gradient_kernel, nr, nb),
        out_shape=jax.ShapeDtypeStruct((2, 8, LANES), F32),
        in_specs=[VMEM] * 8,
        out_specs=VMEM,
        scratch_shapes=[
            pltpu.VMEM((6, NDOF, LANES), F32),
            pltpu.VMEM((6, NDOF, LANES), F32),
            pltpu.VMEM((6, COARSE, LANES), F32),
            pltpu.VMEM((NDOF, LANES), F32),
            pltpu.VMEM((LANES, 2 * LANES), F32),
            pltpu.VMEM((NODES, LANES), F32),
            pltpu.VMEM((NDOF, LANES), F32),
            pltpu.VMEM((NDOF, LANES), F32),
            pltpu.VMEM((NDOF, LANES), F32),
            pltpu.VMEM((NDOF, LANES), F32),
            pltpu.VMEM((4, 1, LANES), F32),
            pltpu.VMEM((4, nb, 1, LANES), F32),
            pltpu.VMEM((4, 1, LANES), F32),
            pltpu.VMEM((4, nr, 1, LANES), F32),
            pltpu.VMEM((3, 8, LANES), F32),
            pltpu.VMEM((3, 4, 8, LANES), F32),
            pltpu.SemaphoreType.DMA((4,)),
            pltpu.SemaphoreType.DMA((4,)),
            pltpu.SemaphoreType.DMA((4,)),
            pltpu.SemaphoreType.DMA((4,)),
            pltpu.SemaphoreType.DMA((3, 4)),
            pltpu.SemaphoreType.DMA((3, 4)),
        ],
        compiler_params=pltpu.CompilerParams(
            collective_id=1, has_side_effects=True, vmem_limit_bytes=limit
        ),
        name="gradients",
    )(
        load.reshape(1, NDOF),
        stiffness.reshape(NDOF, NDOF),
        local_inverse.reshape(NDOF, NDOF),
        intact.reshape(NODES, NODES),
        lists,
        padded.reshape(LANES, 1),
        coarse_basis.reshape(COARSE, NDOF),
        inverse,
    )
    flat = out[:, :6, :NODES].reshape(2, 1, 1, NDOF)
    return flat[0], flat[1]


def solution(mesh):
    in_specs = (
        P("rows", "bricks", None),
        P("rows", "bricks", None, None),
        P("rows", "bricks", None, None),
        P("rows", "bricks", None, None),
        P("rows", "bricks", None, None),
        P("rows", "bricks", None, None),
        P("rows", "bricks", None, None, None),
        P("rows", "bricks", None),
    )
    out_specs = (P("rows", "bricks", None), P("rows", "bricks", None))
    run = functools.partial(body, mesh.shape["rows"], mesh.shape["bricks"])
    return jax.shard_map(run, mesh=mesh, in_specs=in_specs, out_specs=out_specs, check_vma=False)
```

```python
import functools

import jax
import jax.numpy as jnp
from jax import lax
from jax.experimental import pallas as pl
from jax.experimental.pallas import tpu as pltpu
from jax.sharding import PartitionSpec as P

MESH = pl.DeviceIdType.MESH
HI = lax.Precision.HIGHEST
F32 = jnp.float32
NODES, NDOF, COARSE, FACE, W = 96, 576, 64, 24, 128
LANES = 128


def dot(a, b, dims=((1,), (0,))):
    return lax.dot_general(a, b, (dims, ((), ())), precision=HI, preferred_element_type=F32)


def small_product(a, b):
    out = []
    for row in a:
        line = []
        for j in range(len(b[0])):
            acc = row[0] * b[0][j]
            for k in range(1, len(b)):
                acc = acc + row[k] * b[k][j]
            line.append(acc)
        out.append(line)
    return out


def small_inverse(m):
    n = len(m)
    if n == 2:
        a, b, d = m[0][0], m[0][1], m[1][1]
        r = 1.0 / (a * d - b * b)
        off = -(b * r)
        return [[d * r, off], [off, a * r]]
    h = n // 2
    b = [row[h:] for row in m[:h]]
    e = small_inverse([row[:h] for row in m[:h]])
    w = small_product(e, b)
    s = [[None] * h for _ in range(h)]
    for i in range(h):
        for j in range(i, h):
            acc = b[0][i] * w[0][j]
            for k in range(1, h):
                acc = acc + b[k][i] * w[k][j]
            s[i][j] = s[j][i] = m[h + i][h + j] - acc
    t = small_inverse(s)
    x = small_product(w, t)
    top = [[None] * h for _ in range(h)]
    for i in range(h):
        for j in range(i, h):
            acc = x[i][0] * w[j][0]
            for k in range(1, h):
                acc = acc + x[i][k] * w[j][k]
            top[i][j] = top[j][i] = e[i][j] + acc
    neg = [[-v for v in row] for row in x]
    out = [top[i] + neg[i] for i in range(h)]
    out += [[neg[k][i] for k in range(h)] + t[i] for i in range(h)]
    return out


def pivot_groups(count, v):
    shape = (8, LANES)
    sub = lax.broadcasted_iota(jnp.int32, shape, 0)
    lane = lax.broadcasted_iota(jnp.int32, shape, 1)
    v = list(v)
    for g in range(count):
        p = 8 * g
        x = v[g]
        turn = LANES - 8 * count if g == count - 1 else 0
        rows = [jnp.broadcast_to(x[i : i + 1, :], shape) for i in range(8)]
        cols = [jnp.broadcast_to(x[:, p + t : p + t + 1], shape) for t in range(8)]
        m = [[None] * 8 for _ in range(8)]
        for i in range(8):
            for j in range(i, 8):
                m[i][j] = m[j][i] = jnp.broadcast_to(cols[j][i : i + 1, :], shape)
        e = small_inverse(m)
        pivots = (lane >= p) & (lane < p + 8)
        r = [jnp.where(pivots, (lane == p + i).astype(F32), rows[i]) for i in range(8)]
        q = []
        for i in range(8):
            acc = e[i][0] * r[0]
            for j in range(1, 8):
                acc = acc + e[i][j] * r[j]
            q.append(acc)
        new = []
        for k in range(len(v)):
            y = v[k]
            if k == g:
                y = q[0]
                for t in range(1, 8):
                    y = jnp.where(sub == t, q[t], y)
            else:
                acc = jnp.broadcast_to(y[:, p : p + 1], shape) * q[0]
                for t in range(1, 8):
                    acc = acc + jnp.broadcast_to(y[:, p + t : p + t + 1], shape) * q[t]
                y = jnp.where(pivots, 0.0, y) - acc
            new.append(pltpu.roll(y, turn, 1) if turn else y)
        v = new
    return tuple(v[count:] + v[:count])


RUN = 4


class Spread:
    def __init__(self, nb, r, b, all_ref, sems):
        self.nb, self.tiles, self.nx = nb, nb // 2, nb // RUN
        self.r, self.b, self.x, self.z = r, b, lax.div(b, RUN), lax.rem(b, RUN)
        self.all_ref = all_ref
        self.send1, self.recv1, self.send2, self.recv2 = sems

    def slot(self, j, brick, count):
        start = pl.multiple_of(brick * COARSE, COARSE)
        return self.all_ref.at[j, pl.ds(start, count * COARSE), :]

    def copy1(self, j, t):
        part = self.slot(j, self.b, 1)
        z = lax.rem(self.z + t, RUN)
        return pltpu.make_async_remote_copy(
            src_ref=part, dst_ref=part, send_sem=self.send1.at[j, t], recv_sem=self.recv1.at[j, self.z],
            device_id=(self.r, self.x * RUN + z), device_id_type=MESH,
        )

    def copy2(self, j, t, count):
        part = self.slot(j, self.x * RUN, count)
        x = lax.rem(self.x + t, self.nx)
        return pltpu.make_async_remote_copy(
            src_ref=part, dst_ref=part, send_sem=self.send2.at[j, t], recv_sem=self.recv2.at[j, self.x],
            device_id=(self.r, x * RUN + self.z), device_id_type=MESH,
        )

    def each1(self, j, act):
        @pl.when(lax.div(self.b, 2) <= j)
        def _():
            for t in range(1, RUN):
                act(self.copy1(j, t))

    def each2(self, j, act):
        for count, when in ((RUN, 2 * self.x + 1 <= j), (2, 2 * self.x == j)):

            @pl.when(when)
            def _():
                for t in range(1, self.nx):
                    act(self.copy2(j, t, count))

    def first(self, j):
        self.each1(j, lambda copy: copy.start())

    def second(self, j):
        for z in range(RUN):

            @pl.when((self.z != z) & (2 * self.x + z // 2 <= j))
            def _():
                part = self.slot(j, self.x * RUN + z, 1)
                pltpu.make_async_copy(part, part, self.recv1.at[j, z]).wait()

        self.each2(j, lambda copy: copy.start())

    def need(self, j):
        for x in range(self.nx):
            for count, when in ((RUN, 2 * x + 1 <= j), (2, 2 * x == j)):

                @pl.when((self.x != x) & when)
                def _():
                    part = self.slot(j, x * RUN, count)
                    pltpu.make_async_copy(part, part, self.recv2.at[j, x]).wait()

    def finish(self):
        for j in range(self.tiles):
            self.each1(j, lambda copy: copy.wait_send())
            self.each2(j, lambda copy: copy.wait_send())


def factor(nb, b, spread, all_ref, inverse_ref, u_ref, r_ref, l_ref, y_ref, z_ref, p_ref, d_ref):
    tiles = nb // 2
    sub = lax.broadcasted_iota(jnp.int32, (COARSE, W), 0)
    lane = lax.broadcasted_iota(jnp.int32, (COARSE, W), 1)
    groups = W // 8
    unroll = 2

    def tile(k):
        return pl.ds(pl.multiple_of(k * W, W), W)

    def step(k, depth, column):
        if column:
            j = k + 1
            spread.need(j)

            @pl.when(k + 3 < tiles)
            def _():
                spread.second(k + 3)

        def run(it, v):
            if column:
                i = jnp.minimum(it, k)
                u = all_ref[j, tile(i), :] - dot(l_ref[i, :, :depth], u_ref[j, :depth, :])
                u_ref[j, tile(i), :] = u
                scaled = dot(p_ref[i], u)
                r_ref[j, tile(i), :] = scaled
                l_ref[j, :, tile(i)] = scaled.T
            return pivot_groups(unroll, v)

        block = tuple(d_ref[8 * i : 8 * i + 8, :] for i in range(groups))
        inverse = jnp.concatenate(lax.fori_loop(0, groups // unroll, run, block), axis=0)
        p_ref[k] = inverse
        if column:
            scaled = dot(inverse, u_ref[j, tile(k), :])
            r_ref[j, tile(k), :] = scaled
            l_ref[j, :, tile(k)] = scaled.T
            d_ref[...] = all_ref[j, tile(j), :] - dot(l_ref[j, :, :depth], u_ref[j, :depth, :])
        own = (lane + k * W == sub + b * COARSE).astype(F32)
        own = own - dot(y_ref[:, :depth], r_ref[k, :depth, :])
        y_ref[:, tile(k)] = own
        z_ref[k] = dot(own, inverse)

    def loop(start, stop):
        def run(k, carry):
            step(k, stop * W, True)
            return carry

        lax.fori_loop(start, stop, run, 0)

    spread.need(0)
    d_ref[...] = all_ref[0, :W, :]
    loop(0, tiles // 2)
    loop(tiles // 2, tiles - 1)
    step(tiles - 1, (tiles - 1) * W, False)
    solved = [None] * tiles
    low = lane < COARSE
    for k in reversed(range(tiles)):
        acc = z_ref[k]
        for j in range(k + 1, tiles):
            acc = acc - dot(solved[j], r_ref[j, k * W : k * W + W, :], ((1,), (1,)))
        solved[k] = acc
        inverse_ref[2 * k] = jnp.where(low, acc, 0.0)
        inverse_ref[2 * k + 1] = jnp.where(low, pltpu.roll(acc, COARSE, 1), 0.0)


def whole_kernel(
    nr, nb, pattern_ref, matrix_ref, load_ref, stiffness_ref, local_ref, intact_ref, list_row_ref,
    basis_ref, out_ref, all_ref, inverse_ref, u_ref, r_ref, l_ref, y_ref, zf_ref, p_ref, d_ref,
    k_ref, m_ref, c_ref, ct_ref, sel_ref, selt_ref, col_ref, z_ref, w_ref, acc_ref,
    msg_ref, gather_ref, tot_ref, total_ref, face_ref, near_ref, send1, recv1, send2, recv2,
    gather_send, gather_recv, total_send, total_recv, face_send, face_recv,
):
    r, b = lax.axis_index("rows"), lax.axis_index("bricks")
    tiles = nb // 2
    barrier = pltpu.get_barrier_semaphore()
    for t in range(1, nb):
        pl.semaphore_signal(
            barrier, inc=1, device_id=(r, lax.rem(b + t, nb)), device_id_type=MESH
        )
    for t in range(1, nr):
        pl.semaphore_signal(
            barrier, inc=1, device_id=(lax.rem(r + t, nr), b), device_id_type=MESH
        )
    mine = pl.ds(pl.multiple_of(b * COARSE, COARSE), COARSE)
    for j in range(tiles):
        left = matrix_ref[2 * j] * pattern_ref[0, 2 * j].astype(F32)
        right = matrix_ref[2 * j + 1] * pattern_ref[0, 2 * j + 1].astype(F32)
        all_ref[j, mine, :] = jnp.concatenate([left, right], axis=1)
    spread = Spread(nb, r, b, all_ref, (send1, recv1, send2, recv2))
    pl.semaphore_wait(barrier, nb + nr - 2)
    for j in range(tiles):
        spread.first(j)
    for ref in (u_ref, r_ref, l_ref, p_ref):
        for j in range(tiles):
            ref[j] = jnp.zeros(ref.shape[1:], F32)
    y_ref[...] = jnp.zeros(y_ref.shape, F32)
    for j in range(min(3, tiles)):
        spread.second(j)
    lane8 = lax.broadcasted_iota(jnp.int32, (8, LANES), 1)
    lane1 = lax.broadcasted_iota(jnp.int32, (1, LANES), 1)
    gap = jnp.zeros((NDOF, LANES - NODES), F32)
    intact = intact_ref[...].astype(F32)
    for e in range(6):
        span = slice(e * NODES, e * NODES + NODES)
        part = jnp.concatenate([stiffness_ref[:, span], gap], axis=1)
        mask = jnp.concatenate([intact, gap[:NODES]], axis=1)
        for c in range(6):
            rows = slice(c * NODES, c * NODES + NODES)
            k_ref[e, rows, :] = part[rows] * mask
        m_ref[e] = jnp.concatenate([local_ref[:, span], gap], axis=1)
        piece = jnp.concatenate([basis_ref[:, span], gap[:COARSE]], axis=1)
        c_ref[e] = piece
        turned = jnp.concatenate([piece, jnp.zeros((LANES - COARSE, LANES), F32)], axis=0).T
        ct_ref[span, :] = turned[:NODES]
    node_col = lax.broadcasted_iota(jnp.int32, (LANES, LANES), 0)
    node_row = lax.broadcasted_iota(jnp.int32, (LANES, LANES), 1)
    slots = jnp.broadcast_to(list_row_ref[0:1, :], (LANES, LANES))
    swapped = jnp.broadcast_to(list_row_ref[1:2, :], (LANES, LANES))
    sel_ref[:, :LANES] = (node_col == slots).astype(F32)
    sel_ref[:, LANES:] = (node_col == swapped).astype(F32)
    selt_ref[...] = sel_ref[:NODES, :LANES]
    eye = (node_col == node_row)[:NODES]

    def row_to_col(row, ref):
        for c in range(6):
            spread = jnp.where(eye, jnp.broadcast_to(row[c : c + 1, :], (NODES, LANES)), 0.0)
            ref[c * NODES : c * NODES + NODES, :] = jnp.broadcast_to(
                jnp.sum(spread, axis=1, keepdims=True), (NODES, LANES)
            )

    def stack(rows):
        return jnp.concatenate(rows + [jnp.zeros((8 - len(rows), LANES), F32)], axis=0)

    def col_to_row(ref):
        return stack(
            [
                jnp.sum(jnp.where(eye, ref[c * NODES : c * NODES + NODES, :], 0.0), axis=0, keepdims=True)
                for c in range(6)
            ]
        )

    def row_partners(t):
        return (r, lax.rem(b + t, nb))

    def col_partners(t):
        return (lax.rem(r + t, nr), b)

    def exchange(count, partners, msg, land, send_sem, recv_sem):
        for t in range(1, count):
            pltpu.make_async_remote_copy(
                src_ref=msg, dst_ref=land, send_sem=send_sem, recv_sem=recv_sem,
                device_id=partners(t), device_id_type=MESH,
            ).start()

    def wait_bytes(ref, sem):
        pltpu.make_async_copy(ref, ref, sem).wait()

    def gather_start(n, message):
        msg_ref[n] = message
        gather_ref[n, b] = message
        exchange(
            nb, row_partners, msg_ref.at[n], gather_ref.at[n, b], gather_send.at[n], gather_recv.at[n]
        )

    def gather_wait(n):
        wait_bytes(gather_ref.at[n, pl.ds(0, nb - 1)], gather_recv.at[n])

    def total_start(n):
        acc = gather_ref[n, 0]
        for j in range(1, nb):
            acc = acc + gather_ref[n, j]
        tot_ref[n] = acc
        total_ref[n, r] = acc
        exchange(
            nr, col_partners, tot_ref.at[n], total_ref.at[n, r], total_send.at[n], total_recv.at[n]
        )

    def total_wait(n):
        wait_bytes(total_ref.at[n, pl.ds(0, nr - 1)], total_recv.at[n])
        acc = total_ref[n, 0]
        for j in range(1, nr):
            acc = acc + total_ref[n, j]
        first = jnp.sum(jnp.where(lane1 == COARSE, acc, 0.0), axis=1, keepdims=True)
        second = jnp.sum(jnp.where(lane1 == COARSE + 1, acc, 0.0), axis=1, keepdims=True)
        return first, second

    def reduced(ref):
        return jnp.sum(ref[...] * ct_ref[...], axis=0, keepdims=True)

    def with_dots(message, first, second):
        one = jnp.sum(jnp.sum(first, axis=0, keepdims=True), axis=1, keepdims=True)
        two = jnp.sum(jnp.sum(second, axis=0, keepdims=True), axis=1, keepdims=True)
        message = jnp.where(lane1 == COARSE, one, message)
        return jnp.where(lane1 == COARSE + 1, two, message)

    def local_part(ref):
        return [jnp.sum(ref[...] * m_ref[e], axis=0, keepdims=True) for e in range(6)]

    def coarse_part(n):
        acc = inverse_ref[0] * gather_ref[n, 0]
        for j in range(1, nb):
            acc = acc + inverse_ref[j] * gather_ref[n, j]
        solved = jnp.sum(acc, axis=1, keepdims=True)
        return [jnp.sum(solved * c_ref[e], axis=0, keepdims=True) for e in range(6)]

    neighbours = [
        (lax.rem(r + nr - 1, nr), b, r > 0),
        (lax.rem(r + 1, nr), b, r < nr - 1),
        (r, lax.rem(b + nb - 1, nb), b > 0),
        (r, lax.rem(b + 1, nb), b < nb - 1),
    ]

    def face_start(n, row):
        both = dot(row, sel_ref[...])
        face_ref[n] = both[:, LANES:]
        for d in range(4):
            pltpu.make_async_remote_copy(
                src_ref=face_ref.at[n], dst_ref=near_ref.at[n, d ^ 1],
                send_sem=face_send.at[n, d], recv_sem=face_recv.at[n, d ^ 1],
                device_id=neighbours[d][:2], device_id_type=MESH,
            ).start()
        return both[:, :LANES]

    def operate(n, row, face, target):
        for c in range(6):
            rows = slice(c * NODES, c * NODES + NODES)
            acc = k_ref[0, rows, :] * row[0:1, :]
            for e in range(1, 6):
                acc = acc + k_ref[e, rows, :] * row[e : e + 1, :]
            acc_ref[rows, :] = acc
        stretch = face
        for d in range(4):
            wait_bytes(near_ref.at[n, d], face_recv.at[n, d])
            here = (lane8 >= 32 * d) & (lane8 < 32 * d + 32) & neighbours[d][2]
            stretch = stretch - jnp.where(here, near_ref[n, d], 0.0)
        for c in range(6):
            rows = slice(c * NODES, c * NODES + NODES)
            acc = acc_ref[rows, :] + selt_ref[...] * stretch[c : c + 1, :]
            target[rows, :] = jnp.broadcast_to(
                jnp.sum(acc, axis=1, keepdims=True), (NODES, LANES)
            )

    load = stack([jnp.concatenate([load_ref[:, c * NODES : c * NODES + NODES], gap[:1]], axis=1) for c in range(6)])
    row_to_col(load, col_ref)
    factor(nb, b, spread, all_ref, inverse_ref, u_ref, r_ref, l_ref, y_ref, zf_ref, p_ref, d_ref)

    res = load
    gather_start(0, reduced(col_ref))
    part = local_part(col_ref)
    gather_wait(0)
    u = stack([x + y for x, y in zip(part, coarse_part(0))])
    face = face_start(0, u)
    operate(0, u, face, w_ref)
    w = col_to_row(w_ref)
    p = s = q = sol = None
    dot_old = step_old = None
    for i in range(2):
        gather_start(i + 1, with_dots(reduced(w_ref), res * u, w * u))
        part = local_part(w_ref)
        gather_wait(i + 1)
        total_start(i + 1)
        m = stack([x + y for x, y in zip(part, coarse_part(i + 1))])
        face = face_start(i + 1, m)
        operate(i + 1, m, face, col_ref)
        v = col_to_row(col_ref)
        gamma, delta = total_wait(i + 1)
        if i == 0:
            step_size = gamma / delta
            p, s, q, zr = u, w, m, v
            z_ref[...] = col_ref[...]
            sol = step_size * p
        else:
            ratio = gamma / dot_old
            step_size = gamma / (delta - ratio * gamma / step_old)
            p, s, q, zr = u + ratio * p, w + ratio * s, m + ratio * q, v + ratio * zr
            sol = sol + step_size * p
        res = res - step_size * s
        u = u - step_size * q
        w = w - step_size * zr
        if i == 0:
            w_ref[...] = w_ref[...] - step_size * z_ref[...]
        dot_old, step_old = gamma, step_size
    gather_start(3, with_dots(jnp.zeros((1, LANES), F32), res * u, w * u))
    gather_wait(3)
    total_start(3)
    gamma, delta = total_wait(3)
    ratio = gamma / dot_old
    step_size = gamma / (delta - ratio * gamma / step_old)
    out_ref[0] = sol + step_size * (u + ratio * p)
    out_ref[1] = res - step_size * (w + ratio * s)

    spread.finish()
    for n in range(4):
        wait_bytes(gather_ref.at[n, pl.ds(0, nb - 1)], gather_send.at[n])
    for n in range(1, 4):
        wait_bytes(total_ref.at[n, pl.ds(0, nr - 1)], total_send.at[n])
    for n in range(3):
        for d in range(4):
            wait_bytes(face_ref.at[n], face_send.at[n, d])


VMEM = pl.BlockSpec(memory_space=pltpu.VMEM)
SMEM = pl.BlockSpec(memory_space=pltpu.SMEM)


def body(nr, nb, load, stiffness, local_inverse, intact, face_lists, coarse_basis, matrix, pattern):
    tiles = nb // 2
    order = nb * COARSE
    limit = 48 * 1024 * 1024
    padded = jnp.pad(face_lists.reshape(4, FACE), ((0, 0), (0, 32 - FACE)), constant_values=-1)
    swapped = jnp.stack([padded[1], padded[0], padded[3], padded[2]])
    lists = jnp.stack([padded.reshape(LANES), swapped.reshape(LANES)])
    out = pl.pallas_call(
        functools.partial(whole_kernel, nr, nb),
        out_shape=jax.ShapeDtypeStruct((2, 8, LANES), F32),
        in_specs=[SMEM] + [VMEM] * 7,
        out_specs=VMEM,
        scratch_shapes=[
            pltpu.VMEM((tiles, order, LANES), F32),
            pltpu.VMEM((nb, COARSE, LANES), F32),
            pltpu.VMEM((tiles, order, LANES), F32),
            pltpu.VMEM((tiles, order, LANES), F32),
            pltpu.VMEM((tiles, W, order), F32),
            pltpu.VMEM((COARSE, order), F32),
            pltpu.VMEM((tiles, COARSE, W), F32),
            pltpu.VMEM((tiles, W, W), F32),
            pltpu.VMEM((W, W), F32),
            pltpu.VMEM((6, NDOF, LANES), F32),
            pltpu.VMEM((6, NDOF, LANES), F32),
            pltpu.VMEM((6, COARSE, LANES), F32),
            pltpu.VMEM((NDOF, LANES), F32),
            pltpu.VMEM((LANES, 2 * LANES), F32),
            pltpu.VMEM((NODES, LANES), F32),
            pltpu.VMEM((NDOF, LANES), F32),
            pltpu.VMEM((NDOF, LANES), F32),
            pltpu.VMEM((NDOF, LANES), F32),
            pltpu.VMEM((NDOF, LANES), F32),
            pltpu.VMEM((4, 1, LANES), F32),
            pltpu.VMEM((4, nb, 1, LANES), F32),
            pltpu.VMEM((4, 1, LANES), F32),
            pltpu.VMEM((4, nr, 1, LANES), F32),
            pltpu.VMEM((3, 8, LANES), F32),
            pltpu.VMEM((3, 4, 8, LANES), F32),
            pltpu.SemaphoreType.DMA((tiles, RUN)),
            pltpu.SemaphoreType.DMA((tiles, RUN)),
            pltpu.SemaphoreType.DMA((tiles, nb // RUN)),
            pltpu.SemaphoreType.DMA((tiles, nb // RUN)),
            pltpu.SemaphoreType.DMA((4,)),
            pltpu.SemaphoreType.DMA((4,)),
            pltpu.SemaphoreType.DMA((4,)),
            pltpu.SemaphoreType.DMA((4,)),
            pltpu.SemaphoreType.DMA((3, 4)),
            pltpu.SemaphoreType.DMA((3, 4)),
        ],
        compiler_params=pltpu.CompilerParams(
            collective_id=0, has_side_effects=True, vmem_limit_bytes=limit
        ),
        name="whole",
    )(
        pattern.reshape(1, nb),
        matrix.reshape(nb, COARSE, COARSE),
        load.reshape(1, NDOF),
        stiffness.reshape(NDOF, NDOF),
        local_inverse.reshape(NDOF, NDOF),
        intact.reshape(NODES, NODES),
        lists,
        coarse_basis.reshape(COARSE, NDOF),
    )
    flat = out[:, :6, :NODES].reshape(2, 1, 1, NDOF)
    return flat[0], flat[1]


def solution(mesh):
    in_specs = (
        P("rows", "bricks", None),
        P("rows", "bricks", None, None),
        P("rows", "bricks", None, None),
        P("rows", "bricks", None, None),
        P("rows", "bricks", None, None),
        P("rows", "bricks", None, None),
        P("rows", "bricks", None, None, None),
        P("rows", "bricks", None),
    )
    out_specs = (P("rows", "bricks", None), P("rows", "bricks", None))
    run = functools.partial(body, mesh.shape["rows"], mesh.shape["bricks"])
    return jax.shard_map(run, mesh=mesh, in_specs=in_specs, out_specs=out_specs, check_vma=False)
```

```python
import functools

import jax
import jax.numpy as jnp
from jax import lax
from jax.experimental import pallas as pl
from jax.experimental.pallas import tpu as pltpu
from jax.sharding import PartitionSpec as P

MESH = pl.DeviceIdType.MESH
HI = lax.Precision.HIGHEST
F32 = jnp.float32
NODES, NDOF, COARSE, FACE, W = 96, 576, 64, 24, 128
LANES = 128


def dot(a, b, dims=((1,), (0,))):
    return lax.dot_general(a, b, (dims, ((), ())), precision=HI, preferred_element_type=F32)


def small_product(a, b):
    out = []
    for row in a:
        line = []
        for j in range(len(b[0])):
            acc = row[0] * b[0][j]
            for k in range(1, len(b)):
                acc = acc + row[k] * b[k][j]
            line.append(acc)
        out.append(line)
    return out


def small_inverse(m):
    n = len(m)
    if n == 2:
        a, b, d = m[0][0], m[0][1], m[1][1]
        r = 1.0 / (a * d - b * b)
        off = -(b * r)
        return [[d * r, off], [off, a * r]]
    h = n // 2
    b = [row[h:] for row in m[:h]]
    e = small_inverse([row[:h] for row in m[:h]])
    w = small_product(e, b)
    s = [[None] * h for _ in range(h)]
    for i in range(h):
        for j in range(i, h):
            acc = b[0][i] * w[0][j]
            for k in range(1, h):
                acc = acc + b[k][i] * w[k][j]
            s[i][j] = s[j][i] = m[h + i][h + j] - acc
    t = small_inverse(s)
    x = small_product(w, t)
    top = [[None] * h for _ in range(h)]
    for i in range(h):
        for j in range(i, h):
            acc = x[i][0] * w[j][0]
            for k in range(1, h):
                acc = acc + x[i][k] * w[j][k]
            top[i][j] = top[j][i] = e[i][j] + acc
    neg = [[-v for v in row] for row in x]
    out = [top[i] + neg[i] for i in range(h)]
    out += [[neg[k][i] for k in range(h)] + t[i] for i in range(h)]
    return out


def pivot_groups(count, v):
    shape = (8, LANES)
    sub = lax.broadcasted_iota(jnp.int32, shape, 0)
    lane = lax.broadcasted_iota(jnp.int32, shape, 1)
    v = list(v)
    for g in range(count):
        p = 8 * g
        x = v[g]
        turn = LANES - 8 * count if g == count - 1 else 0
        rows = [jnp.broadcast_to(x[i : i + 1, :], shape) for i in range(8)]
        cols = [jnp.broadcast_to(x[:, p + t : p + t + 1], shape) for t in range(8)]
        m = [[None] * 8 for _ in range(8)]
        for i in range(8):
            for j in range(i, 8):
                m[i][j] = m[j][i] = jnp.broadcast_to(cols[j][i : i + 1, :], shape)
        e = small_inverse(m)
        pivots = (lane >= p) & (lane < p + 8)
        r = [jnp.where(pivots, (lane == p + i).astype(F32), rows[i]) for i in range(8)]
        q = []
        for i in range(8):
            acc = e[i][0] * r[0]
            for j in range(1, 8):
                acc = acc + e[i][j] * r[j]
            q.append(acc)
        new = []
        for k in range(len(v)):
            y = v[k]
            if k == g:
                y = q[0]
                for t in range(1, 8):
                    y = jnp.where(sub == t, q[t], y)
            else:
                acc = jnp.broadcast_to(y[:, p : p + 1], shape) * q[0]
                for t in range(1, 8):
                    acc = acc + jnp.broadcast_to(y[:, p + t : p + t + 1], shape) * q[t]
                y = jnp.where(pivots, 0.0, y) - acc
            new.append(pltpu.roll(y, turn, 1) if turn else y)
        v = new
    return tuple(v[count:] + v[:count])


RUN = 4


class Spread:
    def __init__(self, nb, r, b, all_ref, sems):
        self.nb, self.tiles, self.nx = nb, nb // 2, nb // RUN
        self.r, self.b, self.x, self.z = r, b, lax.div(b, RUN), lax.rem(b, RUN)
        self.all_ref = all_ref
        self.send1, self.recv1, self.send2, self.recv2 = sems

    def slot(self, j, brick, count):
        start = pl.multiple_of(brick * COARSE, COARSE)
        return self.all_ref.at[j, pl.ds(start, count * COARSE), :]

    def copy1(self, j, t):
        part = self.slot(j, self.b, 1)
        z = lax.rem(self.z + t, RUN)
        return pltpu.make_async_remote_copy(
            src_ref=part, dst_ref=part, send_sem=self.send1.at[j, t], recv_sem=self.recv1.at[j, self.z],
            device_id=(self.r, self.x * RUN + z), device_id_type=MESH,
        )

    def copy2(self, j, t, count):
        part = self.slot(j, self.x * RUN, count)
        x = lax.rem(self.x + t, self.nx)
        return pltpu.make_async_remote_copy(
            src_ref=part, dst_ref=part, send_sem=self.send2.at[j, t], recv_sem=self.recv2.at[j, self.x],
            device_id=(self.r, x * RUN + self.z), device_id_type=MESH,
        )

    def each1(self, j, act):
        @pl.when(lax.div(self.b, 2) <= j)
        def _():
            for t in range(1, RUN):
                act(self.copy1(j, t))

    def each2(self, j, act):
        for count, when in ((RUN, 2 * self.x + 1 <= j), (2, 2 * self.x == j)):

            @pl.when(when)
            def _():
                for t in range(1, self.nx):
                    act(self.copy2(j, t, count))

    def first(self, j):
        self.each1(j, lambda copy: copy.start())

    def second(self, j):
        for z in range(RUN):

            @pl.when((self.z != z) & (2 * self.x + z // 2 <= j))
            def _():
                part = self.slot(j, self.x * RUN + z, 1)
                pltpu.make_async_copy(part, part, self.recv1.at[j, z]).wait()

        self.each2(j, lambda copy: copy.start())

    def need(self, j):
        for x in range(self.nx):
            for count, when in ((RUN, 2 * x + 1 <= j), (2, 2 * x == j)):

                @pl.when((self.x != x) & when)
                def _():
                    part = self.slot(j, x * RUN, count)
                    pltpu.make_async_copy(part, part, self.recv2.at[j, x]).wait()

    def finish(self):
        for j in range(self.tiles):
            self.each1(j, lambda copy: copy.wait_send())
            self.each2(j, lambda copy: copy.wait_send())


def factor(nb, b, spread, all_ref, inverse_ref, u_ref, r_ref, l_ref, y_ref, z_ref, p_ref, d_ref):
    tiles = nb // 2
    sub = lax.broadcasted_iota(jnp.int32, (COARSE, W), 0)
    lane = lax.broadcasted_iota(jnp.int32, (COARSE, W), 1)
    groups = W // 8
    unroll = 2

    def tile(k):
        return pl.ds(pl.multiple_of(k * W, W), W)

    def step(k, depth, column):
        if column:
            j = k + 1
            spread.need(j)

            @pl.when(k + 5 < tiles)
            def _():
                spread.first(k + 5)

            @pl.when(k + 3 < tiles)
            def _():
                spread.second(k + 3)

        def run(it, v):
            if column:
                i = jnp.minimum(it, k)
                u = all_ref[j, tile(i), :] - dot(l_ref[i, :, :depth], u_ref[j, :depth, :])
                before = jnp.maximum(i - 1, 0)
                scaled = dot(p_ref[before], u_ref[j, tile(before), :])
                u_ref[j, tile(i), :] = u
                r_ref[j, tile(before), :] = scaled
                l_ref[j, :, tile(before)] = scaled.T
            return pivot_groups(unroll, v)

        block = tuple(d_ref[8 * i : 8 * i + 8, :] for i in range(groups))
        inverse = jnp.concatenate(lax.fori_loop(0, groups // unroll, run, block), axis=0)
        p_ref[k] = inverse
        if column:
            scaled = dot(inverse, u_ref[j, tile(k), :])
            r_ref[j, tile(k), :] = scaled
            l_ref[j, :, tile(k)] = scaled.T
            d_ref[...] = all_ref[j, tile(j), :] - dot(l_ref[j, :, :depth], u_ref[j, :depth, :])
        own = (lane + k * W == sub + b * COARSE).astype(F32)
        own = own - dot(y_ref[:, :depth], r_ref[k, :depth, :])
        y_ref[:, tile(k)] = own
        z_ref[k] = dot(own, inverse)

    def loop(start, stop):
        def run(k, carry):
            step(k, stop * W, True)
            return carry

        lax.fori_loop(start, stop, run, 0)

    spread.need(0)
    d_ref[...] = all_ref[0, :W, :]
    loop(0, tiles // 2)
    loop(tiles // 2, tiles - 1)
    step(tiles - 1, (tiles - 1) * W, False)
    solved = [None] * tiles
    low = lane < COARSE
    for k in reversed(range(tiles)):
        acc = z_ref[k]
        for j in range(k + 1, tiles):
            acc = acc - dot(solved[j], l_ref[j, :, k * W : k * W + W])
        solved[k] = acc
        inverse_ref[2 * k] = jnp.where(low, acc, 0.0)
        inverse_ref[2 * k + 1] = jnp.where(low, pltpu.roll(acc, COARSE, 1), 0.0)


def whole_kernel(
    nr, nb, pattern_in, matrix_in, load_in, stiffness_in, local_in, intact_in, lists_in, basis_in,
    out_ref, pattern_ref, matrix_ref, load_ref, stiffness_ref, local_ref, intact_ref, lists_ref, basis_ref, in_sem, all_ref, inverse_ref, u_ref, r_ref, l_ref, y_ref, zf_ref, p_ref, d_ref,
    k_ref, m_ref, c_ref, ct_ref, sel_ref, selt_ref, col_ref, z_ref, w_ref, acc_ref,
    msg_ref, gather_ref, tot_ref, total_ref, face_ref, near_ref, send1, recv1, send2, recv2,
    gather_send, gather_recv, total_send, total_recv, face_send, face_recv,
):
    r, b = lax.axis_index("rows"), lax.axis_index("bricks")
    tiles = nb // 2
    incoming = [
        pltpu.make_async_copy(src, dst, in_sem.at[i])
        for i, (src, dst) in enumerate(
            (
                (pattern_in, pattern_ref), (matrix_in, matrix_ref), (load_in, load_ref), (basis_in, basis_ref),
                (lists_in, lists_ref), (intact_in, intact_ref), (local_in, local_ref), (stiffness_in, stiffness_ref),
            )
        )
    ]
    for copy in incoming:
        copy.start()
    barrier = pltpu.get_barrier_semaphore()
    for t in range(1, nb):
        pl.semaphore_signal(
            barrier, inc=1, device_id=(r, lax.rem(b + t, nb)), device_id_type=MESH
        )
    for t in range(1, nr):
        pl.semaphore_signal(
            barrier, inc=1, device_id=(lax.rem(r + t, nr), b), device_id_type=MESH
        )
    mine = pl.ds(pl.multiple_of(b * COARSE, COARSE), COARSE)
    incoming[0].wait()
    incoming[1].wait()
    for j in range(tiles):
        left = matrix_ref[2 * j] * pattern_ref[0, 2 * j].astype(F32)
        right = matrix_ref[2 * j + 1] * pattern_ref[0, 2 * j + 1].astype(F32)
        all_ref[j, mine, :] = jnp.concatenate([left, right], axis=1)
    spread = Spread(nb, r, b, all_ref, (send1, recv1, send2, recv2))
    pl.semaphore_wait(barrier, nb + nr - 2)
    for j in range(min(3, tiles)):
        spread.first(j)
    for copy in incoming[2:]:
        copy.wait()
    lane8 = lax.broadcasted_iota(jnp.int32, (8, LANES), 1)
    lane1 = lax.broadcasted_iota(jnp.int32, (1, LANES), 1)
    gap = jnp.zeros((NDOF, LANES - NODES), F32)
    for e in range(6):
        span = slice(e * NODES, e * NODES + NODES)
        piece = jnp.concatenate([basis_ref[:, span], gap[:COARSE]], axis=1)
        c_ref[e] = piece
        turned = jnp.concatenate([piece, jnp.zeros((LANES - COARSE, LANES), F32)], axis=0).T
        ct_ref[span, :] = turned[:NODES]
    node_col = lax.broadcasted_iota(jnp.int32, (LANES, LANES), 0)
    node_row = lax.broadcasted_iota(jnp.int32, (LANES, LANES), 1)
    slots = jnp.full((1, LANES), -1, jnp.int32)
    swapped = slots
    for d in range(4):
        line = jnp.concatenate([lists_ref[d : d + 1, :], jnp.zeros((1, LANES - FACE), jnp.int32)], axis=1)
        for other in (False, True):
            at = 32 * (d ^ other)
            moved = pltpu.roll(line, at, 1) if at else line
            here = (lane1 >= at) & (lane1 < at + FACE)
            if other:
                swapped = jnp.where(here, moved, swapped)
            else:
                slots = jnp.where(here, moved, slots)
    sel_ref[:, :LANES] = (node_col == slots).astype(F32)
    sel_ref[:, LANES:] = (node_col == swapped).astype(F32)
    selt_ref[...] = sel_ref[:NODES, :LANES]
    eye = (node_col == node_row)[:NODES]

    def row_to_col(row, ref):
        for c in range(6):
            spread = jnp.where(eye, jnp.broadcast_to(row[c : c + 1, :], (NODES, LANES)), 0.0)
            ref[c * NODES : c * NODES + NODES, :] = jnp.broadcast_to(
                jnp.sum(spread, axis=1, keepdims=True), (NODES, LANES)
            )

    def stack(rows):
        return jnp.concatenate(rows + [jnp.zeros((8 - len(rows), LANES), F32)], axis=0)

    def col_to_row(ref):
        return stack(
            [
                jnp.sum(jnp.where(eye, ref[c * NODES : c * NODES + NODES, :], 0.0), axis=0, keepdims=True)
                for c in range(6)
            ]
        )

    def row_partners(t):
        return (r, lax.rem(b + t, nb))

    def col_partners(t):
        return (lax.rem(r + t, nr), b)

    def exchange(count, partners, msg, land, send_sem, recv_sem):
        for t in range(1, count):
            pltpu.make_async_remote_copy(
                src_ref=msg, dst_ref=land, send_sem=send_sem, recv_sem=recv_sem,
                device_id=partners(t), device_id_type=MESH,
            ).start()

    def wait_bytes(ref, sem):
        pltpu.make_async_copy(ref, ref, sem).wait()

    def gather_start(n, message):
        msg_ref[n] = message
        gather_ref[n, b] = message
        exchange(
            nb, row_partners, msg_ref.at[n], gather_ref.at[n, b], gather_send.at[n], gather_recv.at[n]
        )

    def gather_wait(n):
        wait_bytes(gather_ref.at[n, pl.ds(0, nb - 1)], gather_recv.at[n])

    def total_start(n):
        acc = gather_ref[n, 0]
        for j in range(1, nb):
            acc = acc + gather_ref[n, j]
        tot_ref[n] = acc
        total_ref[n, r] = acc
        exchange(
            nr, col_partners, tot_ref.at[n], total_ref.at[n, r], total_send.at[n], total_recv.at[n]
        )

    def total_wait(n):
        wait_bytes(total_ref.at[n, pl.ds(0, nr - 1)], total_recv.at[n])
        acc = total_ref[n, 0]
        for j in range(1, nr):
            acc = acc + total_ref[n, j]
        first = jnp.sum(jnp.where(lane1 == COARSE, acc, 0.0), axis=1, keepdims=True)
        second = jnp.sum(jnp.where(lane1 == COARSE + 1, acc, 0.0), axis=1, keepdims=True)
        return first, second

    def reduced(ref):
        return jnp.sum(ref[...] * ct_ref[...], axis=0, keepdims=True)

    def with_dots(message, first, second):
        one = jnp.sum(jnp.sum(first, axis=0, keepdims=True), axis=1, keepdims=True)
        two = jnp.sum(jnp.sum(second, axis=0, keepdims=True), axis=1, keepdims=True)
        message = jnp.where(lane1 == COARSE, one, message)
        return jnp.where(lane1 == COARSE + 1, two, message)

    def local_part(ref):
        return [jnp.sum(ref[...] * m_ref[e], axis=0, keepdims=True) for e in range(6)]

    def coarse_part(n):
        acc = inverse_ref[0] * gather_ref[n, 0]
        for j in range(1, nb):
            acc = acc + inverse_ref[j] * gather_ref[n, j]
        solved = jnp.sum(acc, axis=1, keepdims=True)
        return [jnp.sum(solved * c_ref[e], axis=0, keepdims=True) for e in range(6)]

    neighbours = [
        (lax.rem(r + nr - 1, nr), b, r > 0),
        (lax.rem(r + 1, nr), b, r < nr - 1),
        (r, lax.rem(b + nb - 1, nb), b > 0),
        (r, lax.rem(b + 1, nb), b < nb - 1),
    ]

    def face_start(n, row):
        both = dot(row, sel_ref[...])
        face_ref[n] = both[:, LANES:]
        for d in range(4):
            pltpu.make_async_remote_copy(
                src_ref=face_ref.at[n], dst_ref=near_ref.at[n, d ^ 1],
                send_sem=face_send.at[n, d], recv_sem=face_recv.at[n, d ^ 1],
                device_id=neighbours[d][:2], device_id_type=MESH,
            ).start()
        return both[:, :LANES]

    def operate(n, row, face, target):
        for c in range(6):
            rows = slice(c * NODES, c * NODES + NODES)
            acc = k_ref[0, rows, :] * row[0:1, :]
            for e in range(1, 6):
                acc = acc + k_ref[e, rows, :] * row[e : e + 1, :]
            acc_ref[rows, :] = acc
        stretch = face
        for d in range(4):
            wait_bytes(near_ref.at[n, d], face_recv.at[n, d])
            here = (lane8 >= 32 * d) & (lane8 < 32 * d + 32) & neighbours[d][2]
            stretch = stretch - jnp.where(here, near_ref[n, d], 0.0)
        for c in range(6):
            rows = slice(c * NODES, c * NODES + NODES)
            acc = acc_ref[rows, :] + selt_ref[...] * stretch[c : c + 1, :]
            target[rows, :] = jnp.broadcast_to(
                jnp.sum(acc, axis=1, keepdims=True), (NODES, LANES)
            )

    load = stack([jnp.concatenate([load_ref[:, c * NODES : c * NODES + NODES], gap[:1]], axis=1) for c in range(6)])
    row_to_col(load, col_ref)
    res = load
    gather_start(0, reduced(col_ref))
    for j in range(min(2, tiles)):
        spread.second(j)
    if tiles > 3:
        spread.first(3)
    for ref in (u_ref, r_ref, l_ref, p_ref):
        for j in range(tiles):
            ref[j] = jnp.zeros(ref.shape[1:], F32)
    y_ref[...] = jnp.zeros(y_ref.shape, F32)
    if tiles > 2:
        spread.second(2)
    if tiles > 4:
        spread.first(4)
    intact = intact_ref[...].astype(F32)
    for e in range(6):
        span = slice(e * NODES, e * NODES + NODES)
        part = jnp.concatenate([stiffness_ref[:, span], gap], axis=1)
        mask = jnp.concatenate([intact, gap[:NODES]], axis=1)
        for c in range(6):
            rows = slice(c * NODES, c * NODES + NODES)
            k_ref[e, rows, :] = part[rows] * mask
        m_ref[e] = jnp.concatenate([local_ref[:, span], gap], axis=1)
    part = stack(local_part(col_ref))
    gather_wait(0)

    factor(nb, b, spread, all_ref, inverse_ref, u_ref, r_ref, l_ref, y_ref, zf_ref, p_ref, d_ref)

    u = part + stack(coarse_part(0))
    face = face_start(0, u)
    operate(0, u, face, w_ref)
    w = col_to_row(w_ref)
    p = s = q = sol = None
    dot_old = step_old = None
    for i in range(2):
        gather_start(i + 1, with_dots(reduced(w_ref), res * u, w * u))
        part = local_part(w_ref)
        gather_wait(i + 1)
        total_start(i + 1)
        m = stack([x + y for x, y in zip(part, coarse_part(i + 1))])
        face = face_start(i + 1, m)
        operate(i + 1, m, face, col_ref)
        v = col_to_row(col_ref)
        gamma, delta = total_wait(i + 1)
        if i == 0:
            step_size = gamma / delta
            p, s, q, zr = u, w, m, v
            z_ref[...] = col_ref[...]
            sol = step_size * p
        else:
            ratio = gamma / dot_old
            step_size = gamma / (delta - ratio * gamma / step_old)
            p, s, q, zr = u + ratio * p, w + ratio * s, m + ratio * q, v + ratio * zr
            sol = sol + step_size * p
        res = res - step_size * s
        u = u - step_size * q
        w = w - step_size * zr
        if i == 0:
            w_ref[...] = w_ref[...] - step_size * z_ref[...]
        dot_old, step_old = gamma, step_size
    gather_start(3, with_dots(jnp.zeros((1, LANES), F32), res * u, w * u))
    gather_wait(3)
    total_start(3)
    gamma, delta = total_wait(3)
    ratio = gamma / dot_old
    step_size = gamma / (delta - ratio * gamma / step_old)
    out_ref[0] = sol + step_size * (u + ratio * p)
    out_ref[1] = res - step_size * (w + ratio * s)

    spread.finish()
    for n in range(4):
        wait_bytes(gather_ref.at[n, pl.ds(0, nb - 1)], gather_send.at[n])
    for n in range(1, 4):
        wait_bytes(total_ref.at[n, pl.ds(0, nr - 1)], total_send.at[n])
    for n in range(3):
        for d in range(4):
            wait_bytes(face_ref.at[n], face_send.at[n, d])


VMEM = pl.BlockSpec(memory_space=pltpu.VMEM)
ANY = pl.BlockSpec(memory_space=pltpu.HBM)


def body(nr, nb, load, stiffness, local_inverse, intact, face_lists, coarse_basis, matrix, pattern):
    tiles = nb // 2
    order = nb * COARSE
    limit = 62 * 1024 * 1024
    out = pl.pallas_call(
        functools.partial(whole_kernel, nr, nb),
        out_shape=jax.ShapeDtypeStruct((2, 8, LANES), F32),
        in_specs=[ANY] * 8,
        out_specs=VMEM,
        scratch_shapes=[
            pltpu.SMEM((1, nb), jnp.int32),
            pltpu.VMEM((nb, COARSE, COARSE), F32),
            pltpu.VMEM((1, NDOF), F32),
            pltpu.VMEM((NDOF, NDOF), F32),
            pltpu.VMEM((NDOF, NDOF), F32),
            pltpu.VMEM((NODES, NODES), jnp.int32),
            pltpu.VMEM((4, FACE), jnp.int32),
            pltpu.VMEM((COARSE, NDOF), F32),
            pltpu.SemaphoreType.DMA((8,)),
            pltpu.VMEM((tiles, order, LANES), F32),
            pltpu.VMEM((nb, COARSE, LANES), F32),
            pltpu.VMEM((tiles, order, LANES), F32),
            pltpu.VMEM((tiles, order, LANES), F32),
            pltpu.VMEM((tiles, W, order), F32),
            pltpu.VMEM((COARSE, order), F32),
            pltpu.VMEM((tiles, COARSE, W), F32),
            pltpu.VMEM((tiles, W, W), F32),
            pltpu.VMEM((W, W), F32),
            pltpu.VMEM((6, NDOF, LANES), F32),
            pltpu.VMEM((6, NDOF, LANES), F32),
            pltpu.VMEM((6, COARSE, LANES), F32),
            pltpu.VMEM((NDOF, LANES), F32),
            pltpu.VMEM((LANES, 2 * LANES), F32),
            pltpu.VMEM((NODES, LANES), F32),
            pltpu.VMEM((NDOF, LANES), F32),
            pltpu.VMEM((NDOF, LANES), F32),
            pltpu.VMEM((NDOF, LANES), F32),
            pltpu.VMEM((NDOF, LANES), F32),
            pltpu.VMEM((4, 1, LANES), F32),
            pltpu.VMEM((4, nb, 1, LANES), F32),
            pltpu.VMEM((4, 1, LANES), F32),
            pltpu.VMEM((4, nr, 1, LANES), F32),
            pltpu.VMEM((3, 8, LANES), F32),
            pltpu.VMEM((3, 4, 8, LANES), F32),
            pltpu.SemaphoreType.DMA((tiles, RUN)),
            pltpu.SemaphoreType.DMA((tiles, RUN)),
            pltpu.SemaphoreType.DMA((tiles, nb // RUN)),
            pltpu.SemaphoreType.DMA((tiles, nb // RUN)),
            pltpu.SemaphoreType.DMA((4,)),
            pltpu.SemaphoreType.DMA((4,)),
            pltpu.SemaphoreType.DMA((4,)),
            pltpu.SemaphoreType.DMA((4,)),
            pltpu.SemaphoreType.DMA((3, 4)),
            pltpu.SemaphoreType.DMA((3, 4)),
        ],
        compiler_params=pltpu.CompilerParams(
            collective_id=0, has_side_effects=True, vmem_limit_bytes=limit
        ),
        name="whole",
    )(
        pattern.reshape(1, nb),
        matrix.reshape(nb, COARSE, COARSE),
        load.reshape(1, NDOF),
        stiffness.reshape(NDOF, NDOF),
        local_inverse.reshape(NDOF, NDOF),
        intact.reshape(NODES, NODES),
        face_lists.reshape(4, FACE),
        coarse_basis.reshape(COARSE, NDOF),
    )
    flat = out[:, :6, :NODES].reshape(2, 1, 1, NDOF)
    return flat[0], flat[1]


def solution(mesh):
    in_specs = (
        P("rows", "bricks", None),
        P("rows", "bricks", None, None),
        P("rows", "bricks", None, None),
        P("rows", "bricks", None, None),
        P("rows", "bricks", None, None),
        P("rows", "bricks", None, None),
        P("rows", "bricks", None, None, None),
        P("rows", "bricks", None),
    )
    out_specs = (P("rows", "bricks", None), P("rows", "bricks", None))
    run = functools.partial(body, mesh.shape["rows"], mesh.shape["bricks"])
    return jax.shard_map(run, mesh=mesh, in_specs=in_specs, out_specs=out_specs, check_vma=False)
```

```python
import functools

import jax
import jax.numpy as jnp
from jax import lax
from jax.experimental import pallas as pl
from jax.experimental.pallas import tpu as pltpu
from jax.sharding import PartitionSpec as P

MESH = pl.DeviceIdType.MESH
HI = lax.Precision.HIGHEST
F32 = jnp.float32
NODES, NDOF, COARSE, FACE, W = 96, 576, 64, 24, 128
LANES = 128


def dot(a, b, dims=((1,), (0,))):
    return lax.dot_general(a, b, (dims, ((), ())), precision=HI, preferred_element_type=F32)


def small_product(a, b):
    out = []
    for row in a:
        line = []
        for j in range(len(b[0])):
            acc = row[0] * b[0][j]
            for k in range(1, len(b)):
                acc = acc + row[k] * b[k][j]
            line.append(acc)
        out.append(line)
    return out


def small_inverse(m):
    n = len(m)
    if n == 2:
        a, b, d = m[0][0], m[0][1], m[1][1]
        r = 1.0 / (a * d - b * b)
        off = -(b * r)
        return [[d * r, off], [off, a * r]]
    h = n // 2
    b = [row[h:] for row in m[:h]]
    e = small_inverse([row[:h] for row in m[:h]])
    w = small_product(e, b)
    s = [[None] * h for _ in range(h)]
    for i in range(h):
        for j in range(i, h):
            acc = b[0][i] * w[0][j]
            for k in range(1, h):
                acc = acc + b[k][i] * w[k][j]
            s[i][j] = s[j][i] = m[h + i][h + j] - acc
    t = small_inverse(s)
    x = small_product(w, t)
    top = [[None] * h for _ in range(h)]
    for i in range(h):
        for j in range(i, h):
            acc = x[i][0] * w[j][0]
            for k in range(1, h):
                acc = acc + x[i][k] * w[j][k]
            top[i][j] = top[j][i] = e[i][j] + acc
    neg = [[-v for v in row] for row in x]
    out = [top[i] + neg[i] for i in range(h)]
    out += [[neg[k][i] for k in range(h)] + t[i] for i in range(h)]
    return out


def pivot_groups(count, v):
    shape = (8, LANES)
    sub = lax.broadcasted_iota(jnp.int32, shape, 0)
    lane = lax.broadcasted_iota(jnp.int32, shape, 1)
    v = list(v)
    for g in range(count):
        p = 8 * g
        x = v[g]
        turn = LANES - 8 * count if g == count - 1 else 0
        rows = [jnp.broadcast_to(x[i : i + 1, :], shape) for i in range(8)]
        cols = [jnp.broadcast_to(x[:, p + t : p + t + 1], shape) for t in range(8)]
        m = [[None] * 8 for _ in range(8)]
        for i in range(8):
            for j in range(i, 8):
                m[i][j] = m[j][i] = jnp.broadcast_to(cols[j][i : i + 1, :], shape)
        e = small_inverse(m)
        pivots = (lane >= p) & (lane < p + 8)
        r = [jnp.where(pivots, (lane == p + i).astype(F32), rows[i]) for i in range(8)]
        q = []
        for i in range(8):
            acc = e[i][0] * r[0]
            for j in range(1, 8):
                acc = acc + e[i][j] * r[j]
            q.append(acc)
        new = []
        for k in range(len(v)):
            y = v[k]
            if k == g:
                y = q[0]
                for t in range(1, 8):
                    y = jnp.where(sub == t, q[t], y)
            else:
                acc = jnp.broadcast_to(y[:, p : p + 1], shape) * q[0]
                for t in range(1, 8):
                    acc = acc + jnp.broadcast_to(y[:, p + t : p + t + 1], shape) * q[t]
                y = jnp.where(pivots, 0.0, y) - acc
            new.append(pltpu.roll(y, turn, 1) if turn else y)
        v = new
    return tuple(v[count:] + v[:count])


RUN = 4


class Spread:
    def __init__(self, nb, r, b, all_ref, sems):
        self.nb, self.tiles, self.nx = nb, nb // 2, nb // RUN
        self.r, self.b, self.x, self.z = r, b, lax.div(b, RUN), lax.rem(b, RUN)
        self.all_ref = all_ref
        self.send1, self.recv1, self.send2, self.recv2, self.send0, self.recv0 = sems

    def slot(self, j, brick, count):
        start = pl.multiple_of(brick * COARSE, COARSE)
        return self.all_ref.at[j, pl.ds(start, count * COARSE), :]

    def copy0(self, j, t):
        part = self.slot(j, self.b, 1)
        return pltpu.make_async_remote_copy(
            src_ref=part, dst_ref=part, send_sem=self.send0.at[j, t], recv_sem=self.recv0.at[j, self.b],
            device_id=(self.r, lax.rem(self.b + t, self.nb)), device_id_type=MESH,
        )

    def each0(self, j, act):
        @pl.when(lax.div(self.b, 2) <= j)
        def _():
            for t in range(1, self.nb):
                act(self.copy0(j, t))

    def direct(self, j):
        self.each0(j, lambda copy: copy.start())

    def need_direct(self, j):
        for s in range(2 * j + 2):

            @pl.when(self.b != s)
            def _():
                part = self.slot(j, s, 1)
                pltpu.make_async_copy(part, part, self.recv0.at[j, s]).wait()

    def copy1(self, j, t):
        part = self.slot(j, self.b, 1)
        z = lax.rem(self.z + t, RUN)
        return pltpu.make_async_remote_copy(
            src_ref=part, dst_ref=part, send_sem=self.send1.at[j, t], recv_sem=self.recv1.at[j, self.z],
            device_id=(self.r, self.x * RUN + z), device_id_type=MESH,
        )

    def copy2(self, j, t, count):
        part = self.slot(j, self.x * RUN, count)
        x = lax.rem(self.x + t, self.nx)
        return pltpu.make_async_remote_copy(
            src_ref=part, dst_ref=part, send_sem=self.send2.at[j, t], recv_sem=self.recv2.at[j, self.x],
            device_id=(self.r, x * RUN + self.z), device_id_type=MESH,
        )

    def each1(self, j, act):
        @pl.when(lax.div(self.b, 2) <= j)
        def _():
            for t in range(1, RUN):
                act(self.copy1(j, t))

    def each2(self, j, act):
        for count, when in ((RUN, 2 * self.x + 1 <= j), (2, 2 * self.x == j)):

            @pl.when(when)
            def _():
                for t in range(1, self.nx):
                    act(self.copy2(j, t, count))

    def first(self, j):
        self.each1(j, lambda copy: copy.start())

    def second(self, j):
        for z in range(RUN):

            @pl.when((self.z != z) & (2 * self.x + z // 2 <= j))
            def _():
                part = self.slot(j, self.x * RUN + z, 1)
                pltpu.make_async_copy(part, part, self.recv1.at[j, z]).wait()

        self.each2(j, lambda copy: copy.start())

    def need(self, j):
        for x in range(self.nx):
            for count, when in ((RUN, 2 * x + 1 <= j), (2, 2 * x == j)):

                @pl.when((self.x != x) & when)
                def _():
                    part = self.slot(j, x * RUN, count)
                    pltpu.make_async_copy(part, part, self.recv2.at[j, x]).wait()

    def finish(self):
        for j in range(2):
            self.each0(j, lambda copy: copy.wait_send())
        for j in range(2, self.tiles):
            self.each1(j, lambda copy: copy.wait_send())
            self.each2(j, lambda copy: copy.wait_send())


def factor(nb, b, spread, all_ref, inverse_ref, u_ref, r_ref, l_ref, y_ref, z_ref, p_ref, d_ref):
    tiles = nb // 2
    sub = lax.broadcasted_iota(jnp.int32, (COARSE, W), 0)
    lane = lax.broadcasted_iota(jnp.int32, (COARSE, W), 1)
    half = tiles // 2
    unroll = 2
    turns = W // 8 // unroll

    def tile(k):
        return pl.ds(pl.multiple_of(k * W, W), W)

    def plain(it, v):
        return pivot_groups(unroll, v)

    def with_product(j, depth):
        def run(i, v):
            u = all_ref[j, tile(i), :] - dot(l_ref[i, :, :depth], u_ref[j, :depth, :])
            before = jnp.maximum(i - 1, 0)
            scaled = dot(p_ref[before], u_ref[j, tile(before), :])
            u_ref[j, tile(i), :] = u
            r_ref[j, tile(before), :] = scaled
            l_ref[j, :, tile(before)] = scaled.T
            return pivot_groups(unroll, v)

        return run

    def step(k, far, column):
        depth = (tiles - 1 if far else half) * W
        v = tuple(d_ref[8 * i : 8 * i + 8, :] for i in range(W // 8))
        if column:
            j = k + 1

            @pl.when(k + 5 < tiles)
            def _():
                spread.first(k + 5)

            @pl.when(k + 3 < tiles)
            def _():
                spread.second(k + 3)

            v = lax.fori_loop(0, turns - j, plain, v)
            if far:
                spread.need(j)
            else:

                @pl.when(k == 0)
                def _():
                    spread.need_direct(1)

                @pl.when(k > 0)
                def _():
                    spread.need(j)

            v = lax.fori_loop(0, half if far else j, with_product(j, (half - 1) * W), v)
            if far:
                v = lax.fori_loop(half, j, with_product(j, (tiles - 2) * W), v)
        else:
            v = lax.fori_loop(0, turns, plain, v)
        inverse = jnp.concatenate(v, axis=0)
        p_ref[k] = inverse
        if column:
            scaled = dot(inverse, u_ref[j, tile(k), :])
            r_ref[j, tile(k), :] = scaled
            l_ref[j, :, tile(k)] = scaled.T
            d_ref[...] = all_ref[j, tile(j), :] - dot(l_ref[j, :, :depth], u_ref[j, :depth, :])
        own = (lane + k * W == sub + b * COARSE).astype(F32)
        own = own - dot(y_ref[:, :depth], r_ref[k, :depth, :])
        y_ref[:, tile(k)] = own
        z_ref[k] = dot(own, inverse)

    def near_step(k, carry):
        step(k, False, True)
        return carry

    def far_step(k, carry):
        step(k, True, True)
        return carry

    spread.need_direct(0)
    d_ref[...] = all_ref[0, :W, :]
    lax.fori_loop(0, half, near_step, 0)
    lax.fori_loop(half, tiles - 1, far_step, 0)
    step(tiles - 1, True, False)
    solved = [None] * tiles
    low = lane < COARSE
    for k in reversed(range(tiles)):
        acc = z_ref[k]
        for j in range(k + 1, tiles):
            acc = acc - dot(solved[j], l_ref[j, :, k * W : k * W + W])
        solved[k] = acc
        inverse_ref[2 * k] = jnp.where(low, acc, 0.0)
        inverse_ref[2 * k + 1] = jnp.where(low, pltpu.roll(acc, COARSE, 1), 0.0)


def whole_kernel(
    nr, nb, pattern_in, matrix_in, load_in, stiffness_in, local_in, intact_in, lists_in, basis_in,
    out_ref, pattern_ref, matrix_ref, load_ref, stiffness_ref, local_ref, intact_ref, lists_ref, basis_ref, in_sem, all_ref, inverse_ref, u_ref, r_ref, l_ref, y_ref, zf_ref, p_ref, d_ref,
    k_ref, m_ref, c_ref, ct_ref, sel_ref, selt_ref, col_ref, z_ref, w_ref, acc_ref,
    msg_ref, gather_ref, tot_ref, total_ref, face_ref, near_ref, send1, recv1, send2, recv2, send0, recv0,
    gather_send, gather_recv, total_send, total_recv, face_send, face_recv,
):
    r, b = lax.axis_index("rows"), lax.axis_index("bricks")
    tiles = nb // 2
    incoming = [
        pltpu.make_async_copy(src, dst, in_sem.at[i])
        for i, (src, dst) in enumerate(
            (
                (pattern_in, pattern_ref), (matrix_in, matrix_ref), (load_in, load_ref), (basis_in, basis_ref),
                (lists_in, lists_ref), (intact_in, intact_ref), (local_in, local_ref), (stiffness_in, stiffness_ref),
            )
        )
    ]
    for copy in incoming:
        copy.start()
    barrier = pltpu.get_barrier_semaphore()
    for t in range(1, nb):
        pl.semaphore_signal(
            barrier, inc=1, device_id=(r, lax.rem(b + t, nb)), device_id_type=MESH
        )
    for t in range(1, nr):
        pl.semaphore_signal(
            barrier, inc=1, device_id=(lax.rem(r + t, nr), b), device_id_type=MESH
        )
    mine = pl.ds(pl.multiple_of(b * COARSE, COARSE), COARSE)
    incoming[0].wait()
    incoming[1].wait()
    for j in range(tiles):
        left = matrix_ref[2 * j] * pattern_ref[0, 2 * j].astype(F32)
        right = matrix_ref[2 * j + 1] * pattern_ref[0, 2 * j + 1].astype(F32)
        all_ref[j, mine, :] = jnp.concatenate([left, right], axis=1)
    spread = Spread(nb, r, b, all_ref, (send1, recv1, send2, recv2, send0, recv0))
    pl.semaphore_wait(barrier, nb + nr - 2)
    spread.direct(0)
    spread.first(2)
    spread.direct(1)
    spread.first(3)
    for copy in incoming[2:]:
        copy.wait()
    lane8 = lax.broadcasted_iota(jnp.int32, (8, LANES), 1)
    lane1 = lax.broadcasted_iota(jnp.int32, (1, LANES), 1)
    gap = jnp.zeros((NDOF, LANES - NODES), F32)
    for e in range(6):
        span = slice(e * NODES, e * NODES + NODES)
        piece = jnp.concatenate([basis_ref[:, span], gap[:COARSE]], axis=1)
        c_ref[e] = piece
        turned = jnp.concatenate([piece, jnp.zeros((LANES - COARSE, LANES), F32)], axis=0).T
        ct_ref[span, :] = turned[:NODES]
    node_col = lax.broadcasted_iota(jnp.int32, (LANES, LANES), 0)
    node_row = lax.broadcasted_iota(jnp.int32, (LANES, LANES), 1)
    slots = jnp.full((1, LANES), -1, jnp.int32)
    swapped = slots
    for d in range(4):
        line = jnp.concatenate([lists_ref[d : d + 1, :], jnp.zeros((1, LANES - FACE), jnp.int32)], axis=1)
        for other in (False, True):
            at = 32 * (d ^ other)
            moved = pltpu.roll(line, at, 1) if at else line
            here = (lane1 >= at) & (lane1 < at + FACE)
            if other:
                swapped = jnp.where(here, moved, swapped)
            else:
                slots = jnp.where(here, moved, slots)
    sel_ref[:, :LANES] = (node_col == slots).astype(F32)
    sel_ref[:, LANES:] = (node_col == swapped).astype(F32)
    selt_ref[...] = sel_ref[:NODES, :LANES]
    eye = (node_col == node_row)[:NODES]

    def row_to_col(row, ref):
        for c in range(6):
            spread = jnp.where(eye, jnp.broadcast_to(row[c : c + 1, :], (NODES, LANES)), 0.0)
            ref[c * NODES : c * NODES + NODES, :] = jnp.broadcast_to(
                jnp.sum(spread, axis=1, keepdims=True), (NODES, LANES)
            )

    def stack(rows):
        return jnp.concatenate(rows + [jnp.zeros((8 - len(rows), LANES), F32)], axis=0)

    def col_to_row(ref):
        return stack(
            [
                jnp.sum(jnp.where(eye, ref[c * NODES : c * NODES + NODES, :], 0.0), axis=0, keepdims=True)
                for c in range(6)
            ]
        )

    def row_partners(t):
        return (r, lax.rem(b + t, nb))

    def col_partners(t):
        return (lax.rem(r + t, nr), b)

    def exchange(count, partners, msg, land, send_sem, recv_sem):
        for t in range(1, count):
            pltpu.make_async_remote_copy(
                src_ref=msg, dst_ref=land, send_sem=send_sem, recv_sem=recv_sem,
                device_id=partners(t), device_id_type=MESH,
            ).start()

    def wait_bytes(ref, sem):
        pltpu.make_async_copy(ref, ref, sem).wait()

    def gather_start(n, message):
        msg_ref[n] = message
        gather_ref[n, b] = message
        exchange(
            nb, row_partners, msg_ref.at[n], gather_ref.at[n, b], gather_send.at[n], gather_recv.at[n]
        )

    def gather_wait(n):
        wait_bytes(gather_ref.at[n, pl.ds(0, nb - 1)], gather_recv.at[n])

    def total_start(n):
        acc = gather_ref[n, 0]
        for j in range(1, nb):
            acc = acc + gather_ref[n, j]
        tot_ref[n] = acc
        total_ref[n, r] = acc
        exchange(
            nr, col_partners, tot_ref.at[n], total_ref.at[n, r], total_send.at[n], total_recv.at[n]
        )

    def total_wait(n):
        wait_bytes(total_ref.at[n, pl.ds(0, nr - 1)], total_recv.at[n])
        acc = total_ref[n, 0]
        for j in range(1, nr):
            acc = acc + total_ref[n, j]
        first = jnp.sum(jnp.where(lane1 == COARSE, acc, 0.0), axis=1, keepdims=True)
        second = jnp.sum(jnp.where(lane1 == COARSE + 1, acc, 0.0), axis=1, keepdims=True)
        return first, second

    def reduced(ref):
        return jnp.sum(ref[...] * ct_ref[...], axis=0, keepdims=True)

    def with_dots(message, first, second):
        one = jnp.sum(jnp.sum(first, axis=0, keepdims=True), axis=1, keepdims=True)
        two = jnp.sum(jnp.sum(second, axis=0, keepdims=True), axis=1, keepdims=True)
        message = jnp.where(lane1 == COARSE, one, message)
        return jnp.where(lane1 == COARSE + 1, two, message)

    def local_part(ref):
        return [jnp.sum(ref[...] * m_ref[e], axis=0, keepdims=True) for e in range(6)]

    def coarse_part(n):
        acc = inverse_ref[0] * gather_ref[n, 0]
        for j in range(1, nb):
            acc = acc + inverse_ref[j] * gather_ref[n, j]
        solved = jnp.sum(acc, axis=1, keepdims=True)
        return [jnp.sum(solved * c_ref[e], axis=0, keepdims=True) for e in range(6)]

    neighbours = [
        (lax.rem(r + nr - 1, nr), b, r > 0),
        (lax.rem(r + 1, nr), b, r < nr - 1),
        (r, lax.rem(b + nb - 1, nb), b > 0),
        (r, lax.rem(b + 1, nb), b < nb - 1),
    ]

    def face_start(n, row):
        both = dot(row, sel_ref[...])
        face_ref[n] = both[:, LANES:]
        for d in range(4):
            pltpu.make_async_remote_copy(
                src_ref=face_ref.at[n], dst_ref=near_ref.at[n, d ^ 1],
                send_sem=face_send.at[n, d], recv_sem=face_recv.at[n, d ^ 1],
                device_id=neighbours[d][:2], device_id_type=MESH,
            ).start()
        return both[:, :LANES]

    def operate(n, row, face, target):
        for c in range(6):
            rows = slice(c * NODES, c * NODES + NODES)
            acc = k_ref[0, rows, :] * row[0:1, :]
            for e in range(1, 6):
                acc = acc + k_ref[e, rows, :] * row[e : e + 1, :]
            acc_ref[rows, :] = acc
        stretch = face
        for d in range(4):
            wait_bytes(near_ref.at[n, d], face_recv.at[n, d])
            here = (lane8 >= 32 * d) & (lane8 < 32 * d + 32) & neighbours[d][2]
            stretch = stretch - jnp.where(here, near_ref[n, d], 0.0)
        for c in range(6):
            rows = slice(c * NODES, c * NODES + NODES)
            acc = acc_ref[rows, :] + selt_ref[...] * stretch[c : c + 1, :]
            target[rows, :] = jnp.broadcast_to(
                jnp.sum(acc, axis=1, keepdims=True), (NODES, LANES)
            )

    load = stack([jnp.concatenate([load_ref[:, c * NODES : c * NODES + NODES], gap[:1]], axis=1) for c in range(6)])
    row_to_col(load, col_ref)
    res = load
    gather_start(0, reduced(col_ref))
    for ref in (u_ref, r_ref, l_ref, p_ref):
        for j in range(tiles):
            ref[j] = jnp.zeros(ref.shape[1:], F32)
    y_ref[...] = jnp.zeros(y_ref.shape, F32)
    spread.second(2)
    if tiles > 4:
        spread.first(4)
    intact = intact_ref[...].astype(F32)
    for e in range(6):
        span = slice(e * NODES, e * NODES + NODES)
        part = jnp.concatenate([stiffness_ref[:, span], gap], axis=1)
        mask = jnp.concatenate([intact, gap[:NODES]], axis=1)
        for c in range(6):
            rows = slice(c * NODES, c * NODES + NODES)
            k_ref[e, rows, :] = part[rows] * mask
        m_ref[e] = jnp.concatenate([local_ref[:, span], gap], axis=1)
    part = stack(local_part(col_ref))
    gather_wait(0)

    factor(nb, b, spread, all_ref, inverse_ref, u_ref, r_ref, l_ref, y_ref, zf_ref, p_ref, d_ref)

    u = part + stack(coarse_part(0))
    face = face_start(0, u)
    operate(0, u, face, w_ref)
    w = col_to_row(w_ref)
    p = s = q = sol = None
    dot_old = step_old = None
    for i in range(2):
        gather_start(i + 1, with_dots(reduced(w_ref), res * u, w * u))
        part = local_part(w_ref)
        gather_wait(i + 1)
        total_start(i + 1)
        m = stack([x + y for x, y in zip(part, coarse_part(i + 1))])
        face = face_start(i + 1, m)
        operate(i + 1, m, face, col_ref)
        v = col_to_row(col_ref)
        gamma, delta = total_wait(i + 1)
        if i == 0:
            step_size = gamma / delta
            p, s, q, zr = u, w, m, v
            z_ref[...] = col_ref[...]
            sol = step_size * p
        else:
            ratio = gamma / dot_old
            step_size = gamma / (delta - ratio * gamma / step_old)
            p, s, q, zr = u + ratio * p, w + ratio * s, m + ratio * q, v + ratio * zr
            sol = sol + step_size * p
        res = res - step_size * s
        u = u - step_size * q
        w = w - step_size * zr
        if i == 0:
            w_ref[...] = w_ref[...] - step_size * z_ref[...]
        dot_old, step_old = gamma, step_size
    gather_start(3, with_dots(jnp.zeros((1, LANES), F32), res * u, w * u))
    gather_wait(3)
    total_start(3)
    gamma, delta = total_wait(3)
    ratio = gamma / dot_old
    step_size = gamma / (delta - ratio * gamma / step_old)
    out_ref[0] = sol + step_size * (u + ratio * p)
    out_ref[1] = res - step_size * (w + ratio * s)

    spread.finish()
    for n in range(4):
        wait_bytes(gather_ref.at[n, pl.ds(0, nb - 1)], gather_send.at[n])
    for n in range(1, 4):
        wait_bytes(total_ref.at[n, pl.ds(0, nr - 1)], total_send.at[n])
    for n in range(3):
        for d in range(4):
            wait_bytes(face_ref.at[n], face_send.at[n, d])


VMEM = pl.BlockSpec(memory_space=pltpu.VMEM)
ANY = pl.BlockSpec(memory_space=pltpu.HBM)


def body(nr, nb, load, stiffness, local_inverse, intact, face_lists, coarse_basis, matrix, pattern):
    tiles = nb // 2
    order = nb * COARSE
    limit = 62 * 1024 * 1024
    out = pl.pallas_call(
        functools.partial(whole_kernel, nr, nb),
        out_shape=jax.ShapeDtypeStruct((2, 8, LANES), F32),
        in_specs=[ANY] * 8,
        out_specs=VMEM,
        scratch_shapes=[
            pltpu.SMEM((1, nb), jnp.int32),
            pltpu.VMEM((nb, COARSE, COARSE), F32),
            pltpu.VMEM((1, NDOF), F32),
            pltpu.VMEM((NDOF, NDOF), F32),
            pltpu.VMEM((NDOF, NDOF), F32),
            pltpu.VMEM((NODES, NODES), jnp.int32),
            pltpu.VMEM((4, FACE), jnp.int32),
            pltpu.VMEM((COARSE, NDOF), F32),
            pltpu.SemaphoreType.DMA((8,)),
            pltpu.VMEM((tiles, order, LANES), F32),
            pltpu.VMEM((nb, COARSE, LANES), F32),
            pltpu.VMEM((tiles, order, LANES), F32),
            pltpu.VMEM((tiles, order, LANES), F32),
            pltpu.VMEM((tiles, W, order), F32),
            pltpu.VMEM((COARSE, order), F32),
            pltpu.VMEM((tiles, COARSE, W), F32),
            pltpu.VMEM((tiles, W, W), F32),
            pltpu.VMEM((W, W), F32),
            pltpu.VMEM((6, NDOF, LANES), F32),
            pltpu.VMEM((6, NDOF, LANES), F32),
            pltpu.VMEM((6, COARSE, LANES), F32),
            pltpu.VMEM((NDOF, LANES), F32),
            pltpu.VMEM((LANES, 2 * LANES), F32),
            pltpu.VMEM((NODES, LANES), F32),
            pltpu.VMEM((NDOF, LANES), F32),
            pltpu.VMEM((NDOF, LANES), F32),
            pltpu.VMEM((NDOF, LANES), F32),
            pltpu.VMEM((NDOF, LANES), F32),
            pltpu.VMEM((4, 1, LANES), F32),
            pltpu.VMEM((4, nb, 1, LANES), F32),
            pltpu.VMEM((4, 1, LANES), F32),
            pltpu.VMEM((4, nr, 1, LANES), F32),
            pltpu.VMEM((3, 8, LANES), F32),
            pltpu.VMEM((3, 4, 8, LANES), F32),
            pltpu.SemaphoreType.DMA((tiles, RUN)),
            pltpu.SemaphoreType.DMA((tiles, RUN)),
            pltpu.SemaphoreType.DMA((tiles, nb // RUN)),
            pltpu.SemaphoreType.DMA((tiles, nb // RUN)),
            pltpu.SemaphoreType.DMA((2, nb)),
            pltpu.SemaphoreType.DMA((2, 4)),
            pltpu.SemaphoreType.DMA((4,)),
            pltpu.SemaphoreType.DMA((4,)),
            pltpu.SemaphoreType.DMA((4,)),
            pltpu.SemaphoreType.DMA((4,)),
            pltpu.SemaphoreType.DMA((3, 4)),
            pltpu.SemaphoreType.DMA((3, 4)),
        ],
        compiler_params=pltpu.CompilerParams(
            collective_id=0, has_side_effects=True, vmem_limit_bytes=limit
        ),
        name="whole",
    )(
        pattern.reshape(1, nb),
        matrix.reshape(nb, COARSE, COARSE),
        load.reshape(1, NDOF),
        stiffness.reshape(NDOF, NDOF),
        local_inverse.reshape(NDOF, NDOF),
        intact.reshape(NODES, NODES),
        face_lists.reshape(4, FACE),
        coarse_basis.reshape(COARSE, NDOF),
    )
    flat = out[:, :6, :NODES].reshape(2, 1, 1, NDOF)
    return flat[0], flat[1]


def solution(mesh):
    in_specs = (
        P("rows", "bricks", None),
        P("rows", "bricks", None, None),
        P("rows", "bricks", None, None),
        P("rows", "bricks", None, None),
        P("rows", "bricks", None, None),
        P("rows", "bricks", None, None),
        P("rows", "bricks", None, None, None),
        P("rows", "bricks", None),
    )
    out_specs = (P("rows", "bricks", None), P("rows", "bricks", None))
    run = functools.partial(body, mesh.shape["rows"], mesh.shape["bricks"])
    return jax.shard_map(run, mesh=mesh, in_specs=in_specs, out_specs=out_specs, check_vma=False)
```

```python
import functools

import jax
import jax.numpy as jnp
from jax import lax
from jax.experimental import pallas as pl
from jax.experimental.pallas import tpu as pltpu
from jax.sharding import PartitionSpec as P

MESH = pl.DeviceIdType.MESH
HI = lax.Precision.HIGHEST
F32 = jnp.float32
NODES, NDOF, COARSE, FACE, W = 96, 576, 64, 24, 128
LANES = 128


def dot(a, b, dims=((1,), (0,))):
    return lax.dot_general(a, b, (dims, ((), ())), precision=HI, preferred_element_type=F32)


def small_product(a, b):
    out = []
    for row in a:
        line = []
        for j in range(len(b[0])):
            acc = row[0] * b[0][j]
            for k in range(1, len(b)):
                acc = acc + row[k] * b[k][j]
            line.append(acc)
        out.append(line)
    return out


def small_inverse(m):
    n = len(m)
    if n == 2:
        a, b, d = m[0][0], m[0][1], m[1][1]
        r = 1.0 / (a * d - b * b)
        off = -(b * r)
        return [[d * r, off], [off, a * r]]
    h = n // 2
    b = [row[h:] for row in m[:h]]
    e = small_inverse([row[:h] for row in m[:h]])
    w = small_product(e, b)
    s = [[None] * h for _ in range(h)]
    for i in range(h):
        for j in range(i, h):
            acc = b[0][i] * w[0][j]
            for k in range(1, h):
                acc = acc + b[k][i] * w[k][j]
            s[i][j] = s[j][i] = m[h + i][h + j] - acc
    t = small_inverse(s)
    x = small_product(w, t)
    top = [[None] * h for _ in range(h)]
    for i in range(h):
        for j in range(i, h):
            acc = x[i][0] * w[j][0]
            for k in range(1, h):
                acc = acc + x[i][k] * w[j][k]
            top[i][j] = top[j][i] = e[i][j] + acc
    neg = [[-v for v in row] for row in x]
    out = [top[i] + neg[i] for i in range(h)]
    out += [[neg[k][i] for k in range(h)] + t[i] for i in range(h)]
    return out


def pivot_groups(count, v):
    shape = (8, LANES)
    sub = lax.broadcasted_iota(jnp.int32, shape, 0)
    lane = lax.broadcasted_iota(jnp.int32, shape, 1)
    v = list(v)
    for g in range(count):
        p = 8 * g
        x = v[g]
        turn = LANES - 8 * count if g == count - 1 else 0
        rows = [jnp.broadcast_to(x[i : i + 1, :], shape) for i in range(8)]
        cols = [jnp.broadcast_to(x[:, p + t : p + t + 1], shape) for t in range(8)]
        m = [[None] * 8 for _ in range(8)]
        for i in range(8):
            for j in range(i, 8):
                m[i][j] = m[j][i] = jnp.broadcast_to(cols[j][i : i + 1, :], shape)
        e = small_inverse(m)
        pivots = (lane >= p) & (lane < p + 8)
        r = [jnp.where(pivots, (lane == p + i).astype(F32), rows[i]) for i in range(8)]
        q = []
        for i in range(8):
            acc = e[i][0] * r[0]
            for j in range(1, 8):
                acc = acc + e[i][j] * r[j]
            q.append(acc)
        new = []
        for k in range(len(v)):
            y = v[k]
            if k == g:
                y = q[0]
                for t in range(1, 8):
                    y = jnp.where(sub == t, q[t], y)
            else:
                acc = jnp.broadcast_to(y[:, p : p + 1], shape) * q[0]
                for t in range(1, 8):
                    acc = acc + jnp.broadcast_to(y[:, p + t : p + t + 1], shape) * q[t]
                y = jnp.where(pivots, 0.0, y) - acc
            new.append(pltpu.roll(y, turn, 1) if turn else y)
        v = new
    return tuple(v[count:] + v[:count])


RUN = 4


class Spread:
    def __init__(self, nb, r, b, all_ref, sems):
        self.nb, self.tiles, self.nx = nb, nb // 2, nb // RUN
        self.r, self.b, self.x, self.z = r, b, lax.div(b, RUN), lax.rem(b, RUN)
        self.all_ref = all_ref
        self.send1, self.recv1, self.send2, self.recv2, self.send3, self.recv3 = sems

    def slot(self, j, brick, count):
        start = pl.multiple_of(brick * COARSE, COARSE)
        return self.all_ref.at[j, pl.ds(start, count * COARSE), :]

    def remote(self, part, send_sem, recv_sem, x, z):
        return pltpu.make_async_remote_copy(
            src_ref=part, dst_ref=part, send_sem=send_sem, recv_sem=recv_sem,
            device_id=(self.r, x * RUN + z), device_id_type=MESH,
        )

    def arrived(self, j, brick, count, sem):
        part = self.slot(j, brick, count)
        pltpu.make_async_copy(part, part, sem).wait()

    def either(self, j, odd, even):
        if isinstance(j, int):
            (odd if j % 2 else even)()
        else:
            pl.when(lax.rem(j, 2) == 1)(odd)
            pl.when(lax.rem(j, 2) == 0)(even)

    def each1(self, j, act):
        part = self.slot(j, self.b, 1)

        def odd():
            for t in range(1, RUN):
                z = lax.rem(self.z + t, RUN)
                act(self.remote(part, self.send1.at[j, t], self.recv1.at[j, self.z], self.x, z))

        def even():
            for t in range(1, self.nx):
                x = lax.rem(self.x + t, self.nx)
                act(self.remote(part, self.send1.at[j, t], self.recv1.at[j, self.x], x, self.z))

        @pl.when(lax.div(self.b, 2) <= j)
        def _():
            self.either(j, odd, even)

    def each2(self, j, act, wait):
        def odd():
            for z in range(RUN):

                @pl.when((self.z != z) & (2 * self.x + z // 2 <= j))
                def _():
                    if wait:
                        self.arrived(j, self.x * RUN + z, 1, self.recv1.at[j, z])

            for count, when in ((RUN, 2 * self.x + 1 <= j), (2, 2 * self.x == j)):

                @pl.when(when)
                def _():
                    part = self.slot(j, self.x * RUN, count)
                    for t in range(1, self.nx):
                        x = lax.rem(self.x + t, self.nx)
                        act(self.remote(part, self.send2.at[j, t], self.recv2.at[j, self.x], x, self.z))

        def even():
            h = j // 2 if isinstance(j, int) else lax.div(j, 2)
            for x in range(self.nx):

                @pl.when(2 * x + lax.div(self.z, 2) <= j)
                def _():
                    brick = x * RUN + self.z
                    if wait:

                        @pl.when(self.x != x)
                        def _():
                            self.arrived(j, brick, 1, self.recv1.at[j, x])

                    for t in range(1, RUN):
                        z = lax.rem(self.z + t, RUN)
                        part = self.slot(j, brick, 1)
                        act(self.remote(part, self.send3.at[h, x, t], self.recv3.at[h, x, self.z], self.x, z))

        self.either(j, odd, even)

    def first(self, j):
        self.each1(j, lambda copy: copy.start())

    def second(self, j):
        self.each2(j, lambda copy: copy.start(), True)

    def need(self, j):
        def odd():
            for x in range(self.nx):
                for count, when in ((RUN, 2 * x + 1 <= j), (2, 2 * x == j)):

                    @pl.when((self.x != x) & when)
                    def _():
                        self.arrived(j, x * RUN, count, self.recv2.at[j, x])

        def even():
            h = j // 2 if isinstance(j, int) else lax.div(j, 2)
            for x in range(self.nx):
                for z in range(RUN):

                    @pl.when((self.z != z) & (2 * x + z // 2 <= j))
                    def _():
                        self.arrived(j, x * RUN + z, 1, self.recv3.at[h, x, z])

        self.either(j, odd, even)

    def finish(self):
        for j in range(self.tiles):
            self.each1(j, lambda copy: copy.wait_send())
            self.each2(j, lambda copy: copy.wait_send(), False)


def factor(nb, b, spread, all_ref, inverse_ref, u_ref, r_ref, l_ref, y_ref, z_ref, p_ref, d_ref):
    tiles = nb // 2
    sub = lax.broadcasted_iota(jnp.int32, (COARSE, W), 0)
    lane = lax.broadcasted_iota(jnp.int32, (COARSE, W), 1)
    half = tiles // 2
    unroll = 2
    turns = W // 8 // unroll

    def tile(k):
        return pl.ds(pl.multiple_of(k * W, W), W)

    def plain(it, v):
        return pivot_groups(unroll, v)

    def with_product(j, depth):
        def run(i, v):
            u = all_ref[j, tile(i), :] - dot(l_ref[i, :, :depth], u_ref[j, :depth, :])
            before = jnp.maximum(i - 1, 0)
            scaled = dot(p_ref[before], u_ref[j, tile(before), :])
            u_ref[j, tile(i), :] = u
            r_ref[j, tile(before), :] = scaled
            l_ref[j, :, tile(before)] = scaled.T
            return pivot_groups(unroll, v)

        return run

    def step(k, far, column):
        depth = (tiles - 1 if far else half) * W
        v = tuple(d_ref[8 * i : 8 * i + 8, :] for i in range(W // 8))
        if column:
            j = k + 1

            @pl.when(k + 5 < tiles)
            def _():
                spread.first(k + 5)

            @pl.when(k + 3 < tiles)
            def _():
                spread.second(k + 3)

            v = lax.fori_loop(0, turns - j, plain, v)
            spread.need(j)
            v = lax.fori_loop(0, half if far else j, with_product(j, (half - 1) * W), v)
            if far:
                v = lax.fori_loop(half, j, with_product(j, (tiles - 2) * W), v)
        else:
            v = lax.fori_loop(0, turns, plain, v)
        inverse = jnp.concatenate(v, axis=0)
        p_ref[k] = inverse
        if column:
            scaled = dot(inverse, u_ref[j, tile(k), :])
            r_ref[j, tile(k), :] = scaled
            l_ref[j, :, tile(k)] = scaled.T
            d_ref[...] = all_ref[j, tile(j), :] - dot(l_ref[j, :, :depth], u_ref[j, :depth, :])
        own = (lane + k * W == sub + b * COARSE).astype(F32)
        own = own - dot(y_ref[:, :depth], r_ref[k, :depth, :])
        y_ref[:, tile(k)] = own
        z_ref[k] = dot(own, inverse)

    def near_step(k, carry):
        step(k, False, True)
        return carry

    def far_step(k, carry):
        step(k, True, True)
        return carry

    spread.need(0)
    d_ref[...] = all_ref[0, :W, :]
    lax.fori_loop(0, half, near_step, 0)
    lax.fori_loop(half, tiles - 1, far_step, 0)
    step(tiles - 1, True, False)
    solved = [None] * tiles
    low = lane < COARSE
    for k in reversed(range(tiles)):
        acc = z_ref[k]
        for j in range(k + 1, tiles):
            acc = acc - dot(solved[j], l_ref[j, :, k * W : k * W + W])
        solved[k] = acc
        inverse_ref[2 * k] = jnp.where(low, acc, 0.0)
        inverse_ref[2 * k + 1] = jnp.where(low, pltpu.roll(acc, COARSE, 1), 0.0)


def whole_kernel(
    nr, nb, pattern_in, matrix_in, load_in, stiffness_in, local_in, intact_in, lists_in, basis_in,
    out_ref, pattern_ref, matrix_ref, load_ref, stiffness_ref, local_ref, intact_ref, lists_ref, basis_ref, in_sem, all_ref, inverse_ref, u_ref, r_ref, l_ref, y_ref, zf_ref, p_ref, d_ref,
    k_ref, m_ref, c_ref, ct_ref, sel_ref, selt_ref, col_ref, z_ref, w_ref, acc_ref,
    msg_ref, gather_ref, tot_ref, total_ref, face_ref, near_ref, send1, recv1, send2, recv2, send3, recv3,
    gather_send, gather_recv, total_send, total_recv, face_send, face_recv,
):
    r, b = lax.axis_index("rows"), lax.axis_index("bricks")
    tiles = nb // 2
    incoming = [
        pltpu.make_async_copy(src, dst, in_sem.at[i])
        for i, (src, dst) in enumerate(
            (
                (pattern_in, pattern_ref), (matrix_in, matrix_ref), (load_in, load_ref), (basis_in, basis_ref),
                (lists_in, lists_ref), (intact_in, intact_ref), (local_in, local_ref), (stiffness_in, stiffness_ref),
            )
        )
    ]
    for copy in incoming:
        copy.start()
    barrier = pltpu.get_barrier_semaphore()
    for t in range(1, nb):
        pl.semaphore_signal(
            barrier, inc=1, device_id=(r, lax.rem(b + t, nb)), device_id_type=MESH
        )
    for t in range(1, nr):
        pl.semaphore_signal(
            barrier, inc=1, device_id=(lax.rem(r + t, nr), b), device_id_type=MESH
        )
    mine = pl.ds(pl.multiple_of(b * COARSE, COARSE), COARSE)
    incoming[0].wait()
    incoming[1].wait()
    for j in range(tiles):
        left = matrix_ref[2 * j] * pattern_ref[0, 2 * j].astype(F32)
        right = matrix_ref[2 * j + 1] * pattern_ref[0, 2 * j + 1].astype(F32)
        all_ref[j, mine, :] = jnp.concatenate([left, right], axis=1)
    spread = Spread(nb, r, b, all_ref, (send1, recv1, send2, recv2, send3, recv3))
    pl.semaphore_wait(barrier, nb + nr - 2)
    for j in range(3):
        spread.first(j)
    for copy in incoming[2:]:
        copy.wait()
    lane8 = lax.broadcasted_iota(jnp.int32, (8, LANES), 1)
    lane1 = lax.broadcasted_iota(jnp.int32, (1, LANES), 1)
    gap = jnp.zeros((NDOF, LANES - NODES), F32)
    for e in range(6):
        span = slice(e * NODES, e * NODES + NODES)
        piece = jnp.concatenate([basis_ref[:, span], gap[:COARSE]], axis=1)
        c_ref[e] = piece
        turned = jnp.concatenate([piece, jnp.zeros((LANES - COARSE, LANES), F32)], axis=0).T
        ct_ref[span, :] = turned[:NODES]
    node_col = lax.broadcasted_iota(jnp.int32, (LANES, LANES), 0)
    node_row = lax.broadcasted_iota(jnp.int32, (LANES, LANES), 1)
    slots = jnp.full((1, LANES), -1, jnp.int32)
    swapped = slots
    for d in range(4):
        line = jnp.concatenate([lists_ref[d : d + 1, :], jnp.zeros((1, LANES - FACE), jnp.int32)], axis=1)
        for other in (False, True):
            at = 32 * (d ^ other)
            moved = pltpu.roll(line, at, 1) if at else line
            here = (lane1 >= at) & (lane1 < at + FACE)
            if other:
                swapped = jnp.where(here, moved, swapped)
            else:
                slots = jnp.where(here, moved, slots)
    sel_ref[:, :LANES] = (node_col == slots).astype(F32)
    sel_ref[:, LANES:] = (node_col == swapped).astype(F32)
    selt_ref[...] = sel_ref[:NODES, :LANES]
    eye = (node_col == node_row)[:NODES]

    def row_to_col(row, ref):
        for c in range(6):
            spread = jnp.where(eye, jnp.broadcast_to(row[c : c + 1, :], (NODES, LANES)), 0.0)
            ref[c * NODES : c * NODES + NODES, :] = jnp.broadcast_to(
                jnp.sum(spread, axis=1, keepdims=True), (NODES, LANES)
            )

    def stack(rows):
        return jnp.concatenate(rows + [jnp.zeros((8 - len(rows), LANES), F32)], axis=0)

    def col_to_row(ref):
        return stack(
            [
                jnp.sum(jnp.where(eye, ref[c * NODES : c * NODES + NODES, :], 0.0), axis=0, keepdims=True)
                for c in range(6)
            ]
        )

    def row_partners(t):
        return (r, lax.rem(b + t, nb))

    def col_partners(t):
        return (lax.rem(r + t, nr), b)

    def exchange(count, partners, msg, land, send_sem, recv_sem):
        for t in range(1, count):
            pltpu.make_async_remote_copy(
                src_ref=msg, dst_ref=land, send_sem=send_sem, recv_sem=recv_sem,
                device_id=partners(t), device_id_type=MESH,
            ).start()

    def wait_bytes(ref, sem):
        pltpu.make_async_copy(ref, ref, sem).wait()

    def gather_start(n, message):
        msg_ref[n] = message
        gather_ref[n, b] = message
        exchange(
            nb, row_partners, msg_ref.at[n], gather_ref.at[n, b], gather_send.at[n], gather_recv.at[n]
        )

    def gather_wait(n):
        wait_bytes(gather_ref.at[n, pl.ds(0, nb - 1)], gather_recv.at[n])

    def total_start(n):
        acc = gather_ref[n, 0]
        for j in range(1, nb):
            acc = acc + gather_ref[n, j]
        tot_ref[n] = acc
        total_ref[n, r] = acc
        exchange(
            nr, col_partners, tot_ref.at[n], total_ref.at[n, r], total_send.at[n], total_recv.at[n]
        )

    def total_wait(n):
        wait_bytes(total_ref.at[n, pl.ds(0, nr - 1)], total_recv.at[n])
        acc = total_ref[n, 0]
        for j in range(1, nr):
            acc = acc + total_ref[n, j]
        first = jnp.sum(jnp.where(lane1 == COARSE, acc, 0.0), axis=1, keepdims=True)
        second = jnp.sum(jnp.where(lane1 == COARSE + 1, acc, 0.0), axis=1, keepdims=True)
        return first, second

    def reduced(ref):
        return jnp.sum(ref[...] * ct_ref[...], axis=0, keepdims=True)

    def with_dots(message, first, second):
        one = jnp.sum(jnp.sum(first, axis=0, keepdims=True), axis=1, keepdims=True)
        two = jnp.sum(jnp.sum(second, axis=0, keepdims=True), axis=1, keepdims=True)
        message = jnp.where(lane1 == COARSE, one, message)
        return jnp.where(lane1 == COARSE + 1, two, message)

    def local_part(ref):
        return [jnp.sum(ref[...] * m_ref[e], axis=0, keepdims=True) for e in range(6)]

    def coarse_part(n):
        acc = inverse_ref[0] * gather_ref[n, 0]
        for j in range(1, nb):
            acc = acc + inverse_ref[j] * gather_ref[n, j]
        solved = jnp.sum(acc, axis=1, keepdims=True)
        return [jnp.sum(solved * c_ref[e], axis=0, keepdims=True) for e in range(6)]

    neighbours = [
        (lax.rem(r + nr - 1, nr), b, r > 0),
        (lax.rem(r + 1, nr), b, r < nr - 1),
        (r, lax.rem(b + nb - 1, nb), b > 0),
        (r, lax.rem(b + 1, nb), b < nb - 1),
    ]

    def face_start(n, row):
        both = dot(row, sel_ref[...])
        face_ref[n] = both[:, LANES:]
        for d in range(4):
            pltpu.make_async_remote_copy(
                src_ref=face_ref.at[n], dst_ref=near_ref.at[n, d ^ 1],
                send_sem=face_send.at[n, d], recv_sem=face_recv.at[n, d ^ 1],
                device_id=neighbours[d][:2], device_id_type=MESH,
            ).start()
        return both[:, :LANES]

    def operate(n, row, face, target):
        for c in range(6):
            rows = slice(c * NODES, c * NODES + NODES)
            acc = k_ref[0, rows, :] * row[0:1, :]
            for e in range(1, 6):
                acc = acc + k_ref[e, rows, :] * row[e : e + 1, :]
            acc_ref[rows, :] = acc
        stretch = face
        for d in range(4):
            wait_bytes(near_ref.at[n, d], face_recv.at[n, d])
            here = (lane8 >= 32 * d) & (lane8 < 32 * d + 32) & neighbours[d][2]
            stretch = stretch - jnp.where(here, near_ref[n, d], 0.0)
        for c in range(6):
            rows = slice(c * NODES, c * NODES + NODES)
            acc = acc_ref[rows, :] + selt_ref[...] * stretch[c : c + 1, :]
            target[rows, :] = jnp.broadcast_to(
                jnp.sum(acc, axis=1, keepdims=True), (NODES, LANES)
            )

    load = stack([jnp.concatenate([load_ref[:, c * NODES : c * NODES + NODES], gap[:1]], axis=1) for c in range(6)])
    row_to_col(load, col_ref)
    res = load
    gather_start(0, reduced(col_ref))
    for j in range(2):
        spread.second(j)
    spread.first(3)
    for ref in (u_ref, r_ref, l_ref, p_ref):
        for j in range(tiles):
            ref[j] = jnp.zeros(ref.shape[1:], F32)
    y_ref[...] = jnp.zeros(y_ref.shape, F32)
    spread.second(2)
    if tiles > 4:
        spread.first(4)
    intact = intact_ref[...].astype(F32)
    for e in range(6):
        span = slice(e * NODES, e * NODES + NODES)
        part = jnp.concatenate([stiffness_ref[:, span], gap], axis=1)
        mask = jnp.concatenate([intact, gap[:NODES]], axis=1)
        for c in range(6):
            rows = slice(c * NODES, c * NODES + NODES)
            k_ref[e, rows, :] = part[rows] * mask
        m_ref[e] = jnp.concatenate([local_ref[:, span], gap], axis=1)
    part = stack(local_part(col_ref))
    gather_wait(0)

    factor(nb, b, spread, all_ref, inverse_ref, u_ref, r_ref, l_ref, y_ref, zf_ref, p_ref, d_ref)

    u = part + stack(coarse_part(0))
    face = face_start(0, u)
    operate(0, u, face, w_ref)
    w = col_to_row(w_ref)
    p = s = q = sol = None
    dot_old = step_old = None
    for i in range(2):
        gather_start(i + 1, with_dots(reduced(w_ref), res * u, w * u))
        part = local_part(w_ref)
        gather_wait(i + 1)
        total_start(i + 1)
        m = stack([x + y for x, y in zip(part, coarse_part(i + 1))])
        face = face_start(i + 1, m)
        operate(i + 1, m, face, col_ref)
        v = col_to_row(col_ref)
        gamma, delta = total_wait(i + 1)
        if i == 0:
            step_size = gamma / delta
            p, s, q, zr = u, w, m, v
            z_ref[...] = col_ref[...]
            sol = step_size * p
        else:
            ratio = gamma / dot_old
            step_size = gamma / (delta - ratio * gamma / step_old)
            p, s, q, zr = u + ratio * p, w + ratio * s, m + ratio * q, v + ratio * zr
            sol = sol + step_size * p
        res = res - step_size * s
        u = u - step_size * q
        w = w - step_size * zr
        if i == 0:
            w_ref[...] = w_ref[...] - step_size * z_ref[...]
        dot_old, step_old = gamma, step_size
    gather_start(3, with_dots(jnp.zeros((1, LANES), F32), res * u, w * u))
    gather_wait(3)
    total_start(3)
    gamma, delta = total_wait(3)
    ratio = gamma / dot_old
    step_size = gamma / (delta - ratio * gamma / step_old)
    out_ref[0] = sol + step_size * (u + ratio * p)
    out_ref[1] = res - step_size * (w + ratio * s)

    spread.finish()
    for n in range(4):
        wait_bytes(gather_ref.at[n, pl.ds(0, nb - 1)], gather_send.at[n])
    for n in range(1, 4):
        wait_bytes(total_ref.at[n, pl.ds(0, nr - 1)], total_send.at[n])
    for n in range(3):
        for d in range(4):
            wait_bytes(face_ref.at[n], face_send.at[n, d])


VMEM = pl.BlockSpec(memory_space=pltpu.VMEM)
ANY = pl.BlockSpec(memory_space=pltpu.HBM)


def body(nr, nb, load, stiffness, local_inverse, intact, face_lists, coarse_basis, matrix, pattern):
    tiles = nb // 2
    order = nb * COARSE
    limit = 62 * 1024 * 1024
    out = pl.pallas_call(
        functools.partial(whole_kernel, nr, nb),
        out_shape=jax.ShapeDtypeStruct((2, 8, LANES), F32),
        in_specs=[ANY] * 8,
        out_specs=VMEM,
        scratch_shapes=[
            pltpu.SMEM((1, nb), jnp.int32),
            pltpu.VMEM((nb, COARSE, COARSE), F32),
            pltpu.VMEM((1, NDOF), F32),
            pltpu.VMEM((NDOF, NDOF), F32),
            pltpu.VMEM((NDOF, NDOF), F32),
            pltpu.VMEM((NODES, NODES), jnp.int32),
            pltpu.VMEM((4, FACE), jnp.int32),
            pltpu.VMEM((COARSE, NDOF), F32),
            pltpu.SemaphoreType.DMA((8,)),
            pltpu.VMEM((tiles, order, LANES), F32),
            pltpu.VMEM((nb, COARSE, LANES), F32),
            pltpu.VMEM((tiles, order, LANES), F32),
            pltpu.VMEM((tiles, order, LANES), F32),
            pltpu.VMEM((tiles, W, order), F32),
            pltpu.VMEM((COARSE, order), F32),
            pltpu.VMEM((tiles, COARSE, W), F32),
            pltpu.VMEM((tiles, W, W), F32),
            pltpu.VMEM((W, W), F32),
            pltpu.VMEM((6, NDOF, LANES), F32),
            pltpu.VMEM((6, NDOF, LANES), F32),
            pltpu.VMEM((6, COARSE, LANES), F32),
            pltpu.VMEM((NDOF, LANES), F32),
            pltpu.VMEM((LANES, 2 * LANES), F32),
            pltpu.VMEM((NODES, LANES), F32),
            pltpu.VMEM((NDOF, LANES), F32),
            pltpu.VMEM((NDOF, LANES), F32),
            pltpu.VMEM((NDOF, LANES), F32),
            pltpu.VMEM((NDOF, LANES), F32),
            pltpu.VMEM((4, 1, LANES), F32),
            pltpu.VMEM((4, nb, 1, LANES), F32),
            pltpu.VMEM((4, 1, LANES), F32),
            pltpu.VMEM((4, nr, 1, LANES), F32),
            pltpu.VMEM((3, 8, LANES), F32),
            pltpu.VMEM((3, 4, 8, LANES), F32),
            pltpu.SemaphoreType.DMA((tiles, RUN)),
            pltpu.SemaphoreType.DMA((tiles, RUN)),
            pltpu.SemaphoreType.DMA((tiles, nb // RUN)),
            pltpu.SemaphoreType.DMA((tiles, nb // RUN)),
            pltpu.SemaphoreType.DMA((tiles // 2, nb // RUN, RUN)),
            pltpu.SemaphoreType.DMA((tiles // 2, nb // RUN, RUN)),
            pltpu.SemaphoreType.DMA((4,)),
            pltpu.SemaphoreType.DMA((4,)),
            pltpu.SemaphoreType.DMA((4,)),
            pltpu.SemaphoreType.DMA((4,)),
            pltpu.SemaphoreType.DMA((3, 4)),
            pltpu.SemaphoreType.DMA((3, 4)),
        ],
        compiler_params=pltpu.CompilerParams(
            collective_id=0, has_side_effects=True, vmem_limit_bytes=limit
        ),
        name="whole",
    )(
        pattern.reshape(1, nb),
        matrix.reshape(nb, COARSE, COARSE),
        load.reshape(1, NDOF),
        stiffness.reshape(NDOF, NDOF),
        local_inverse.reshape(NDOF, NDOF),
        intact.reshape(NODES, NODES),
        face_lists.reshape(4, FACE),
        coarse_basis.reshape(COARSE, NDOF),
    )
    flat = out[:, :6, :NODES].reshape(2, 1, 1, NDOF)
    return flat[0], flat[1]


def solution(mesh):
    in_specs = (
        P("rows", "bricks", None),
        P("rows", "bricks", None, None),
        P("rows", "bricks", None, None),
        P("rows", "bricks", None, None),
        P("rows", "bricks", None, None),
        P("rows", "bricks", None, None),
        P("rows", "bricks", None, None, None),
        P("rows", "bricks", None),
    )
    out_specs = (P("rows", "bricks", None), P("rows", "bricks", None))
    run = functools.partial(body, mesh.shape["rows"], mesh.shape["bricks"])
    return jax.shard_map(run, mesh=mesh, in_specs=in_specs, out_specs=out_specs, check_vma=False)
```

```python
import functools

import jax
import jax.numpy as jnp
from jax import lax
from jax.experimental import pallas as pl
from jax.experimental.pallas import tpu as pltpu
from jax.sharding import PartitionSpec as P

MESH = pl.DeviceIdType.MESH
HI = lax.Precision.HIGHEST
MID = lax.Precision.HIGH
F32 = jnp.float32
NODES, NDOF, COARSE, FACE, W = 96, 576, 64, 24, 128
LANES = 128


def dot(a, b, precision=HI):
    return lax.dot_general(
        a, b, (((1,), (0,)), ((), ())), precision=precision, preferred_element_type=F32
    )


def small_product(a, b):
    out = []
    for row in a:
        line = []
        for j in range(len(b[0])):
            acc = row[0] * b[0][j]
            for k in range(1, len(b)):
                acc = acc + row[k] * b[k][j]
            line.append(acc)
        out.append(line)
    return out


def small_inverse(m):
    n = len(m)
    if n == 2:
        a, b, d = m[0][0], m[0][1], m[1][1]
        r = 1.0 / (a * d - b * b)
        off = -(b * r)
        return [[d * r, off], [off, a * r]]
    h = n // 2
    b = [row[h:] for row in m[:h]]
    e = small_inverse([row[:h] for row in m[:h]])
    w = small_product(e, b)
    s = [[None] * h for _ in range(h)]
    for i in range(h):
        for j in range(i, h):
            acc = b[0][i] * w[0][j]
            for k in range(1, h):
                acc = acc + b[k][i] * w[k][j]
            s[i][j] = s[j][i] = m[h + i][h + j] - acc
    t = small_inverse(s)
    x = small_product(w, t)
    top = [[None] * h for _ in range(h)]
    for i in range(h):
        for j in range(i, h):
            acc = x[i][0] * w[j][0]
            for k in range(1, h):
                acc = acc + x[i][k] * w[j][k]
            top[i][j] = top[j][i] = e[i][j] + acc
    neg = [[-v for v in row] for row in x]
    out = [top[i] + neg[i] for i in range(h)]
    out += [[neg[k][i] for k in range(h)] + t[i] for i in range(h)]
    return out


def pivot_groups(count, v):
    shape = (8, LANES)
    sub = lax.broadcasted_iota(jnp.int32, shape, 0)
    lane = lax.broadcasted_iota(jnp.int32, shape, 1)
    v = list(v)
    for g in range(count):
        p = 8 * g
        x = v[g]
        turn = LANES - 8 * count if g == count - 1 else 0
        rows = [jnp.broadcast_to(x[i : i + 1, :], shape) for i in range(8)]
        cols = [jnp.broadcast_to(x[:, p + t : p + t + 1], shape) for t in range(8)]
        m = [[None] * 8 for _ in range(8)]
        for i in range(8):
            for j in range(i, 8):
                m[i][j] = m[j][i] = jnp.broadcast_to(cols[j][i : i + 1, :], shape)
        e = small_inverse(m)
        pivots = (lane >= p) & (lane < p + 8)
        r = [jnp.where(pivots, (lane == p + i).astype(F32), rows[i]) for i in range(8)]
        q = []
        for i in range(8):
            acc = e[i][0] * r[0]
            for j in range(1, 8):
                acc = acc + e[i][j] * r[j]
            q.append(acc)
        new = []
        for k in range(len(v)):
            y = v[k]
            if k == g:
                y = q[0]
                for t in range(1, 8):
                    y = jnp.where(sub == t, q[t], y)
            else:
                acc = jnp.broadcast_to(y[:, p : p + 1], shape) * q[0]
                for t in range(1, 8):
                    acc = acc + jnp.broadcast_to(y[:, p + t : p + t + 1], shape) * q[t]
                y = jnp.where(pivots, 0.0, y) - acc
            new.append(pltpu.roll(y, turn, 1) if turn else y)
        v = new
    return tuple(v[count:] + v[:count])


RUN = 4


class Spread:
    def __init__(self, nb, r, b, all_ref, sems):
        self.nb, self.tiles, self.nx = nb, nb // 2, nb // RUN
        self.r, self.b, self.x, self.z = r, b, lax.div(b, RUN), lax.rem(b, RUN)
        self.all_ref = all_ref
        self.send1, self.recv1, self.send2, self.recv2, self.send3, self.recv3 = sems

    def slot(self, j, brick, count):
        start = pl.multiple_of(brick * COARSE, COARSE)
        return self.all_ref.at[j, pl.ds(start, count * COARSE), :]

    def remote(self, part, send_sem, recv_sem, x, z):
        return pltpu.make_async_remote_copy(
            src_ref=part, dst_ref=part, send_sem=send_sem, recv_sem=recv_sem,
            device_id=(self.r, x * RUN + z), device_id_type=MESH,
        )

    def arrived(self, j, brick, count, sem):
        part = self.slot(j, brick, count)
        pltpu.make_async_copy(part, part, sem).wait()

    def either(self, j, odd, even):
        if isinstance(j, int):
            (odd if j % 2 else even)()
        else:
            pl.when(lax.rem(j, 2) == 1)(odd)
            pl.when(lax.rem(j, 2) == 0)(even)

    def each1(self, j, act):
        part = self.slot(j, self.b, 1)

        def odd():
            for t in range(1, RUN):
                z = lax.rem(self.z + t, RUN)
                act(self.remote(part, self.send1.at[j, t], self.recv1.at[j, self.z], self.x, z))

        def even():
            for t in range(1, self.nx):
                x = lax.rem(self.x + t, self.nx)
                act(self.remote(part, self.send1.at[j, t], self.recv1.at[j, self.x], x, self.z))

        @pl.when(lax.div(self.b, 2) <= j)
        def _():
            self.either(j, odd, even)

    def each2(self, j, act, wait):
        def odd():
            for z in range(RUN):

                @pl.when((self.z != z) & (2 * self.x + z // 2 <= j))
                def _():
                    if wait:
                        self.arrived(j, self.x * RUN + z, 1, self.recv1.at[j, z])

            for count, when in ((RUN, 2 * self.x + 1 <= j), (2, 2 * self.x == j)):

                @pl.when(when)
                def _():
                    part = self.slot(j, self.x * RUN, count)
                    for t in range(1, self.nx):
                        x = lax.rem(self.x + t, self.nx)
                        act(self.remote(part, self.send2.at[j, t], self.recv2.at[j, self.x], x, self.z))

        def even():
            h = j // 2 if isinstance(j, int) else lax.div(j, 2)
            for x in range(self.nx):

                @pl.when(2 * x + lax.div(self.z, 2) <= j)
                def _():
                    brick = x * RUN + self.z
                    if wait:

                        @pl.when(self.x != x)
                        def _():
                            self.arrived(j, brick, 1, self.recv1.at[j, x])

                    for t in range(1, RUN):
                        z = lax.rem(self.z + t, RUN)
                        part = self.slot(j, brick, 1)
                        act(self.remote(part, self.send3.at[h, x, t], self.recv3.at[h, x, self.z], self.x, z))

        self.either(j, odd, even)

    def first(self, j):
        self.each1(j, lambda copy: copy.start())

    def second(self, j):
        self.each2(j, lambda copy: copy.start(), True)

    def need(self, j):
        def odd():
            for x in range(self.nx):
                for count, when in ((RUN, 2 * x + 1 <= j), (2, 2 * x == j)):

                    @pl.when((self.x != x) & when)
                    def _():
                        self.arrived(j, x * RUN, count, self.recv2.at[j, x])

        def even():
            h = j // 2 if isinstance(j, int) else lax.div(j, 2)
            for x in range(self.nx):
                for z in range(RUN):

                    @pl.when((self.z != z) & (2 * x + z // 2 <= j))
                    def _():
                        self.arrived(j, x * RUN + z, 1, self.recv3.at[h, x, z])

        self.either(j, odd, even)

    def finish(self):
        for j in range(self.tiles):
            self.each1(j, lambda copy: copy.wait_send())
            self.each2(j, lambda copy: copy.wait_send(), False)


def factor(nb, b, spread, all_ref, inverse_ref, u_ref, r_ref, l_ref, y_ref, z_ref, p_ref, d_ref):
    tiles = nb // 2
    sub = lax.broadcasted_iota(jnp.int32, (COARSE, W), 0)
    lane = lax.broadcasted_iota(jnp.int32, (COARSE, W), 1)
    half = tiles // 2
    unroll = 2
    turns = W // 8 // unroll

    def tile(k):
        return pl.ds(pl.multiple_of(k * W, W), W)

    def plain(it, v):
        return pivot_groups(unroll, v)

    def with_product(j, depth):
        def run(i, v):
            u = all_ref[j, tile(i), :] - dot(l_ref[i, :, :depth], u_ref[j, :depth, :], MID)
            before = jnp.maximum(i - 1, 0)
            scaled = dot(p_ref[before], u_ref[j, tile(before), :], MID)
            u_ref[j, tile(i), :] = u
            r_ref[j, tile(before), :] = scaled
            l_ref[j, :, tile(before)] = scaled.T
            return pivot_groups(unroll, v)

        return run

    def step(k, far, column):
        depth = (tiles - 1 if far else half) * W
        v = tuple(d_ref[8 * i : 8 * i + 8, :] for i in range(W // 8))
        if column:
            j = k + 1

            @pl.when(k + 5 < tiles)
            def _():
                spread.first(k + 5)

            @pl.when(k + 3 < tiles)
            def _():
                spread.second(k + 3)

            v = lax.fori_loop(0, turns - j, plain, v)
            spread.need(j)
            v = lax.fori_loop(0, half if far else j, with_product(j, (half - 1) * W), v)
            if far:
                v = lax.fori_loop(half, j, with_product(j, (tiles - 2) * W), v)
        else:
            v = lax.fori_loop(0, turns, plain, v)
        inverse = jnp.concatenate(v, axis=0)
        p_ref[k] = inverse
        if column:
            scaled = dot(inverse, u_ref[j, tile(k), :])
            r_ref[j, tile(k), :] = scaled
            l_ref[j, :, tile(k)] = scaled.T
            d_ref[...] = all_ref[j, tile(j), :] - dot(l_ref[j, :, :depth], u_ref[j, :depth, :])
        own = (lane + k * W == sub + b * COARSE).astype(F32)
        own = own - dot(y_ref[:, :depth], r_ref[k, :depth, :], MID)
        y_ref[:, tile(k)] = own
        z_ref[k] = dot(own, inverse, MID)

    def near_step(k, carry):
        step(k, False, True)
        return carry

    def far_step(k, carry):
        step(k, True, True)
        return carry

    spread.need(0)
    d_ref[...] = all_ref[0, :W, :]
    lax.fori_loop(0, half, near_step, 0)
    lax.fori_loop(half, tiles - 1, far_step, 0)
    step(tiles - 1, True, False)
    solved = [None] * tiles
    low = lane < COARSE
    for k in reversed(range(tiles)):
        acc = z_ref[k]
        for j in range(k + 1, tiles):
            acc = acc - dot(solved[j], l_ref[j, :, k * W : k * W + W], MID)
        solved[k] = acc
        inverse_ref[2 * k] = jnp.where(low, acc, 0.0)
        inverse_ref[2 * k + 1] = jnp.where(low, pltpu.roll(acc, COARSE, 1), 0.0)


def whole_kernel(
    nr, nb, pattern_in, matrix_in, load_in, stiffness_in, local_in, intact_in, lists_in, basis_in,
    out_ref, pattern_ref, matrix_ref, load_ref, stiffness_ref, local_ref, intact_ref, lists_ref, basis_ref, in_sem, all_ref, inverse_ref, u_ref, r_ref, l_ref, y_ref, zf_ref, p_ref, d_ref,
    k_ref, m_ref, c_ref, ct_ref, sel_ref, selt_ref, col_ref, z_ref, w_ref, acc_ref,
    msg_ref, gather_ref, tot_ref, total_ref, face_ref, near_ref, send1, recv1, send2, recv2, send3, recv3,
    gather_send, gather_recv, total_send, total_recv, face_send, face_recv,
):
    r, b = lax.axis_index("rows"), lax.axis_index("bricks")
    tiles = nb // 2
    incoming = [
        pltpu.make_async_copy(src, dst, in_sem.at[i])
        for i, (src, dst) in enumerate(
            (
                (pattern_in, pattern_ref), (matrix_in, matrix_ref), (load_in, load_ref), (basis_in, basis_ref),
                (lists_in, lists_ref), (intact_in, intact_ref), (local_in, local_ref), (stiffness_in, stiffness_ref),
            )
        )
    ]
    for copy in incoming:
        copy.start()
    barrier = pltpu.get_barrier_semaphore()
    for t in range(1, nb):
        pl.semaphore_signal(
            barrier, inc=1, device_id=(r, lax.rem(b + t, nb)), device_id_type=MESH
        )
    for t in range(1, nr):
        pl.semaphore_signal(
            barrier, inc=1, device_id=(lax.rem(r + t, nr), b), device_id_type=MESH
        )
    mine = pl.ds(pl.multiple_of(b * COARSE, COARSE), COARSE)
    incoming[0].wait()
    incoming[1].wait()
    for j in range(tiles):
        left = matrix_ref[2 * j] * pattern_ref[0, 2 * j].astype(F32)
        right = matrix_ref[2 * j + 1] * pattern_ref[0, 2 * j + 1].astype(F32)
        all_ref[j, mine, :] = jnp.concatenate([left, right], axis=1)
    spread = Spread(nb, r, b, all_ref, (send1, recv1, send2, recv2, send3, recv3))
    pl.semaphore_wait(barrier, nb + nr - 2)
    for j in range(3):
        spread.first(j)
    for copy in incoming[2:]:
        copy.wait()
    lane8 = lax.broadcasted_iota(jnp.int32, (8, LANES), 1)
    lane1 = lax.broadcasted_iota(jnp.int32, (1, LANES), 1)
    gap = jnp.zeros((NDOF, LANES - NODES), F32)
    for e in range(6):
        span = slice(e * NODES, e * NODES + NODES)
        piece = jnp.concatenate([basis_ref[:, span], gap[:COARSE]], axis=1)
        c_ref[e] = piece
        turned = jnp.concatenate([piece, jnp.zeros((LANES - COARSE, LANES), F32)], axis=0).T
        ct_ref[span, :] = turned[:NODES]
    node_col = lax.broadcasted_iota(jnp.int32, (LANES, LANES), 0)
    node_row = lax.broadcasted_iota(jnp.int32, (LANES, LANES), 1)
    slots = jnp.full((1, LANES), -1, jnp.int32)
    swapped = slots
    for d in range(4):
        line = jnp.concatenate([lists_ref[d : d + 1, :], jnp.zeros((1, LANES - FACE), jnp.int32)], axis=1)
        for other in (False, True):
            at = 32 * (d ^ other)
            moved = pltpu.roll(line, at, 1) if at else line
            here = (lane1 >= at) & (lane1 < at + FACE)
            if other:
                swapped = jnp.where(here, moved, swapped)
            else:
                slots = jnp.where(here, moved, slots)
    sel_ref[:, :LANES] = (node_col == slots).astype(F32)
    sel_ref[:, LANES:] = (node_col == swapped).astype(F32)
    selt_ref[...] = sel_ref[:NODES, :LANES]
    eye = (node_col == node_row)[:NODES]

    def row_to_col(row, ref):
        for c in range(6):
            spread = jnp.where(eye, jnp.broadcast_to(row[c : c + 1, :], (NODES, LANES)), 0.0)
            ref[c * NODES : c * NODES + NODES, :] = jnp.broadcast_to(
                jnp.sum(spread, axis=1, keepdims=True), (NODES, LANES)
            )

    def stack(rows):
        return jnp.concatenate(rows + [jnp.zeros((8 - len(rows), LANES), F32)], axis=0)

    def col_to_row(ref):
        return stack(
            [
                jnp.sum(jnp.where(eye, ref[c * NODES : c * NODES + NODES, :], 0.0), axis=0, keepdims=True)
                for c in range(6)
            ]
        )

    def row_partners(t):
        return (r, lax.rem(b + t, nb))

    def col_partners(t):
        return (lax.rem(r + t, nr), b)

    def exchange(count, partners, msg, land, send_sem, recv_sem):
        for t in range(1, count):
            pltpu.make_async_remote_copy(
                src_ref=msg, dst_ref=land, send_sem=send_sem, recv_sem=recv_sem,
                device_id=partners(t), device_id_type=MESH,
            ).start()

    def wait_bytes(ref, sem):
        pltpu.make_async_copy(ref, ref, sem).wait()

    def gather_start(n, message):
        msg_ref[n] = message
        gather_ref[n, b] = message
        exchange(
            nb, row_partners, msg_ref.at[n], gather_ref.at[n, b], gather_send.at[n], gather_recv.at[n]
        )

    def gather_wait(n):
        wait_bytes(gather_ref.at[n, pl.ds(0, nb - 1)], gather_recv.at[n])

    def total_start(n):
        acc = gather_ref[n, 0]
        for j in range(1, nb):
            acc = acc + gather_ref[n, j]
        tot_ref[n] = acc
        total_ref[n, r] = acc
        exchange(
            nr, col_partners, tot_ref.at[n], total_ref.at[n, r], total_send.at[n], total_recv.at[n]
        )

    def total_wait(n):
        wait_bytes(total_ref.at[n, pl.ds(0, nr - 1)], total_recv.at[n])
        acc = total_ref[n, 0]
        for j in range(1, nr):
            acc = acc + total_ref[n, j]
        first = jnp.sum(jnp.where(lane1 == COARSE, acc, 0.0), axis=1, keepdims=True)
        second = jnp.sum(jnp.where(lane1 == COARSE + 1, acc, 0.0), axis=1, keepdims=True)
        return first, second

    def reduced(ref):
        return jnp.sum(ref[...] * ct_ref[...], axis=0, keepdims=True)

    def with_dots(message, first, second):
        one = jnp.sum(jnp.sum(first, axis=0, keepdims=True), axis=1, keepdims=True)
        two = jnp.sum(jnp.sum(second, axis=0, keepdims=True), axis=1, keepdims=True)
        message = jnp.where(lane1 == COARSE, one, message)
        return jnp.where(lane1 == COARSE + 1, two, message)

    def local_part(ref):
        return [jnp.sum(ref[...] * m_ref[e], axis=0, keepdims=True) for e in range(6)]

    def coarse_part(n):
        acc = inverse_ref[0] * gather_ref[n, 0]
        for j in range(1, nb):
            acc = acc + inverse_ref[j] * gather_ref[n, j]
        solved = jnp.sum(acc, axis=1, keepdims=True)
        return [jnp.sum(solved * c_ref[e], axis=0, keepdims=True) for e in range(6)]

    neighbours = [
        (lax.rem(r + nr - 1, nr), b, r > 0),
        (lax.rem(r + 1, nr), b, r < nr - 1),
        (r, lax.rem(b + nb - 1, nb), b > 0),
        (r, lax.rem(b + 1, nb), b < nb - 1),
    ]

    def face_start(n, row):
        both = dot(row, sel_ref[...])
        face_ref[n] = both[:, LANES:]
        for d in range(4):
            pltpu.make_async_remote_copy(
                src_ref=face_ref.at[n], dst_ref=near_ref.at[n, d ^ 1],
                send_sem=face_send.at[n, d], recv_sem=face_recv.at[n, d ^ 1],
                device_id=neighbours[d][:2], device_id_type=MESH,
            ).start()
        return both[:, :LANES]

    def operate(n, row, face, target):
        for c in range(6):
            rows = slice(c * NODES, c * NODES + NODES)
            acc = k_ref[0, rows, :] * row[0:1, :]
            for e in range(1, 6):
                acc = acc + k_ref[e, rows, :] * row[e : e + 1, :]
            acc_ref[rows, :] = acc
        stretch = face
        for d in range(4):
            wait_bytes(near_ref.at[n, d], face_recv.at[n, d])
            here = (lane8 >= 32 * d) & (lane8 < 32 * d + 32) & neighbours[d][2]
            stretch = stretch - jnp.where(here, near_ref[n, d], 0.0)
        for c in range(6):
            rows = slice(c * NODES, c * NODES + NODES)
            acc = acc_ref[rows, :] + selt_ref[...] * stretch[c : c + 1, :]
            target[rows, :] = jnp.broadcast_to(
                jnp.sum(acc, axis=1, keepdims=True), (NODES, LANES)
            )

    load = stack([jnp.concatenate([load_ref[:, c * NODES : c * NODES + NODES], gap[:1]], axis=1) for c in range(6)])
    row_to_col(load, col_ref)
    res = load
    gather_start(0, reduced(col_ref))
    for j in range(2):
        spread.second(j)
    spread.first(3)
    for ref in (u_ref, r_ref, l_ref, p_ref):
        for j in range(tiles):
            ref[j] = jnp.zeros(ref.shape[1:], F32)
    y_ref[...] = jnp.zeros(y_ref.shape, F32)
    spread.second(2)
    if tiles > 4:
        spread.first(4)
    intact = intact_ref[...].astype(F32)
    for e in range(6):
        span = slice(e * NODES, e * NODES + NODES)
        part = jnp.concatenate([stiffness_ref[:, span], gap], axis=1)
        mask = jnp.concatenate([intact, gap[:NODES]], axis=1)
        for c in range(6):
            rows = slice(c * NODES, c * NODES + NODES)
            k_ref[e, rows, :] = part[rows] * mask
        m_ref[e] = jnp.concatenate([local_ref[:, span], gap], axis=1)
    part = stack(local_part(col_ref))

    factor(nb, b, spread, all_ref, inverse_ref, u_ref, r_ref, l_ref, y_ref, zf_ref, p_ref, d_ref)

    gather_wait(0)
    u = part + stack(coarse_part(0))
    face = face_start(0, u)
    operate(0, u, face, w_ref)
    w = col_to_row(w_ref)
    p = s = q = sol = None
    dot_old = step_old = None
    for i in range(2):
        gather_start(i + 1, with_dots(reduced(w_ref), res * u, w * u))
        part = local_part(w_ref)
        gather_wait(i + 1)
        total_start(i + 1)
        m = stack([x + y for x, y in zip(part, coarse_part(i + 1))])
        face = face_start(i + 1, m)
        operate(i + 1, m, face, col_ref)
        v = col_to_row(col_ref)
        gamma, delta = total_wait(i + 1)
        if i == 0:
            step_size = gamma / delta
            p, s, q, zr = u, w, m, v
            z_ref[...] = col_ref[...]
            sol = step_size * p
        else:
            ratio = gamma / dot_old
            step_size = gamma / (delta - ratio * gamma / step_old)
            p, s, q, zr = u + ratio * p, w + ratio * s, m + ratio * q, v + ratio * zr
            sol = sol + step_size * p
        res = res - step_size * s
        u = u - step_size * q
        w = w - step_size * zr
        if i == 0:
            w_ref[...] = w_ref[...] - step_size * z_ref[...]
        dot_old, step_old = gamma, step_size
    gather_start(3, with_dots(jnp.zeros((1, LANES), F32), res * u, w * u))
    gather_wait(3)
    total_start(3)
    gamma, delta = total_wait(3)
    ratio = gamma / dot_old
    step_size = gamma / (delta - ratio * gamma / step_old)
    out_ref[0] = sol + step_size * (u + ratio * p)
    out_ref[1] = res - step_size * (w + ratio * s)

    spread.finish()
    for n in range(4):
        wait_bytes(gather_ref.at[n, pl.ds(0, nb - 1)], gather_send.at[n])
    for n in range(1, 4):
        wait_bytes(total_ref.at[n, pl.ds(0, nr - 1)], total_send.at[n])
    for n in range(3):
        for d in range(4):
            wait_bytes(face_ref.at[n], face_send.at[n, d])


VMEM = pl.BlockSpec(memory_space=pltpu.VMEM)
ANY = pl.BlockSpec(memory_space=pltpu.HBM)


def body(nr, nb, load, stiffness, local_inverse, intact, face_lists, coarse_basis, matrix, pattern):
    tiles = nb // 2
    order = nb * COARSE
    limit = 62 * 1024 * 1024
    out = pl.pallas_call(
        functools.partial(whole_kernel, nr, nb),
        out_shape=jax.ShapeDtypeStruct((2, 8, LANES), F32),
        in_specs=[ANY] * 8,
        out_specs=VMEM,
        scratch_shapes=[
            pltpu.SMEM((1, nb), jnp.int32),
            pltpu.VMEM((nb, COARSE, COARSE), F32),
            pltpu.VMEM((1, NDOF), F32),
            pltpu.VMEM((NDOF, NDOF), F32),
            pltpu.VMEM((NDOF, NDOF), F32),
            pltpu.VMEM((NODES, NODES), jnp.int32),
            pltpu.VMEM((4, FACE), jnp.int32),
            pltpu.VMEM((COARSE, NDOF), F32),
            pltpu.SemaphoreType.DMA((8,)),
            pltpu.VMEM((tiles, order, LANES), F32),
            pltpu.VMEM((nb, COARSE, LANES), F32),
            pltpu.VMEM((tiles, order, LANES), F32),
            pltpu.VMEM((tiles, order, LANES), F32),
            pltpu.VMEM((tiles, W, order), F32),
            pltpu.VMEM((COARSE, order), F32),
            pltpu.VMEM((tiles, COARSE, W), F32),
            pltpu.VMEM((tiles, W, W), F32),
            pltpu.VMEM((W, W), F32),
            pltpu.VMEM((6, NDOF, LANES), F32),
            pltpu.VMEM((6, NDOF, LANES), F32),
            pltpu.VMEM((6, COARSE, LANES), F32),
            pltpu.VMEM((NDOF, LANES), F32),
            pltpu.VMEM((LANES, 2 * LANES), F32),
            pltpu.VMEM((NODES, LANES), F32),
            pltpu.VMEM((NDOF, LANES), F32),
            pltpu.VMEM((NDOF, LANES), F32),
            pltpu.VMEM((NDOF, LANES), F32),
            pltpu.VMEM((NDOF, LANES), F32),
            pltpu.VMEM((4, 1, LANES), F32),
            pltpu.VMEM((4, nb, 1, LANES), F32),
            pltpu.VMEM((4, 1, LANES), F32),
            pltpu.VMEM((4, nr, 1, LANES), F32),
            pltpu.VMEM((3, 8, LANES), F32),
            pltpu.VMEM((3, 4, 8, LANES), F32),
            pltpu.SemaphoreType.DMA((tiles, RUN)),
            pltpu.SemaphoreType.DMA((tiles, RUN)),
            pltpu.SemaphoreType.DMA((tiles, nb // RUN)),
            pltpu.SemaphoreType.DMA((tiles, nb // RUN)),
            pltpu.SemaphoreType.DMA((tiles // 2, nb // RUN, RUN)),
            pltpu.SemaphoreType.DMA((tiles // 2, nb // RUN, RUN)),
            pltpu.SemaphoreType.DMA((4,)),
            pltpu.SemaphoreType.DMA((4,)),
            pltpu.SemaphoreType.DMA((4,)),
            pltpu.SemaphoreType.DMA((4,)),
            pltpu.SemaphoreType.DMA((3, 4)),
            pltpu.SemaphoreType.DMA((3, 4)),
        ],
        compiler_params=pltpu.CompilerParams(
            collective_id=0, has_side_effects=True, vmem_limit_bytes=limit
        ),
        name="whole",
    )(
        pattern.reshape(1, nb),
        matrix.reshape(nb, COARSE, COARSE),
        load.reshape(1, NDOF),
        stiffness.reshape(NDOF, NDOF),
        local_inverse.reshape(NDOF, NDOF),
        intact.reshape(NODES, NODES),
        face_lists.reshape(4, FACE),
        coarse_basis.reshape(COARSE, NDOF),
    )
    flat = out[:, :6, :NODES].reshape(2, 1, 1, NDOF)
    return flat[0], flat[1]


def solution(mesh):
    in_specs = (
        P("rows", "bricks", None),
        P("rows", "bricks", None, None),
        P("rows", "bricks", None, None),
        P("rows", "bricks", None, None),
        P("rows", "bricks", None, None),
        P("rows", "bricks", None, None),
        P("rows", "bricks", None, None, None),
        P("rows", "bricks", None),
    )
    out_specs = (P("rows", "bricks", None), P("rows", "bricks", None))
    run = functools.partial(body, mesh.shape["rows"], mesh.shape["bricks"])
    return jax.shard_map(run, mesh=mesh, in_specs=in_specs, out_specs=out_specs, check_vma=False)
```

```python
import functools

import jax
import jax.numpy as jnp
from jax import lax
from jax.experimental import pallas as pl
from jax.experimental.pallas import tpu as pltpu
from jax.sharding import PartitionSpec as P

MESH = pl.DeviceIdType.MESH
HI = lax.Precision.HIGHEST
MID = lax.Precision.HIGH
F32 = jnp.float32
NODES, NDOF, COARSE, FACE, W = 96, 576, 64, 24, 128
LANES = 128


def dot(a, b, precision=HI):
    return lax.dot_general(
        a, b, (((1,), (0,)), ((), ())), precision=precision, preferred_element_type=F32
    )


def small_product(a, b):
    out = []
    for row in a:
        line = []
        for j in range(len(b[0])):
            acc = row[0] * b[0][j]
            for k in range(1, len(b)):
                acc = acc + row[k] * b[k][j]
            line.append(acc)
        out.append(line)
    return out


def small_inverse(m):
    n = len(m)
    if n == 2:
        a, b, d = m[0][0], m[0][1], m[1][1]
        r = 1.0 / (a * d - b * b)
        off = -(b * r)
        return [[d * r, off], [off, a * r]]
    h = n // 2
    b = [row[h:] for row in m[:h]]
    e = small_inverse([row[:h] for row in m[:h]])
    w = small_product(e, b)
    s = [[None] * h for _ in range(h)]
    for i in range(h):
        for j in range(i, h):
            acc = b[0][i] * w[0][j]
            for k in range(1, h):
                acc = acc + b[k][i] * w[k][j]
            s[i][j] = s[j][i] = m[h + i][h + j] - acc
    t = small_inverse(s)
    x = small_product(w, t)
    top = [[None] * h for _ in range(h)]
    for i in range(h):
        for j in range(i, h):
            acc = x[i][0] * w[j][0]
            for k in range(1, h):
                acc = acc + x[i][k] * w[j][k]
            top[i][j] = top[j][i] = e[i][j] + acc
    neg = [[-v for v in row] for row in x]
    out = [top[i] + neg[i] for i in range(h)]
    out += [[neg[k][i] for k in range(h)] + t[i] for i in range(h)]
    return out


def pivot_groups(count, v):
    shape = (8, LANES)
    sub = lax.broadcasted_iota(jnp.int32, shape, 0)
    lane = lax.broadcasted_iota(jnp.int32, shape, 1)
    v = list(v)
    for g in range(count):
        p = 8 * g
        x = v[g]
        turn = LANES - 8 * count if g == count - 1 else 0
        rows = [jnp.broadcast_to(x[i : i + 1, :], shape) for i in range(8)]
        cols = [jnp.broadcast_to(x[:, p + t : p + t + 1], shape) for t in range(8)]
        m = [[None] * 8 for _ in range(8)]
        for i in range(8):
            for j in range(i, 8):
                m[i][j] = m[j][i] = jnp.broadcast_to(cols[j][i : i + 1, :], shape)
        e = small_inverse(m)
        pivots = (lane >= p) & (lane < p + 8)
        r = [jnp.where(pivots, (lane == p + i).astype(F32), rows[i]) for i in range(8)]
        q = []
        for i in range(8):
            acc = e[i][0] * r[0]
            for j in range(1, 8):
                acc = acc + e[i][j] * r[j]
            q.append(acc)
        new = []
        for k in range(len(v)):
            y = v[k]
            if k == g:
                y = q[0]
                for t in range(1, 8):
                    y = jnp.where(sub == t, q[t], y)
            else:
                acc = jnp.broadcast_to(y[:, p : p + 1], shape) * q[0]
                for t in range(1, 8):
                    acc = acc + jnp.broadcast_to(y[:, p + t : p + t + 1], shape) * q[t]
                y = jnp.where(pivots, 0.0, y) - acc
            new.append(pltpu.roll(y, turn, 1) if turn else y)
        v = new
    return tuple(v[count:] + v[:count])


RUN = 4


class Spread:
    def __init__(self, nb, r, b, all_ref, sems):
        self.nb, self.tiles, self.nx = nb, nb // 2, nb // RUN
        self.r, self.b, self.x, self.z = r, b, lax.div(b, RUN), lax.rem(b, RUN)
        self.all_ref = all_ref
        self.send1, self.recv1, self.send2, self.recv2, self.send3, self.recv3 = sems

    def slot(self, j, brick, count):
        start = pl.multiple_of(brick * COARSE, COARSE)
        return self.all_ref.at[j, pl.ds(start, count * COARSE), :]

    def remote(self, part, send_sem, recv_sem, x, z):
        return pltpu.make_async_remote_copy(
            src_ref=part, dst_ref=part, send_sem=send_sem, recv_sem=recv_sem,
            device_id=(self.r, x * RUN + z), device_id_type=MESH,
        )

    def arrived(self, j, brick, count, sem):
        part = self.slot(j, brick, count)
        pltpu.make_async_copy(part, part, sem).wait()

    def either(self, j, odd, even):
        if isinstance(j, int):
            (odd if j % 2 else even)()
        else:
            pl.when(lax.rem(j, 2) == 1)(odd)
            pl.when(lax.rem(j, 2) == 0)(even)

    def each1(self, j, act):
        part = self.slot(j, self.b, 1)

        def odd():
            for t in range(1, RUN):
                z = lax.rem(self.z + t, RUN)
                act(self.remote(part, self.send1.at[j, t], self.recv1.at[j, self.z], self.x, z))

        def even():
            for t in range(1, self.nx):
                x = lax.rem(self.x + t, self.nx)
                act(self.remote(part, self.send1.at[j, t], self.recv1.at[j, self.x], x, self.z))

        @pl.when(lax.div(self.b, 2) <= j)
        def _():
            self.either(j, odd, even)

    def each2(self, j, act, wait):
        def odd():
            for z in range(RUN):

                @pl.when((self.z != z) & (2 * self.x + z // 2 <= j))
                def _():
                    if wait:
                        self.arrived(j, self.x * RUN + z, 1, self.recv1.at[j, z])

            for count, when in ((RUN, 2 * self.x + 1 <= j), (2, 2 * self.x == j)):

                @pl.when(when)
                def _():
                    part = self.slot(j, self.x * RUN, count)
                    for t in range(1, self.nx):
                        x = lax.rem(self.x + t, self.nx)
                        act(self.remote(part, self.send2.at[j, t], self.recv2.at[j, self.x], x, self.z))

        def even():
            h = j // 2 if isinstance(j, int) else lax.div(j, 2)
            for x in range(self.nx):

                @pl.when(2 * x + lax.div(self.z, 2) <= j)
                def _():
                    brick = x * RUN + self.z
                    if wait:

                        @pl.when(self.x != x)
                        def _():
                            self.arrived(j, brick, 1, self.recv1.at[j, x])

                    for t in range(1, RUN):
                        z = lax.rem(self.z + t, RUN)
                        part = self.slot(j, brick, 1)
                        act(self.remote(part, self.send3.at[h, x, t], self.recv3.at[h, x, self.z], self.x, z))

        self.either(j, odd, even)

    def first(self, j):
        self.each1(j, lambda copy: copy.start())

    def second(self, j):
        self.each2(j, lambda copy: copy.start(), True)

    def need(self, j):
        def odd():
            for x in range(self.nx):
                for count, when in ((RUN, 2 * x + 1 <= j), (2, 2 * x == j)):

                    @pl.when((self.x != x) & when)
                    def _():
                        self.arrived(j, x * RUN, count, self.recv2.at[j, x])

        def even():
            h = j // 2 if isinstance(j, int) else lax.div(j, 2)
            for x in range(self.nx):
                for z in range(RUN):

                    @pl.when((self.z != z) & (2 * x + z // 2 <= j))
                    def _():
                        self.arrived(j, x * RUN + z, 1, self.recv3.at[h, x, z])

        self.either(j, odd, even)

    def finish(self):
        for j in range(self.tiles):
            self.each1(j, lambda copy: copy.wait_send())
            self.each2(j, lambda copy: copy.wait_send(), False)


def factor(nb, b, spread, all_ref, inverse_ref, u_ref, r_ref, l_ref, y_ref, z_ref, p_ref, d_ref):
    tiles = nb // 2
    sub = lax.broadcasted_iota(jnp.int32, (COARSE, W), 0)
    lane = lax.broadcasted_iota(jnp.int32, (COARSE, W), 1)
    half = tiles // 2
    unroll = 2
    turns = W // 8 // unroll

    def tile(k):
        return pl.ds(pl.multiple_of(k * W, W), W)

    def plain(it, v):
        return pivot_groups(unroll, v)

    def with_product(j, depth):
        def run(i, v):
            u = all_ref[j, tile(i), :] - dot(l_ref[i, :, :depth], u_ref[j, :depth, :], MID)
            before = jnp.maximum(i - 1, 0)
            scaled = dot(p_ref[before], u_ref[j, tile(before), :], MID)
            u_ref[j, tile(i), :] = u
            r_ref[j, tile(before), :] = scaled
            l_ref[j, :, tile(before)] = scaled.T
            return pivot_groups(unroll, v)

        return run

    def step(k, far, column):
        depth = (tiles - 1 if far else half) * W
        v = tuple(d_ref[8 * i : 8 * i + 8, :] for i in range(W // 8))
        if column:
            j = k + 1

            @pl.when(k + 5 < tiles)
            def _():
                spread.first(k + 5)

            @pl.when(k + 3 < tiles)
            def _():
                spread.second(k + 3)

            v = lax.fori_loop(0, turns - j, plain, v)
            spread.need(j)
            v = lax.fori_loop(0, half if far else j, with_product(j, (half - 1) * W), v)
            if far:
                v = lax.fori_loop(half, j, with_product(j, (tiles - 2) * W), v)
        else:
            v = lax.fori_loop(0, turns, plain, v)
        inverse = jnp.concatenate(v, axis=0)
        p_ref[k] = inverse
        if column:
            scaled = dot(inverse, u_ref[j, tile(k), :])
            r_ref[j, tile(k), :] = scaled
            l_ref[j, :, tile(k)] = scaled.T
            d_ref[...] = all_ref[j, tile(j), :] - dot(l_ref[j, :, :depth], u_ref[j, :depth, :])
        own = (lane + k * W == sub + b * COARSE).astype(F32)
        own = own - dot(y_ref[:, :depth], r_ref[k, :depth, :], MID)
        y_ref[:, tile(k)] = own
        z_ref[k] = dot(own, inverse, MID)

    def near_step(k, carry):
        step(k, False, True)
        return carry

    def far_step(k, carry):
        step(k, True, True)
        return carry

    spread.need(0)
    d_ref[...] = all_ref[0, :W, :]
    lax.fori_loop(0, half, near_step, 0)
    lax.fori_loop(half, tiles - 1, far_step, 0)
    step(tiles - 1, True, False)
    solved = [None] * tiles
    low = lane < COARSE
    for k in reversed(range(tiles)):
        acc = z_ref[k]
        for j in range(k + 1, tiles):
            acc = acc - dot(solved[j], l_ref[j, :, k * W : k * W + W], MID)
        solved[k] = acc
        inverse_ref[2 * k] = jnp.where(low, acc, 0.0)
        inverse_ref[2 * k + 1] = jnp.where(low, pltpu.roll(acc, COARSE, 1), 0.0)


def whole_kernel(
    nr, nb, pattern_in, matrix_in, load_in, stiffness_in, local_in, intact_in, lists_in, basis_in,
    out_ref, pattern_ref, matrix_ref, load_ref, stiffness_ref, local_ref, intact_ref, lists_ref, basis_ref, in_sem, all_ref, inverse_ref, u_ref, r_ref, l_ref, y_ref, zf_ref, p_ref, d_ref,
    k_ref, m_ref, c_ref, ct_ref, sel_ref, selt_ref, col_ref, z_ref, w_ref, acc_ref,
    msg_ref, gather_ref, tot_ref, total_ref, face_ref, near_ref, send1, recv1, send2, recv2, send3, recv3,
    gather_send, gather_recv, total_send, total_recv, face_send, face_recv,
):
    r, b = lax.axis_index("rows"), lax.axis_index("bricks")
    tiles = nb // 2
    incoming = [
        pltpu.make_async_copy(src, dst, in_sem.at[i])
        for i, (src, dst) in enumerate(
            (
                (pattern_in, pattern_ref), (matrix_in, matrix_ref), (load_in, load_ref), (basis_in, basis_ref),
                (lists_in, lists_ref), (intact_in, intact_ref), (local_in, local_ref), (stiffness_in, stiffness_ref),
            )
        )
    ]
    for copy in incoming:
        copy.start()
    barrier = pltpu.get_barrier_semaphore()
    for t in range(1, nb):
        pl.semaphore_signal(
            barrier, inc=1, device_id=(r, lax.rem(b + t, nb)), device_id_type=MESH
        )
    for t in range(1, nr):
        pl.semaphore_signal(
            barrier, inc=1, device_id=(lax.rem(r + t, nr), b), device_id_type=MESH
        )
    mine = pl.ds(pl.multiple_of(b * COARSE, COARSE), COARSE)
    incoming[0].wait()
    incoming[1].wait()
    for j in range(tiles):
        left = matrix_ref[2 * j] * pattern_ref[0, 2 * j].astype(F32)
        right = matrix_ref[2 * j + 1] * pattern_ref[0, 2 * j + 1].astype(F32)
        all_ref[j, mine, :] = jnp.concatenate([left, right], axis=1)
    spread = Spread(nb, r, b, all_ref, (send1, recv1, send2, recv2, send3, recv3))
    pl.semaphore_wait(barrier, nb + nr - 2)
    for j in range(3):
        spread.first(j)
    for copy in incoming[2:]:
        copy.wait()
    lane8 = lax.broadcasted_iota(jnp.int32, (8, LANES), 1)
    lane1 = lax.broadcasted_iota(jnp.int32, (1, LANES), 1)
    gap = jnp.zeros((NDOF, LANES - NODES), F32)
    for e in range(6):
        span = slice(e * NODES, e * NODES + NODES)
        piece = jnp.concatenate([basis_ref[:, span], gap[:COARSE]], axis=1)
        c_ref[e] = piece
        turned = jnp.concatenate([piece, jnp.zeros((LANES - COARSE, LANES), F32)], axis=0).T
        ct_ref[span, :] = turned[:NODES]
    node_col = lax.broadcasted_iota(jnp.int32, (LANES, LANES), 0)
    node_row = lax.broadcasted_iota(jnp.int32, (LANES, LANES), 1)
    slots = jnp.full((1, LANES), -1, jnp.int32)
    swapped = slots
    for d in range(4):
        line = jnp.concatenate([lists_ref[d : d + 1, :], jnp.zeros((1, LANES - FACE), jnp.int32)], axis=1)
        for other in (False, True):
            at = 32 * (d ^ other)
            moved = pltpu.roll(line, at, 1) if at else line
            here = (lane1 >= at) & (lane1 < at + FACE)
            if other:
                swapped = jnp.where(here, moved, swapped)
            else:
                slots = jnp.where(here, moved, slots)
    sel_ref[:, :LANES] = (node_col == slots).astype(F32)
    sel_ref[:, LANES:] = (node_col == swapped).astype(F32)
    selt_ref[...] = sel_ref[:NODES, :LANES]
    eye = (node_col == node_row)[:NODES]

    def row_to_col(row, ref):
        for c in range(6):
            spread = jnp.where(eye, jnp.broadcast_to(row[c : c + 1, :], (NODES, LANES)), 0.0)
            ref[c * NODES : c * NODES + NODES, :] = jnp.broadcast_to(
                jnp.sum(spread, axis=1, keepdims=True), (NODES, LANES)
            )

    def stack(rows):
        return jnp.concatenate(rows + [jnp.zeros((8 - len(rows), LANES), F32)], axis=0)

    def col_to_row(ref):
        return stack(
            [
                jnp.sum(jnp.where(eye, ref[c * NODES : c * NODES + NODES, :], 0.0), axis=0, keepdims=True)
                for c in range(6)
            ]
        )

    def row_partners(t):
        return (r, lax.rem(b + t, nb))

    def col_partners(t):
        return (lax.rem(r + t, nr), b)

    def exchange(count, partners, msg, land, send_sem, recv_sem):
        for t in range(1, count):
            pltpu.make_async_remote_copy(
                src_ref=msg, dst_ref=land, send_sem=send_sem, recv_sem=recv_sem,
                device_id=partners(t), device_id_type=MESH,
            ).start()

    def wait_bytes(ref, sem):
        pltpu.make_async_copy(ref, ref, sem).wait()

    def gather_start(n, message):
        msg_ref[n] = message
        gather_ref[n, b] = message
        exchange(
            nb, row_partners, msg_ref.at[n], gather_ref.at[n, b], gather_send.at[n], gather_recv.at[n]
        )

    def gather_wait(n):
        wait_bytes(gather_ref.at[n, pl.ds(0, nb - 1)], gather_recv.at[n])

    def total_start(n):
        acc = gather_ref[n, 0]
        for j in range(1, nb):
            acc = acc + gather_ref[n, j]
        tot_ref[n] = acc
        total_ref[n, r] = acc
        exchange(
            nr, col_partners, tot_ref.at[n], total_ref.at[n, r], total_send.at[n], total_recv.at[n]
        )

    def total_wait(n):
        wait_bytes(total_ref.at[n, pl.ds(0, nr - 1)], total_recv.at[n])
        acc = total_ref[n, 0]
        for j in range(1, nr):
            acc = acc + total_ref[n, j]
        first = jnp.sum(jnp.where(lane1 == COARSE, acc, 0.0), axis=1, keepdims=True)
        second = jnp.sum(jnp.where(lane1 == COARSE + 1, acc, 0.0), axis=1, keepdims=True)
        return first, second

    def reduced(ref):
        return jnp.sum(ref[...] * ct_ref[...], axis=0, keepdims=True)

    def with_dots(message, first, second):
        one = jnp.sum(jnp.sum(first, axis=0, keepdims=True), axis=1, keepdims=True)
        two = jnp.sum(jnp.sum(second, axis=0, keepdims=True), axis=1, keepdims=True)
        message = jnp.where(lane1 == COARSE, one, message)
        return jnp.where(lane1 == COARSE + 1, two, message)

    def local_part(ref):
        return [jnp.sum(ref[...] * m_ref[e], axis=0, keepdims=True) for e in range(6)]

    def coarse_part(n):
        acc = inverse_ref[0] * gather_ref[n, 0]
        for j in range(1, nb):
            acc = acc + inverse_ref[j] * gather_ref[n, j]
        solved = jnp.sum(acc, axis=1, keepdims=True)
        return [jnp.sum(solved * c_ref[e], axis=0, keepdims=True) for e in range(6)]

    neighbours = [
        (lax.rem(r + nr - 1, nr), b, r > 0),
        (lax.rem(r + 1, nr), b, r < nr - 1),
        (r, lax.rem(b + nb - 1, nb), b > 0),
        (r, lax.rem(b + 1, nb), b < nb - 1),
    ]

    def face_start(n, row):
        both = dot(row, sel_ref[...])
        face_ref[n] = both[:, LANES:]
        for d in range(4):
            pltpu.make_async_remote_copy(
                src_ref=face_ref.at[n], dst_ref=near_ref.at[n, d ^ 1],
                send_sem=face_send.at[n, d], recv_sem=face_recv.at[n, d ^ 1],
                device_id=neighbours[d][:2], device_id_type=MESH,
            ).start()
        return both[:, :LANES]

    def operate(n, row, face, target):
        for c in range(6):
            rows = slice(c * NODES, c * NODES + NODES)
            acc = k_ref[0, rows, :] * row[0:1, :]
            for e in range(1, 6):
                acc = acc + k_ref[e, rows, :] * row[e : e + 1, :]
            acc_ref[rows, :] = acc
        stretch = face
        for d in range(4):
            wait_bytes(near_ref.at[n, d], face_recv.at[n, d])
            here = (lane8 >= 32 * d) & (lane8 < 32 * d + 32) & neighbours[d][2]
            stretch = stretch - jnp.where(here, near_ref[n, d], 0.0)
        for c in range(6):
            rows = slice(c * NODES, c * NODES + NODES)
            acc = acc_ref[rows, :] + selt_ref[...] * stretch[c : c + 1, :]
            target[rows, :] = jnp.broadcast_to(
                jnp.sum(acc, axis=1, keepdims=True), (NODES, LANES)
            )

    load = stack([jnp.concatenate([load_ref[:, c * NODES : c * NODES + NODES], gap[:1]], axis=1) for c in range(6)])
    row_to_col(load, col_ref)
    res = load
    gather_start(0, reduced(col_ref))
    for j in range(2):
        spread.second(j)
    spread.first(3)
    for ref in (u_ref, r_ref, l_ref, p_ref):
        for j in range(tiles):
            ref[j] = jnp.zeros(ref.shape[1:], F32)
    y_ref[...] = jnp.zeros(y_ref.shape, F32)
    spread.second(2)
    if tiles > 4:
        spread.first(4)
    for e in range(6):
        span = slice(e * NODES, e * NODES + NODES)
        m_ref[e] = jnp.concatenate([local_ref[:, span], gap], axis=1)
    part = stack(local_part(col_ref))

    factor(nb, b, spread, all_ref, inverse_ref, u_ref, r_ref, l_ref, y_ref, zf_ref, p_ref, d_ref)

    gather_wait(0)
    u = part + stack(coarse_part(0))
    face = face_start(0, u)
    intact = jnp.concatenate([intact_ref[...].astype(F32), gap[:NODES]], axis=1)
    for e in range(6):
        wide = jnp.concatenate([stiffness_ref[:, e * NODES : e * NODES + NODES], gap], axis=1)
        for c in range(6):
            rows = slice(c * NODES, c * NODES + NODES)
            k_ref[e, rows, :] = wide[rows] * intact
    operate(0, u, face, w_ref)
    w = col_to_row(w_ref)
    p = s = q = sol = None
    dot_old = step_old = None
    for i in range(2):
        gather_start(i + 1, with_dots(reduced(w_ref), res * u, w * u))
        if i == 0:
            spread.finish()
        part = local_part(w_ref)
        gather_wait(i + 1)
        total_start(i + 1)
        m = stack([x + y for x, y in zip(part, coarse_part(i + 1))])
        face = face_start(i + 1, m)
        operate(i + 1, m, face, col_ref)
        v = col_to_row(col_ref)
        gamma, delta = total_wait(i + 1)
        if i == 0:
            step_size = gamma / delta
            p, s, q, zr = u, w, m, v
            z_ref[...] = col_ref[...]
            sol = step_size * p
        else:
            ratio = gamma / dot_old
            step_size = gamma / (delta - ratio * gamma / step_old)
            p, s, q, zr = u + ratio * p, w + ratio * s, m + ratio * q, v + ratio * zr
            sol = sol + step_size * p
        res = res - step_size * s
        u = u - step_size * q
        w = w - step_size * zr
        if i == 0:
            w_ref[...] = w_ref[...] - step_size * z_ref[...]
        dot_old, step_old = gamma, step_size
    gather_start(3, with_dots(jnp.zeros((1, LANES), F32), res * u, w * u))
    gather_wait(3)
    total_start(3)
    for n in range(4):
        wait_bytes(gather_ref.at[n, pl.ds(0, nb - 1)], gather_send.at[n])
    for n in range(1, 3):
        wait_bytes(total_ref.at[n, pl.ds(0, nr - 1)], total_send.at[n])
    for n in range(3):
        for d in range(4):
            wait_bytes(face_ref.at[n], face_send.at[n, d])
    gamma, delta = total_wait(3)
    ratio = gamma / dot_old
    step_size = gamma / (delta - ratio * gamma / step_old)
    out_ref[0] = sol + step_size * (u + ratio * p)
    out_ref[1] = res - step_size * (w + ratio * s)

    wait_bytes(total_ref.at[3, pl.ds(0, nr - 1)], total_send.at[3])


VMEM = pl.BlockSpec(memory_space=pltpu.VMEM)
ANY = pl.BlockSpec(memory_space=pltpu.HBM)


def body(nr, nb, load, stiffness, local_inverse, intact, face_lists, coarse_basis, matrix, pattern):
    tiles = nb // 2
    order = nb * COARSE
    limit = 62 * 1024 * 1024
    out = pl.pallas_call(
        functools.partial(whole_kernel, nr, nb),
        out_shape=jax.ShapeDtypeStruct((2, 8, LANES), F32),
        in_specs=[ANY] * 8,
        out_specs=VMEM,
        scratch_shapes=[
            pltpu.SMEM((1, nb), jnp.int32),
            pltpu.VMEM((nb, COARSE, COARSE), F32),
            pltpu.VMEM((1, NDOF), F32),
            pltpu.VMEM((NDOF, NDOF), F32),
            pltpu.VMEM((NDOF, NDOF), F32),
            pltpu.VMEM((NODES, NODES), jnp.int32),
            pltpu.VMEM((4, FACE), jnp.int32),
            pltpu.VMEM((COARSE, NDOF), F32),
            pltpu.SemaphoreType.DMA((8,)),
            pltpu.VMEM((tiles, order, LANES), F32),
            pltpu.VMEM((nb, COARSE, LANES), F32),
            pltpu.VMEM((tiles, order, LANES), F32),
            pltpu.VMEM((tiles, order, LANES), F32),
            pltpu.VMEM((tiles, W, order), F32),
            pltpu.VMEM((COARSE, order), F32),
            pltpu.VMEM((tiles, COARSE, W), F32),
            pltpu.VMEM((tiles, W, W), F32),
            pltpu.VMEM((W, W), F32),
            pltpu.VMEM((6, NDOF, LANES), F32),
            pltpu.VMEM((6, NDOF, LANES), F32),
            pltpu.VMEM((6, COARSE, LANES), F32),
            pltpu.VMEM((NDOF, LANES), F32),
            pltpu.VMEM((LANES, 2 * LANES), F32),
            pltpu.VMEM((NODES, LANES), F32),
            pltpu.VMEM((NDOF, LANES), F32),
            pltpu.VMEM((NDOF, LANES), F32),
            pltpu.VMEM((NDOF, LANES), F32),
            pltpu.VMEM((NDOF, LANES), F32),
            pltpu.VMEM((4, 1, LANES), F32),
            pltpu.VMEM((4, nb, 1, LANES), F32),
            pltpu.VMEM((4, 1, LANES), F32),
            pltpu.VMEM((4, nr, 1, LANES), F32),
            pltpu.VMEM((3, 8, LANES), F32),
            pltpu.VMEM((3, 4, 8, LANES), F32),
            pltpu.SemaphoreType.DMA((tiles, RUN)),
            pltpu.SemaphoreType.DMA((tiles, RUN)),
            pltpu.SemaphoreType.DMA((tiles, nb // RUN)),
            pltpu.SemaphoreType.DMA((tiles, nb // RUN)),
            pltpu.SemaphoreType.DMA((tiles // 2, nb // RUN, RUN)),
            pltpu.SemaphoreType.DMA((tiles // 2, nb // RUN, RUN)),
            pltpu.SemaphoreType.DMA((4,)),
            pltpu.SemaphoreType.DMA((4,)),
            pltpu.SemaphoreType.DMA((4,)),
            pltpu.SemaphoreType.DMA((4,)),
            pltpu.SemaphoreType.DMA((3, 4)),
            pltpu.SemaphoreType.DMA((3, 4)),
        ],
        compiler_params=pltpu.CompilerParams(
            collective_id=0, has_side_effects=True, vmem_limit_bytes=limit
        ),
        name="whole",
    )(
        pattern.reshape(1, nb),
        matrix.reshape(nb, COARSE, COARSE),
        load.reshape(1, NDOF),
        stiffness.reshape(NDOF, NDOF),
        local_inverse.reshape(NDOF, NDOF),
        intact.reshape(NODES, NODES),
        face_lists.reshape(4, FACE),
        coarse_basis.reshape(COARSE, NDOF),
    )
    flat = out[:, :6, :NODES].reshape(2, 1, 1, NDOF)
    return flat[0], flat[1]


def solution(mesh):
    in_specs = (
        P("rows", "bricks", None),
        P("rows", "bricks", None, None),
        P("rows", "bricks", None, None),
        P("rows", "bricks", None, None),
        P("rows", "bricks", None, None),
        P("rows", "bricks", None, None),
        P("rows", "bricks", None, None, None),
        P("rows", "bricks", None),
    )
    out_specs = (P("rows", "bricks", None), P("rows", "bricks", None))
    run = functools.partial(body, mesh.shape["rows"], mesh.shape["bricks"])
    return jax.shard_map(run, mesh=mesh, in_specs=in_specs, out_specs=out_specs, check_vma=False)
```

```python
import functools

import jax
import jax.numpy as jnp
from jax import lax
from jax.experimental import pallas as pl
from jax.experimental.pallas import tpu as pltpu
from jax.sharding import PartitionSpec as P

MESH = pl.DeviceIdType.MESH
HI = lax.Precision.HIGHEST
MID = lax.Precision.HIGH
F32 = jnp.float32
NODES, NDOF, COARSE, FACE, W = 96, 576, 64, 24, 128
LANES = 128


def dot(a, b, precision=HI):
    return lax.dot_general(
        a, b, (((1,), (0,)), ((), ())), precision=precision, preferred_element_type=F32
    )


def small_product(a, b):
    out = []
    for row in a:
        line = []
        for j in range(len(b[0])):
            acc = row[0] * b[0][j]
            for k in range(1, len(b)):
                acc = acc + row[k] * b[k][j]
            line.append(acc)
        out.append(line)
    return out


def small_inverse(m):
    n = len(m)
    if n == 2:
        a, b, d = m[0][0], m[0][1], m[1][1]
        r = 1.0 / (a * d - b * b)
        off = -(b * r)
        return [[d * r, off], [off, a * r]]
    h = n // 2
    b = [row[h:] for row in m[:h]]
    e = small_inverse([row[:h] for row in m[:h]])
    w = small_product(e, b)
    s = [[None] * h for _ in range(h)]
    for i in range(h):
        for j in range(i, h):
            acc = b[0][i] * w[0][j]
            for k in range(1, h):
                acc = acc + b[k][i] * w[k][j]
            s[i][j] = s[j][i] = m[h + i][h + j] - acc
    t = small_inverse(s)
    x = small_product(w, t)
    top = [[None] * h for _ in range(h)]
    for i in range(h):
        for j in range(i, h):
            acc = x[i][0] * w[j][0]
            for k in range(1, h):
                acc = acc + x[i][k] * w[j][k]
            top[i][j] = top[j][i] = e[i][j] + acc
    neg = [[-v for v in row] for row in x]
    out = [top[i] + neg[i] for i in range(h)]
    out += [[neg[k][i] for k in range(h)] + t[i] for i in range(h)]
    return out


def pivot_groups(count, v):
    shape = (8, LANES)
    sub = lax.broadcasted_iota(jnp.int32, shape, 0)
    lane = lax.broadcasted_iota(jnp.int32, shape, 1)
    v = list(v)
    for g in range(count):
        p = 8 * g
        x = v[g]
        turn = LANES - 8 * count if g == count - 1 else 0
        rows = [jnp.broadcast_to(x[i : i + 1, :], shape) for i in range(8)]
        cols = [jnp.broadcast_to(x[:, p + t : p + t + 1], shape) for t in range(8)]
        m = [[None] * 8 for _ in range(8)]
        for i in range(8):
            for j in range(i, 8):
                m[i][j] = m[j][i] = jnp.broadcast_to(cols[j][i : i + 1, :], shape)
        e = small_inverse(m)
        pivots = (lane >= p) & (lane < p + 8)
        r = [jnp.where(pivots, (lane == p + i).astype(F32), rows[i]) for i in range(8)]
        q = []
        for i in range(8):
            acc = e[i][0] * r[0]
            for j in range(1, 8):
                acc = acc + e[i][j] * r[j]
            q.append(acc)
        new = []
        for k in range(len(v)):
            y = v[k]
            if k == g:
                y = q[0]
                for t in range(1, 8):
                    y = jnp.where(sub == t, q[t], y)
            else:
                acc = jnp.broadcast_to(y[:, p : p + 1], shape) * q[0]
                for t in range(1, 8):
                    acc = acc + jnp.broadcast_to(y[:, p + t : p + t + 1], shape) * q[t]
                y = jnp.where(pivots, 0.0, y) - acc
            new.append(pltpu.roll(y, turn, 1) if turn else y)
        v = new
    return tuple(v[count:] + v[:count])


RUN = 4


class Spread:
    def __init__(self, nb, r, b, all_ref, sems):
        self.nb, self.tiles, self.nx = nb, nb // 2, nb // RUN
        self.r, self.b, self.x, self.z = r, b, lax.div(b, RUN), lax.rem(b, RUN)
        self.all_ref = all_ref
        self.send1, self.recv1, self.send2, self.recv2, self.send3, self.recv3 = sems

    def slot(self, j, brick, count):
        start = pl.multiple_of(brick * COARSE, COARSE)
        return self.all_ref.at[j, pl.ds(start, count * COARSE), :]

    def remote(self, part, send_sem, recv_sem, x, z):
        return pltpu.make_async_remote_copy(
            src_ref=part, dst_ref=part, send_sem=send_sem, recv_sem=recv_sem,
            device_id=(self.r, x * RUN + z), device_id_type=MESH,
        )

    def arrived(self, j, brick, count, sem):
        part = self.slot(j, brick, count)
        pltpu.make_async_copy(part, part, sem).wait()

    def either(self, j, odd, even):
        if isinstance(j, int):
            (odd if j % 2 else even)()
        else:
            pl.when(lax.rem(j, 2) == 1)(odd)
            pl.when(lax.rem(j, 2) == 0)(even)

    def each1(self, j, act):
        part = self.slot(j, self.b, 1)

        def odd():
            for t in range(1, RUN):
                z = lax.rem(self.z + t, RUN)
                act(self.remote(part, self.send1.at[j, t], self.recv1.at[j, self.z], self.x, z))

        def even():
            for t in range(1, self.nx):
                x = lax.rem(self.x + t, self.nx)
                act(self.remote(part, self.send1.at[j, t], self.recv1.at[j, self.x], x, self.z))

        @pl.when(lax.div(self.b, 2) <= j)
        def _():
            self.either(j, odd, even)

    def each2(self, j, act, wait):
        def odd():
            for z in range(RUN):

                @pl.when((self.z != z) & (2 * self.x + z // 2 <= j))
                def _():
                    if wait:
                        self.arrived(j, self.x * RUN + z, 1, self.recv1.at[j, z])

            for count, when in ((RUN, 2 * self.x + 1 <= j), (2, 2 * self.x == j)):

                @pl.when(when)
                def _():
                    part = self.slot(j, self.x * RUN, count)
                    for t in range(1, self.nx):
                        x = lax.rem(self.x + t, self.nx)
                        act(self.remote(part, self.send2.at[j, t], self.recv2.at[j, self.x], x, self.z))

        def even():
            h = j // 2 if isinstance(j, int) else lax.div(j, 2)
            for x in range(self.nx):

                @pl.when(2 * x + lax.div(self.z, 2) <= j)
                def _():
                    brick = x * RUN + self.z
                    if wait:

                        @pl.when(self.x != x)
                        def _():
                            self.arrived(j, brick, 1, self.recv1.at[j, x])

                    for t in range(1, RUN):
                        z = lax.rem(self.z + t, RUN)
                        part = self.slot(j, brick, 1)
                        act(self.remote(part, self.send3.at[h, x, t], self.recv3.at[h, x, self.z], self.x, z))

        self.either(j, odd, even)

    def first(self, j):
        self.each1(j, lambda copy: copy.start())

    def second(self, j):
        self.each2(j, lambda copy: copy.start(), True)

    def need(self, j):
        def odd():
            for x in range(self.nx):
                for count, when in ((RUN, 2 * x + 1 <= j), (2, 2 * x == j)):

                    @pl.when((self.x != x) & when)
                    def _():
                        self.arrived(j, x * RUN, count, self.recv2.at[j, x])

        def even():
            h = j // 2 if isinstance(j, int) else lax.div(j, 2)
            for x in range(self.nx):
                for z in range(RUN):

                    @pl.when((self.z != z) & (2 * x + z // 2 <= j))
                    def _():
                        self.arrived(j, x * RUN + z, 1, self.recv3.at[h, x, z])

        self.either(j, odd, even)

    def finish(self):
        for j in range(self.tiles):
            self.each1(j, lambda copy: copy.wait_send())
            self.each2(j, lambda copy: copy.wait_send(), False)


def factor(nb, b, spread, all_ref, inverse_ref, u_ref, r_ref, l_ref, y_ref, z_ref, p_ref, d_ref):
    tiles = nb // 2
    sub = lax.broadcasted_iota(jnp.int32, (COARSE, W), 0)
    lane = lax.broadcasted_iota(jnp.int32, (COARSE, W), 1)
    half = tiles // 2
    unroll = 2
    turns = W // 8 // unroll

    def tile(k):
        return pl.ds(pl.multiple_of(k * W, W), W)

    def plain(it, v):
        return pivot_groups(unroll, v)

    def with_product(j, depth):
        def run(i, v):
            u = all_ref[j, tile(i), :] - dot(l_ref[i, :, :depth], u_ref[j, :depth, :], MID)
            before = jnp.maximum(i - 1, 0)
            scaled = dot(p_ref[before], u_ref[j, tile(before), :], MID)
            u_ref[j, tile(i), :] = u
            r_ref[j, tile(before), :] = scaled
            l_ref[j, :, tile(before)] = scaled.T
            return pivot_groups(unroll, v)

        return run

    def step(k, far, column):
        depth = (tiles - 1 if far else half) * W
        v = tuple(d_ref[8 * i : 8 * i + 8, :] for i in range(W // 8))
        if column:
            j = k + 1

            @pl.when(k + 6 < tiles)
            def _():
                spread.first(k + 6)

            @pl.when(k + 4 < tiles)
            def _():
                spread.second(k + 4)

            v = lax.fori_loop(0, turns - j, plain, v)
            spread.need(j)
            v = lax.fori_loop(0, half if far else j, with_product(j, (half - 1) * W), v)
            if far:
                v = lax.fori_loop(half, j, with_product(j, (tiles - 2) * W), v)
        else:
            v = lax.fori_loop(0, turns, plain, v)
        inverse = jnp.concatenate(v, axis=0)
        p_ref[k] = inverse
        if column:
            scaled = dot(inverse, u_ref[j, tile(k), :])
            r_ref[j, tile(k), :] = scaled
            l_ref[j, :, tile(k)] = scaled.T
            d_ref[...] = all_ref[j, tile(j), :] - dot(l_ref[j, :, :depth], u_ref[j, :depth, :])
        own = (lane + k * W == sub + b * COARSE).astype(F32)
        own = own - dot(y_ref[:, :depth], r_ref[k, :depth, :], MID)
        y_ref[:, tile(k)] = own
        z_ref[k] = dot(own, inverse, MID)

    def near_step(k, carry):
        step(k, False, True)
        return carry

    def far_step(k, carry):
        step(k, True, True)
        return carry

    spread.need(0)
    d_ref[...] = all_ref[0, :W, :]
    lax.fori_loop(0, half, near_step, 0)
    lax.fori_loop(half, tiles - 1, far_step, 0)
    step(tiles - 1, True, False)
    solved = [None] * tiles
    low = lane < COARSE
    for k in reversed(range(tiles)):
        acc = z_ref[k]
        for j in range(k + 1, tiles):
            acc = acc - dot(solved[j], l_ref[j, :, k * W : k * W + W], MID)
        solved[k] = acc
        inverse_ref[2 * k] = jnp.where(low, acc, 0.0)
        inverse_ref[2 * k + 1] = jnp.where(low, pltpu.roll(acc, COARSE, 1), 0.0)


def whole_kernel(
    nr, nb, pattern_in, matrix_in, load_in, stiffness_in, local_in, intact_in, lists_in, basis_in,
    out_ref, pattern_ref, matrix_ref, load_ref, stiffness_ref, local_ref, intact_ref, lists_ref, basis_ref, in_sem, all_ref, inverse_ref, u_ref, r_ref, l_ref, y_ref, zf_ref, p_ref, d_ref,
    k_ref, m_ref, c_ref, ct_ref, sel_ref, selt_ref, col_ref, z_ref, w_ref, acc_ref,
    msg_ref, gather_ref, tot_ref, total_ref, face_ref, near_ref, send1, recv1, send2, recv2, send3, recv3,
    gather_send, gather_recv, total_send, total_recv, face_send, face_recv,
):
    r, b = lax.axis_index("rows"), lax.axis_index("bricks")
    tiles = nb // 2
    incoming = [
        pltpu.make_async_copy(src, dst, in_sem.at[i])
        for i, (src, dst) in enumerate(
            (
                (pattern_in, pattern_ref), (matrix_in, matrix_ref), (load_in, load_ref), (basis_in, basis_ref),
                (lists_in, lists_ref), (intact_in, intact_ref), (local_in, local_ref), (stiffness_in, stiffness_ref),
            )
        )
    ]
    for copy in incoming:
        copy.start()
    barrier = pltpu.get_barrier_semaphore()
    for t in range(1, nb):
        pl.semaphore_signal(
            barrier, inc=1, device_id=(r, lax.rem(b + t, nb)), device_id_type=MESH
        )
    for t in range(1, nr):
        pl.semaphore_signal(
            barrier, inc=1, device_id=(lax.rem(r + t, nr), b), device_id_type=MESH
        )
    mine = pl.ds(pl.multiple_of(b * COARSE, COARSE), COARSE)
    incoming[0].wait()
    incoming[1].wait()
    for j in range(tiles):
        left = matrix_ref[2 * j] * pattern_ref[0, 2 * j].astype(F32)
        right = matrix_ref[2 * j + 1] * pattern_ref[0, 2 * j + 1].astype(F32)
        all_ref[j, mine, :] = jnp.concatenate([left, right], axis=1)
    spread = Spread(nb, r, b, all_ref, (send1, recv1, send2, recv2, send3, recv3))
    pl.semaphore_wait(barrier, nb + nr - 2)
    for j in range(3):
        spread.first(j)
    for copy in incoming[2:]:
        copy.wait()
    lane8 = lax.broadcasted_iota(jnp.int32, (8, LANES), 1)
    lane1 = lax.broadcasted_iota(jnp.int32, (1, LANES), 1)
    gap = jnp.zeros((NDOF, LANES - NODES), F32)
    for e in range(6):
        span = slice(e * NODES, e * NODES + NODES)
        piece = jnp.concatenate([basis_ref[:, span], gap[:COARSE]], axis=1)
        c_ref[e] = piece
        turned = jnp.concatenate([piece, jnp.zeros((LANES - COARSE, LANES), F32)], axis=0).T
        ct_ref[span, :] = turned[:NODES]
    node_col = lax.broadcasted_iota(jnp.int32, (LANES, LANES), 0)
    node_row = lax.broadcasted_iota(jnp.int32, (LANES, LANES), 1)
    slots = jnp.full((1, LANES), -1, jnp.int32)
    swapped = slots
    for d in range(4):
        line = jnp.concatenate([lists_ref[d : d + 1, :], jnp.zeros((1, LANES - FACE), jnp.int32)], axis=1)
        for other in (False, True):
            at = 32 * (d ^ other)
            moved = pltpu.roll(line, at, 1) if at else line
            here = (lane1 >= at) & (lane1 < at + FACE)
            if other:
                swapped = jnp.where(here, moved, swapped)
            else:
                slots = jnp.where(here, moved, slots)
    sel_ref[:, :LANES] = (node_col == slots).astype(F32)
    sel_ref[:, LANES:] = (node_col == swapped).astype(F32)
    selt_ref[...] = sel_ref[:NODES, :LANES]
    eye = (node_col == node_row)[:NODES]

    def row_to_col(row, ref):
        for c in range(6):
            spread = jnp.where(eye, jnp.broadcast_to(row[c : c + 1, :], (NODES, LANES)), 0.0)
            ref[c * NODES : c * NODES + NODES, :] = jnp.broadcast_to(
                jnp.sum(spread, axis=1, keepdims=True), (NODES, LANES)
            )

    def stack(rows):
        return jnp.concatenate(rows + [jnp.zeros((8 - len(rows), LANES), F32)], axis=0)

    def col_to_row(ref):
        return stack(
            [
                jnp.sum(jnp.where(eye, ref[c * NODES : c * NODES + NODES, :], 0.0), axis=0, keepdims=True)
                for c in range(6)
            ]
        )

    def row_partners(t):
        return (r, lax.rem(b + t, nb))

    def col_partners(t):
        return (lax.rem(r + t, nr), b)

    def exchange(count, partners, msg, land, send_sem, recv_sem):
        for t in range(1, count):
            pltpu.make_async_remote_copy(
                src_ref=msg, dst_ref=land, send_sem=send_sem, recv_sem=recv_sem,
                device_id=partners(t), device_id_type=MESH,
            ).start()

    def wait_bytes(ref, sem):
        pltpu.make_async_copy(ref, ref, sem).wait()

    def gather_start(n, message):
        msg_ref[n] = message
        gather_ref[n, b] = message
        exchange(
            nb, row_partners, msg_ref.at[n], gather_ref.at[n, b], gather_send.at[n], gather_recv.at[n]
        )

    def gather_wait(n):
        wait_bytes(gather_ref.at[n, pl.ds(0, nb - 1)], gather_recv.at[n])

    def total_start(n):
        acc = gather_ref[n, 0]
        for j in range(1, nb):
            acc = acc + gather_ref[n, j]
        tot_ref[n] = acc
        total_ref[n, r] = acc
        exchange(
            nr, col_partners, tot_ref.at[n], total_ref.at[n, r], total_send.at[n], total_recv.at[n]
        )

    def total_wait(n):
        wait_bytes(total_ref.at[n, pl.ds(0, nr - 1)], total_recv.at[n])
        acc = total_ref[n, 0]
        for j in range(1, nr):
            acc = acc + total_ref[n, j]
        first = jnp.sum(jnp.where(lane1 == COARSE, acc, 0.0), axis=1, keepdims=True)
        second = jnp.sum(jnp.where(lane1 == COARSE + 1, acc, 0.0), axis=1, keepdims=True)
        return first, second

    def reduced(ref):
        return jnp.sum(ref[...] * ct_ref[...], axis=0, keepdims=True)

    def with_dots(message, first, second):
        one = jnp.sum(jnp.sum(first, axis=0, keepdims=True), axis=1, keepdims=True)
        two = jnp.sum(jnp.sum(second, axis=0, keepdims=True), axis=1, keepdims=True)
        message = jnp.where(lane1 == COARSE, one, message)
        return jnp.where(lane1 == COARSE + 1, two, message)

    def local_part(ref):
        return [jnp.sum(ref[...] * m_ref[e], axis=0, keepdims=True) for e in range(6)]

    def coarse_part(n):
        acc = inverse_ref[0] * gather_ref[n, 0]
        for j in range(1, nb):
            acc = acc + inverse_ref[j] * gather_ref[n, j]
        solved = jnp.sum(acc, axis=1, keepdims=True)
        return [jnp.sum(solved * c_ref[e], axis=0, keepdims=True) for e in range(6)]

    neighbours = [
        (lax.rem(r + nr - 1, nr), b, r > 0),
        (lax.rem(r + 1, nr), b, r < nr - 1),
        (r, lax.rem(b + nb - 1, nb), b > 0),
        (r, lax.rem(b + 1, nb), b < nb - 1),
    ]

    def face_start(n, row):
        both = dot(row, sel_ref[...])
        face_ref[n] = both[:, LANES:]
        for d in range(4):
            pltpu.make_async_remote_copy(
                src_ref=face_ref.at[n], dst_ref=near_ref.at[n, d ^ 1],
                send_sem=face_send.at[n, d], recv_sem=face_recv.at[n, d ^ 1],
                device_id=neighbours[d][:2], device_id_type=MESH,
            ).start()
        return both[:, :LANES]

    def operate(n, row, face, target):
        for c in range(6):
            rows = slice(c * NODES, c * NODES + NODES)
            acc = k_ref[0, rows, :] * row[0:1, :]
            for e in range(1, 6):
                acc = acc + k_ref[e, rows, :] * row[e : e + 1, :]
            acc_ref[rows, :] = acc
        stretch = face
        for d in range(4):
            wait_bytes(near_ref.at[n, d], face_recv.at[n, d])
            here = (lane8 >= 32 * d) & (lane8 < 32 * d + 32) & neighbours[d][2]
            stretch = stretch - jnp.where(here, near_ref[n, d], 0.0)
        for c in range(6):
            rows = slice(c * NODES, c * NODES + NODES)
            acc = acc_ref[rows, :] + selt_ref[...] * stretch[c : c + 1, :]
            target[rows, :] = jnp.broadcast_to(
                jnp.sum(acc, axis=1, keepdims=True), (NODES, LANES)
            )

    load = stack([jnp.concatenate([load_ref[:, c * NODES : c * NODES + NODES], gap[:1]], axis=1) for c in range(6)])
    row_to_col(load, col_ref)
    res = load
    gather_start(0, reduced(col_ref))
    for j in range(2):
        spread.second(j)
    spread.first(3)
    for ref in (u_ref, r_ref, l_ref, p_ref):
        for j in range(tiles):
            ref[j] = jnp.zeros(ref.shape[1:], F32)
    y_ref[...] = jnp.zeros(y_ref.shape, F32)
    spread.second(2)
    if tiles > 4:
        spread.first(4)
    for e in range(6):
        span = slice(e * NODES, e * NODES + NODES)
        m_ref[e] = jnp.concatenate([local_ref[:, span], gap], axis=1)
    part = stack(local_part(col_ref))
    if tiles > 3:
        spread.second(3)
    if tiles > 5:
        spread.first(5)

    factor(nb, b, spread, all_ref, inverse_ref, u_ref, r_ref, l_ref, y_ref, zf_ref, p_ref, d_ref)

    gather_wait(0)
    u = part + stack(coarse_part(0))
    face = face_start(0, u)
    intact = jnp.concatenate([intact_ref[...].astype(F32), gap[:NODES]], axis=1)
    for e in range(6):
        wide = jnp.concatenate([stiffness_ref[:, e * NODES : e * NODES + NODES], gap], axis=1)
        for c in range(6):
            rows = slice(c * NODES, c * NODES + NODES)
            k_ref[e, rows, :] = wide[rows] * intact
    operate(0, u, face, w_ref)
    w = col_to_row(w_ref)
    p = s = q = sol = None
    dot_old = step_old = None
    for i in range(2):
        gather_start(i + 1, with_dots(reduced(w_ref), res * u, w * u))
        if i == 0:
            spread.finish()
        part = local_part(w_ref)
        gather_wait(i + 1)
        total_start(i + 1)
        m = stack([x + y for x, y in zip(part, coarse_part(i + 1))])
        face = face_start(i + 1, m)
        operate(i + 1, m, face, col_ref)
        v = col_to_row(col_ref)
        gamma, delta = total_wait(i + 1)
        if i == 0:
            step_size = gamma / delta
            p, s, q, zr = u, w, m, v
            z_ref[...] = col_ref[...]
            sol = step_size * p
        else:
            ratio = gamma / dot_old
            step_size = gamma / (delta - ratio * gamma / step_old)
            p, s, q, zr = u + ratio * p, w + ratio * s, m + ratio * q, v + ratio * zr
            sol = sol + step_size * p
        res = res - step_size * s
        u = u - step_size * q
        w = w - step_size * zr
        if i == 0:
            w_ref[...] = w_ref[...] - step_size * z_ref[...]
        dot_old, step_old = gamma, step_size
    gather_start(3, with_dots(jnp.zeros((1, LANES), F32), res * u, w * u))
    gather_wait(3)
    total_start(3)
    for n in range(4):
        wait_bytes(gather_ref.at[n, pl.ds(0, nb - 1)], gather_send.at[n])
    for n in range(1, 3):
        wait_bytes(total_ref.at[n, pl.ds(0, nr - 1)], total_send.at[n])
    for n in range(3):
        for d in range(4):
            wait_bytes(face_ref.at[n], face_send.at[n, d])
    gamma, delta = total_wait(3)
    ratio = gamma / dot_old
    step_size = gamma / (delta - ratio * gamma / step_old)
    out_ref[0] = sol + step_size * (u + ratio * p)
    out_ref[1] = res - step_size * (w + ratio * s)

    wait_bytes(total_ref.at[3, pl.ds(0, nr - 1)], total_send.at[3])


VMEM = pl.BlockSpec(memory_space=pltpu.VMEM)
ANY = pl.BlockSpec(memory_space=pltpu.HBM)


def body(nr, nb, load, stiffness, local_inverse, intact, face_lists, coarse_basis, matrix, pattern):
    tiles = nb // 2
    order = nb * COARSE
    limit = 62 * 1024 * 1024
    out = pl.pallas_call(
        functools.partial(whole_kernel, nr, nb),
        out_shape=jax.ShapeDtypeStruct((2, 8, LANES), F32),
        in_specs=[ANY] * 8,
        out_specs=VMEM,
        scratch_shapes=[
            pltpu.SMEM((1, nb), jnp.int32),
            pltpu.VMEM((nb, COARSE, COARSE), F32),
            pltpu.VMEM((1, NDOF), F32),
            pltpu.VMEM((NDOF, NDOF), F32),
            pltpu.VMEM((NDOF, NDOF), F32),
            pltpu.VMEM((NODES, NODES), jnp.int32),
            pltpu.VMEM((4, FACE), jnp.int32),
            pltpu.VMEM((COARSE, NDOF), F32),
            pltpu.SemaphoreType.DMA((8,)),
            pltpu.VMEM((tiles, order, LANES), F32),
            pltpu.VMEM((nb, COARSE, LANES), F32),
            pltpu.VMEM((tiles, order, LANES), F32),
            pltpu.VMEM((tiles, order, LANES), F32),
            pltpu.VMEM((tiles, W, order), F32),
            pltpu.VMEM((COARSE, order), F32),
            pltpu.VMEM((tiles, COARSE, W), F32),
            pltpu.VMEM((tiles, W, W), F32),
            pltpu.VMEM((W, W), F32),
            pltpu.VMEM((6, NDOF, LANES), F32),
            pltpu.VMEM((6, NDOF, LANES), F32),
            pltpu.VMEM((6, COARSE, LANES), F32),
            pltpu.VMEM((NDOF, LANES), F32),
            pltpu.VMEM((LANES, 2 * LANES), F32),
            pltpu.VMEM((NODES, LANES), F32),
            pltpu.VMEM((NDOF, LANES), F32),
            pltpu.VMEM((NDOF, LANES), F32),
            pltpu.VMEM((NDOF, LANES), F32),
            pltpu.VMEM((NDOF, LANES), F32),
            pltpu.VMEM((4, 1, LANES), F32),
            pltpu.VMEM((4, nb, 1, LANES), F32),
            pltpu.VMEM((4, 1, LANES), F32),
            pltpu.VMEM((4, nr, 1, LANES), F32),
            pltpu.VMEM((3, 8, LANES), F32),
            pltpu.VMEM((3, 4, 8, LANES), F32),
            pltpu.SemaphoreType.DMA((tiles, RUN)),
            pltpu.SemaphoreType.DMA((tiles, RUN)),
            pltpu.SemaphoreType.DMA((tiles, nb // RUN)),
            pltpu.SemaphoreType.DMA((tiles, nb // RUN)),
            pltpu.SemaphoreType.DMA((tiles // 2, nb // RUN, RUN)),
            pltpu.SemaphoreType.DMA((tiles // 2, nb // RUN, RUN)),
            pltpu.SemaphoreType.DMA((4,)),
            pltpu.SemaphoreType.DMA((4,)),
            pltpu.SemaphoreType.DMA((4,)),
            pltpu.SemaphoreType.DMA((4,)),
            pltpu.SemaphoreType.DMA((3, 4)),
            pltpu.SemaphoreType.DMA((3, 4)),
        ],
        compiler_params=pltpu.CompilerParams(
            collective_id=0, has_side_effects=True, vmem_limit_bytes=limit
        ),
        name="whole",
    )(
        pattern.reshape(1, nb),
        matrix.reshape(nb, COARSE, COARSE),
        load.reshape(1, NDOF),
        stiffness.reshape(NDOF, NDOF),
        local_inverse.reshape(NDOF, NDOF),
        intact.reshape(NODES, NODES),
        face_lists.reshape(4, FACE),
        coarse_basis.reshape(COARSE, NDOF),
    )
    flat = out[:, :6, :NODES].reshape(2, 1, 1, NDOF)
    return flat[0], flat[1]


def solution(mesh):
    in_specs = (
        P("rows", "bricks", None),
        P("rows", "bricks", None, None),
        P("rows", "bricks", None, None),
        P("rows", "bricks", None, None),
        P("rows", "bricks", None, None),
        P("rows", "bricks", None, None),
        P("rows", "bricks", None, None, None),
        P("rows", "bricks", None),
    )
    out_specs = (P("rows", "bricks", None), P("rows", "bricks", None))
    run = functools.partial(body, mesh.shape["rows"], mesh.shape["bricks"])
    return jax.shard_map(run, mesh=mesh, in_specs=in_specs, out_specs=out_specs, check_vma=False)
```
